32 devices in a mesh: ctx: 4 (over z), fsdp: 8 (over y, x, core).
Axes of the slice: x: 2, y: 2, z: 4, core: 2. Of those that a mesh axis runs over, the one named last changes fastest.
Arguments:
- inputs: float32 [8, 1024, 2048], P('fsdp', 'ctx'), may hold values from -6 to 6
- out_grad: float32 [8, 1024, 2048], P('fsdp', 'ctx'), may hold values from -6 to 6
- block_order: int32 [8, 8], P('fsdp'), may hold values from 0 to 7, each once within a row
- ln_gain: float32 [2048], replicated, may hold values from 0.5 to 1.5
- ln_beta: float32 [2048], replicated, may hold values from -2 to 2
- w_in: bfloat16 [2048, 14336], P('fsdp'), may hold values from -0.125 to 0.125
- b_in: float32 [14336], replicated, may hold values from -2 to 2
- w_out: bfloat16 [10240, 2048], P('fsdp'), may hold values from -0.125 to 0.125
- b_out: float32 [2048], replicated, may hold values from -2 to 2
Outputs:
- out_y: float32 [8, 1024, 2048], P('fsdp', 'ctx')
- d_input: float32 [8, 1024, 2048], P('fsdp', 'ctx')
- g_w_in: float32 [2048, 14336], P('fsdp')
- g_b_in: float32 [14336], P('fsdp')
- g_w_out: float32 [10240, 2048], P('fsdp')
- g_b_out: float32 [2048], P('fsdp')
- g_gain: float32 [2048], P('fsdp')
- g_beta: float32 [2048], P('fsdp')
The draws below stay inside these ranges and needn't reach their ends.
Inputs may be any that keep to these rules, and one draw needn't show every extreme that they name: Each row of block_order names every block of a sequence once; stored slot j of a sequence holds positions block_order[j] * 128 to block_order[j] * 128 + 127.
All inputs are finite; a program needn't handle non-finite values.
Results may differ from the reference program's by a relative error of at most 0.0059.
Values may be sent and summed in bfloat16 or wider, within the bound.
No kernel may reach another device: no remote copies, remote signals or barrier semaphores. Data moves between devices by JAX's collectives and lax.ppermute only.
A program may use at most 704 MiB of HBM per device.

```python
import math
import jax
import jax.numpy as jnp
from jax import lax

D = 2048
FF = 8192
HEADS = 32
HEAD_DIM = 64
ROT_DIM = 32
LENGTH = 1024
SEQS = 8
NBLK = 8
N_CTX = 4


def level_of(key, shape, cuts, smallest, top_value):
    def one(axis_at, parts):
        draws = jax.random.uniform(jax.random.fold_in(jax.random.fold_in(key, 6), axis_at), (parts,), jnp.float32, smallest / len(cuts), top_value / len(cuts))
        return jnp.repeat(jnp.exp(draws), shape[axis_at] // parts).reshape((-1,) + (1,) * (len(shape) - axis_at - 1))

    gain = one(*cuts[0])
    for cut in cuts[1:]:
        gain = gain * one(*cut)
    return gain


def scatter_about(own_key, extent, spread, limit, shards=(), kind=jnp.bfloat16):
    gain = level_of(own_key, extent, shards, -0.22, 0.18) if shards else 1.0
    entries = jax.random.normal(own_key, extent, jnp.float32) * spread * gain
    return jnp.minimum(jnp.maximum(entries, -limit), limit).astype(kind)


def setup_inputs(seed: int = 0) -> dict:
    seeds = jax.random.split(jax.random.key(seed), 10)
    return {
        "inputs": scatter_about(seeds[0], (SEQS, LENGTH, D), 1.0, 6.0, ((0, 8), (1, 4)), jnp.float32),
        "out_grad": scatter_about(seeds[1], (SEQS, LENGTH, D), 1.0, 6.0, ((0, 8), (1, 4)), jnp.float32),
        "block_order": jax.vmap(lambda own: jax.random.permutation(own, NBLK))(jax.random.split(seeds[2], SEQS)).reshape((SEQS, NBLK)).astype(jnp.int32),
        "ln_gain": jnp.clip(1.0 + 0.1 * jax.random.normal(seeds[3], (D,), jnp.float32), 0.5, 1.5),
        "ln_beta": scatter_about(seeds[4], (D,), 0.3, 2.0, (), jnp.float32),
        "w_in": scatter_about(seeds[5], (D, 3 * D + FF), D ** -0.5, 0.125, ((0, 8),)),
        "b_in": scatter_about(seeds[6], (3 * D + FF,), 0.3, 2.0, (), jnp.float32),
        "w_out": scatter_about(seeds[7], (D + FF, D), D ** -0.5, 0.125, ((0, 8),)),
        "b_out": scatter_about(seeds[8], (D,), 0.3, 2.0, (), jnp.float32),
    }


LN_EPS = 1e-05
NEG_BIG = -1e+30
ROPE_BASE = 10000.0

def row_positions(blk_order, first_row, row_count, blk_size):
    row_index = first_row + jnp.arange(row_count, dtype=jnp.int32)
    slot_ids = row_index // blk_size
    table = (slot_ids[:, None] == jnp.arange(blk_order.shape[0], dtype=jnp.int32)[None, :]).astype(jnp.int32)
    picked = lax.optimization_barrier(jnp.sum(table * blk_order[None, :], axis=1, dtype=jnp.int32))
    return (picked * blk_size + row_index % blk_size).astype(jnp.int32)

def rotary_tables(positions):
    half_rot = ROT_DIM // 2
    expon = jnp.arange(half_rot, dtype=jnp.float32) * (2.0 / ROT_DIM)
    freqs = ROPE_BASE ** (-expon)
    angles = positions.astype(jnp.float32)[:, None] * freqs[None, :]
    return (jnp.cos(angles)[:, None, :], jnp.sin(angles)[:, None, :])

def rotate(values, cosine, sine):
    half_rot = ROT_DIM // 2
    first = values[..., :half_rot]
    second = values[..., half_rot:ROT_DIM]
    return jnp.concatenate([first * cosine - second * sine, second * cosine + first * sine, values[..., ROT_DIM:]], axis=-1)

def rotate_back(grads, cosine, sine):
    half_rot = ROT_DIM // 2
    first = grads[..., :half_rot]
    second = grads[..., half_rot:ROT_DIM]
    return jnp.concatenate([first * cosine + second * sine, second * cosine - first * sine, grads[..., ROT_DIM:]], axis=-1)

def gelu_tanh(values):
    return jax.nn.gelu(values, approximate=True)

def rounded(values):
    return lax.optimization_barrier(values.astype(jnp.bfloat16)).astype(jnp.float32)

def one_sequence(seq_in, seq_grad, blk_order, ln_gain, ln_beta, w_in, b_in, w_out, b_out):
    seq_len = seq_in.shape[0]
    blk_size = seq_len // (2 * N_CTX)
    scale_val = 1.0 / math.sqrt(HEAD_DIM)
    positions = row_positions(blk_order, 0, seq_len, blk_size)
    centred = seq_in - lax.optimization_barrier(jnp.mean(seq_in, axis=1, keepdims=True))
    inv_std = lax.rsqrt(lax.optimization_barrier(jnp.mean(centred * centred, axis=1, keepdims=True)) + LN_EPS)
    x_hat = centred * inv_std
    normed = (x_hat * ln_gain + ln_beta).astype(jnp.bfloat16)
    project = jnp.dot(normed, w_in, preferred_element_type=jnp.float32) + b_in
    cosine, sine = rotary_tables(positions)
    q_f = rounded(rotate(project[:, :D].reshape(seq_len, HEADS, HEAD_DIM), cosine, sine))
    k_f = rounded(rotate(project[:, D:2 * D].reshape(seq_len, HEADS, HEAD_DIM), cosine, sine))
    v_f = rounded(project[:, 2 * D:3 * D].reshape(seq_len, HEADS, HEAD_DIM))
    pre_act = project[:, 3 * D:]
    act_b = gelu_tanh(pre_act).astype(jnp.bfloat16)
    qblk = math.gcd(seq_len, 512)
    nqblk = seq_len // qblk

    def masked_scores(q_index):
        q_rows = lax.dynamic_slice_in_dim(q_f, q_index * qblk, qblk, 0)
        q_pos = lax.dynamic_slice_in_dim(positions, q_index * qblk, qblk, 0)
        allowed = positions[None, None, :] <= q_pos[None, :, None]
        scores = jnp.einsum('thd,ghd->htg', q_rows, k_f) * scale_val
        return (q_rows, allowed, jnp.where(allowed, scores, NEG_BIG))

    def attend(q_index):
        q_rows, allowed, scores = masked_scores(q_index)
        top_val = lax.optimization_barrier(jnp.max(scores, axis=2, keepdims=True))
        weight_sum = lax.optimization_barrier(jnp.sum(jnp.where(allowed, jnp.exp(scores - top_val), 0.0), axis=2, keepdims=True))
        log_total = top_val + jnp.log(weight_sum)
        probs = rounded(jnp.where(allowed, jnp.exp(scores - log_total), 0.0))
        return (jnp.einsum('htg,ghd->thd', probs, v_f), log_total[:, :, 0])
    att_rows, log_sums = lax.map(attend, jnp.arange(nqblk, dtype=jnp.int32))
    att_b = att_rows.reshape(seq_len, D).astype(jnp.bfloat16)
    cat_b = jnp.concatenate([att_b, act_b], axis=1)
    out_y = seq_in + jnp.dot(cat_b, w_out, preferred_element_type=jnp.float32) + b_out
    dy_b = seq_grad.astype(jnp.bfloat16)
    g_w_out = jnp.dot(cat_b.T, dy_b, preferred_element_type=jnp.float32)
    g_b_out = lax.optimization_barrier(jnp.sum(seq_grad, axis=0))
    d_cat = jnp.dot(dy_b, w_out.T, preferred_element_type=jnp.float32)
    d_att = rounded(d_cat[:, :D]).reshape(seq_len, HEADS, HEAD_DIM)
    d_pre = jax.vjp(gelu_tanh, pre_act)[1](d_cat[:, D:])[0]
    att_f = att_b.astype(jnp.float32).reshape(seq_len, HEADS, HEAD_DIM)
    delta = lax.optimization_barrier(jnp.sum(d_att * att_f, axis=2))

    def back(running, q_index):
        d_keys, d_vals = running
        q_rows, allowed, scores = masked_scores(q_index)
        do_rows = lax.dynamic_slice_in_dim(d_att, q_index * qblk, qblk, 0)
        delta_rows = lax.dynamic_slice_in_dim(delta, q_index * qblk, qblk, 0).T
        probs = jnp.where(allowed, jnp.exp(scores - log_sums[q_index][:, :, None]), 0.0)
        d_vals = d_vals + jnp.einsum('htg,thd->ghd', rounded(probs), do_rows)
        d_prob = jnp.einsum('thd,ghd->htg', do_rows, v_f)
        d_score = rounded(probs * (d_prob - delta_rows[:, :, None]) * scale_val)
        d_query = jnp.einsum('htg,ghd->thd', d_score, k_f)
        d_keys = d_keys + jnp.einsum('htg,thd->ghd', d_score, q_rows)
        return ((d_keys, d_vals), d_query)
    zero_kv = jnp.zeros((seq_len, HEADS, HEAD_DIM), jnp.float32)
    (d_keys, d_vals), d_queries = lax.scan(back, (zero_kv, zero_kv), jnp.arange(nqblk, dtype=jnp.int32))
    dq_rot = rotate_back(d_queries.reshape(seq_len, HEADS, HEAD_DIM), cosine, sine).reshape(seq_len, D)
    dk_rot = rotate_back(d_keys, cosine, sine).reshape(seq_len, D)
    d_proj = jnp.concatenate([dq_rot, dk_rot, d_vals.reshape(seq_len, D), d_pre], axis=1)
    g_b_in = lax.optimization_barrier(jnp.sum(d_proj, axis=0))
    d_proj_b = d_proj.astype(jnp.bfloat16)
    g_w_in = jnp.dot(normed.T, d_proj_b, preferred_element_type=jnp.float32)
    d_norm = jnp.dot(d_proj_b, w_in.T, preferred_element_type=jnp.float32)
    g_gain = lax.optimization_barrier(jnp.sum(d_norm * x_hat, axis=0))
    g_beta = lax.optimization_barrier(jnp.sum(d_norm, axis=0))
    gain_grad = d_norm * ln_gain
    d_input = seq_grad + inv_std * (gain_grad - lax.optimization_barrier(jnp.mean(gain_grad, axis=1, keepdims=True)) - x_hat * lax.optimization_barrier(jnp.mean(gain_grad * x_hat, axis=1, keepdims=True)))
    return (out_y, d_input, g_w_in, g_b_in, g_w_out, g_b_out, g_gain, g_beta)

def reference(inputs, out_grad, block_order, ln_gain, ln_beta, w_in, b_in, w_out, b_out):

    def step(running, items):
        seq_in, seq_grad, blk_order = items
        seq_outs = one_sequence(seq_in, seq_grad, blk_order, ln_gain, ln_beta, w_in, b_in, w_out, b_out)
        running = tuple((prior + fresh for prior, fresh in zip(running, seq_outs[2:])))
        return (running, (seq_outs[0], seq_outs[1]))
    start_grads = (jnp.zeros(w_in.shape, jnp.float32), jnp.zeros(b_in.shape, jnp.float32), jnp.zeros(w_out.shape, jnp.float32), jnp.zeros(b_out.shape, jnp.float32), jnp.zeros(ln_gain.shape, jnp.float32), jnp.zeros(ln_beta.shape, jnp.float32))
    grads, (outputs, d_inputs) = lax.scan(step, start_grads, (inputs, out_grad, block_order))
    return (outputs, d_inputs, grads[0], grads[1], grads[2], grads[3], grads[4], grads[5])
```

```python
import functools
import math

import jax
import jax.numpy as jnp
from jax import lax
from jax.experimental import pallas as pl
from jax.experimental.pallas import tpu as pltpu
from jax.sharding import PartitionSpec as P

D = 2048
HEADS = 32
HEAD_DIM = 64
ROT_DIM = 32

LN_EPS = 1e-05
NEG_BIG = -1e30
ROPE_BASE = 10000.0
BF = jnp.bfloat16
F32 = jnp.float32
VMEM_BYTES = 56 * 1024 * 1024


def plan(n_fsdp, n_ctx, cat_rows):
    shard = cat_rows // n_fsdp
    even = True
    att, act = [[] for _ in range(n_ctx)], [[] for _ in range(n_ctx)]
    for f in range(n_fsdp):
        a = min(max(D - shard * f, 0), shard)
        m = shard - a
        if a % (n_ctx * HEAD_DIM) or m % (n_ctx * 16):
            even = False
        for z in range(n_ctx):
            if a:
                att[z].append((shard * f + z * (a // n_ctx), a // n_ctx))
            if m:
                act[z].append((shard * f + a + z * (m // n_ctx), m // n_ctx))
    if not even:
        wide_a, wide_m = D // n_ctx, (cat_rows - D) // n_ctx
        att = [[(z * wide_a, wide_a)] for z in range(n_ctx)]
        act = [[(D + z * wide_m, wide_m)] for z in range(n_ctx)]
    return even, att, act


def in_runs(att, act):
    runs = [(part * D + s, n) for part in range(3) for s, n in att]
    return runs + [(2 * D + s, n) for s, n in act]


def pick_kernel(all_runs, z_ref, src_ref, dst_ref):
    for z, runs in enumerate(all_runs):

        @pl.when(z_ref[0] == z)
        def _():
            at = 0
            for start, size in runs:
                dst_ref[:, at : at + size] = src_ref[:, start : start + size]
                at += size


def pick_columns(src, z, all_runs):
    rows, cols = src.shape
    width = sum(n for _, n in all_runs[0])
    step = min(rows, 64)
    return pl.pallas_call(
        functools.partial(pick_kernel, all_runs),
        grid_spec=pltpu.PrefetchScalarGridSpec(
            num_scalar_prefetch=1,
            grid=(rows // step,),
            in_specs=[pl.BlockSpec((step, cols), lambda i, z_ref: (i, 0))],
            out_specs=pl.BlockSpec((step, width), lambda i, z_ref: (i, 0)),
        ),
        out_shape=jax.ShapeDtypeStruct((rows, width), src.dtype),
        compiler_params=pltpu.CompilerParams(vmem_limit_bytes=VMEM_BYTES),
        name="pick_columns",
    )(z[None], src)


def spread_kernel(all_runs, n_ctx, z_ref, *refs):
    srcs, dst_ref = refs[:-1], refs[-1]
    for z in range(n_ctx):

        @pl.when(z_ref[0] == z)
        def _():
            for j, src_ref in enumerate(srcs):
                at = 0
                for start, size in all_runs[(z - j) % n_ctx]:
                    dst_ref[:, start : start + size] = src_ref[:, at : at + size].astype(F32)
                    at += size


def spread_columns(parts, z, all_runs, cols):
    rows, width = parts[0].shape
    n_ctx = len(parts)
    step = min(rows, 64)
    return pl.pallas_call(
        functools.partial(spread_kernel, all_runs, n_ctx),
        grid_spec=pltpu.PrefetchScalarGridSpec(
            num_scalar_prefetch=1,
            grid=(rows // step,),
            in_specs=[pl.BlockSpec((step, width), lambda i, z_ref: (i, 0))] * n_ctx,
            out_specs=pl.BlockSpec((step, cols), lambda i, z_ref: (i, 0)),
        ),
        out_shape=jax.ShapeDtypeStruct((rows, cols), F32),
        compiler_params=pltpu.CompilerParams(vmem_limit_bytes=VMEM_BYTES),
        name="spread_columns",
    )(z[None], *parts)


def turn(u, c, s_up, s_down):
    half_rot = ROT_DIM // 2
    wide = u.shape[1]
    return (
        u * c
        + pltpu.roll(u, half_rot, 1) * s_up
        + pltpu.roll(u, wide - half_rot, 1) * s_down
    )


def dot(a, b, ca, cb):
    return lax.dot_general(a, b, (((ca,), (cb,)), ((), ())), preferred_element_type=F32)


def causal(size, keys, first):
    key_at = lax.broadcasted_iota(jnp.int32, (keys, size), 0)
    query_at = lax.broadcasted_iota(jnp.int32, (keys, size), 1) + first
    return key_at <= query_at


def att_kernel(q_ref, k_ref, v_ref, c_ref, u_ref, d_ref, qb_ref, kb_ref, vb_ref, att_ref, lse_ref):
    seq = q_ref.shape[0]
    size = math.gcd(seq, 256)
    c, su, sd = c_ref[...], u_ref[...], d_ref[...]
    qb_ref[...] = turn(q_ref[...], c, su, sd).astype(BF)
    kb_ref[...] = turn(k_ref[...], c, su, sd).astype(BF)
    vb_ref[...] = v_ref[...].astype(BF)
    scale = 1.0 / math.sqrt(HEAD_DIM)
    for i in range(seq // size):
        rows = slice(i * size, (i + 1) * size)
        keys = (i + 1) * size
        outs = []
        for h in range(2):
            lanes = slice(h * HEAD_DIM, (h + 1) * HEAD_DIM)
            s = dot(kb_ref[:keys, lanes], qb_ref[rows, lanes], 1, 1) * scale
            s = jnp.where(causal(size, keys, i * size), s, NEG_BIG)
            top = jnp.max(s, axis=0, keepdims=True)
            e = jnp.exp(s - top)
            total = jnp.sum(e, axis=0, keepdims=True)
            lse_ref[0, h : h + 1, rows] = top + jnp.log(total)
            p = (e * (1.0 / total)).astype(BF)
            outs.append(dot(p, vb_ref[:keys, lanes], 0, 0))
        att_ref[rows, :] = jnp.concatenate(outs, axis=1).astype(BF)


def attention(project, tables, n_heads):
    seq = project.shape[0]
    pairs = n_heads // 2
    wide = 2 * HEAD_DIM

    def col(base):
        return pl.BlockSpec((seq, wide), lambda p: (0, base + p))

    table = pl.BlockSpec((seq, wide), lambda p: (0, 0))
    own = jax.ShapeDtypeStruct((seq, n_heads * HEAD_DIM), BF)
    return pl.pallas_call(
        att_kernel,
        grid=(pairs,),
        in_specs=[col(0), col(pairs), col(2 * pairs), table, table, table],
        out_specs=[col(0)] * 4 + [pl.BlockSpec((1, 2, seq), lambda p: (p, 0, 0))],
        out_shape=[own] * 4 + [jax.ShapeDtypeStruct((pairs, 2, seq), F32)],
        compiler_params=pltpu.CompilerParams(vmem_limit_bytes=VMEM_BYTES),
        cost_estimate=pl.CostEstimate(
            flops=n_heads * seq * seq * 256, bytes_accessed=seq * n_heads * 64 * 20,
            transcendentals=n_heads * seq * seq // 2,
        ),
        name="attention",
    )(project, project, project, *tables)


def back_kernel(
    q_ref, k_ref, v_ref, att_ref, datt_ref, lse_ref, c_ref, u_ref, d_ref,
    dq_ref, dk_ref, dv_ref, sq_ref, sk_ref, sv_ref, aq, ak, av,
):
    seq = q_ref.shape[0]
    size = math.gcd(seq, 256)
    scale = 1.0 / math.sqrt(HEAD_DIM)
    ak[...] = jnp.zeros_like(ak)
    av[...] = jnp.zeros_like(av)
    for i in range(seq // size):
        rows = slice(i * size, (i + 1) * size)
        keys = (i + 1) * size
        dqs, dks, dvs = [], [], []
        prod = datt_ref[rows, :].astype(F32) * att_ref[rows, :].astype(F32)
        prod_t = prod.T
        for h in range(2):
            lanes = slice(h * HEAD_DIM, (h + 1) * HEAD_DIM)
            q, do = q_ref[rows, lanes], datt_ref[rows, lanes]
            k, v = k_ref[:keys, lanes], v_ref[:keys, lanes]
            delta = jnp.sum(prod_t[lanes, :], axis=0, keepdims=True)
            s = dot(k, q, 1, 1) * scale
            s = jnp.where(causal(size, keys, i * size), s, NEG_BIG)
            p = jnp.exp(s - lse_ref[0, h : h + 1, rows])
            dp = dot(v, do, 1, 1)
            ds = (p * (dp - delta) * scale).astype(BF)
            dvs.append(dot(p.astype(BF), do, 1, 0))
            dks.append(dot(ds, q, 1, 0))
            dqs.append(dot(ds, k, 0, 0))
        av[:keys, :] += jnp.concatenate(dvs, axis=1)
        ak[:keys, :] += jnp.concatenate(dks, axis=1)
        aq[rows, :] = jnp.concatenate(dqs, axis=1)
    c, su, sd = c_ref[...], -u_ref[...], -d_ref[...]
    dq = turn(aq[...], c, su, sd)
    dk = turn(ak[...], c, su, sd)
    dv = av[...]
    for g, out, tot in ((dq, dq_ref, sq_ref), (dk, dk_ref, sk_ref), (dv, dv_ref, sv_ref)):
        out[...] = g.astype(BF)
        tot[0] = jnp.sum(g, axis=0, keepdims=True)


def attention_back(q, k, v, att, d_att, lse, tables, n_heads):
    seq = q.shape[0]
    pairs = n_heads // 2
    wide = 2 * HEAD_DIM
    col = pl.BlockSpec((seq, wide), lambda p: (0, p))
    table = pl.BlockSpec((seq, wide), lambda p: (0, 0))
    own = jax.ShapeDtypeStruct((seq, n_heads * HEAD_DIM), BF)
    return pl.pallas_call(
        back_kernel,
        grid=(pairs,),
        in_specs=[col] * 5 + [pl.BlockSpec((1, 2, seq), lambda p: (p, 0, 0))] + [table] * 3,
        out_specs=[col] * 3 + [pl.BlockSpec((1, 1, wide), lambda p: (p, 0, 0))] * 3,
        out_shape=[own] * 3 + [jax.ShapeDtypeStruct((pairs, 1, wide), F32)] * 3,
        scratch_shapes=[pltpu.VMEM((seq, wide), F32)] * 3,
        compiler_params=pltpu.CompilerParams(vmem_limit_bytes=VMEM_BYTES),
        cost_estimate=pl.CostEstimate(
            flops=n_heads * seq * seq * 640, bytes_accessed=seq * n_heads * 64 * 16,
            transcendentals=n_heads * seq * seq // 2,
        ),
        name="attention_back",
    )(q, k, v, att, d_att, lse, *tables)


def ring(part):
    n = lax.axis_size("ctx")
    perm = [(i, (i + 1) % n) for i in range(n)]
    parts = [part]
    for _ in range(n - 1):
        parts.append(lax.ppermute(parts[-1], "ctx", perm))
    return parts


def ring_sum(take):
    n = lax.axis_size("ctx")
    perm = [(i, (i + 1) % n) for i in range(n)]
    run = take(1).astype(BF)
    for j in range(2, n):
        run = (take(j) + lax.ppermute(run, "ctx", perm).astype(F32)).astype(BF)
    return take(0) + lax.ppermute(run, "ctx", perm).astype(F32)


def swap(x, axis, bit):
    n = lax.axis_size(axis)
    return lax.ppermute(x, axis, [(i, i ^ bit) for i in range(n)])


def far_bits(n):
    return [1 << b for b in range(1, n.bit_length() - 1)]


def gather_near(shard):
    n = lax.axis_size("fsdp")
    rows = shard.shape[0]
    found = {}
    for half in range(2):
        order = far_bits(n)
        if half:
            order = order[::-1]
        lo = half * (rows // 2)
        have = {0: shard[lo : lo + rows // 2]}
        for bit in order:
            keys = sorted(have)
            got = swap(jnp.stack([have[k] for k in keys]), "fsdp", bit)
            for i, k in enumerate(keys):
                have[k ^ bit] = got[i]
        keys = sorted(have)
        got = swap(jnp.stack([have[k] for k in keys]), "fsdp", 1)
        for i, k in enumerate(keys):
            have[k ^ 1] = got[i]
        for k in range(n):
            found[k, half] = have[k]
    return [(found[k, 0], found[k, 1]) for k in range(n)]


def scatter_near(blocks):
    n = lax.axis_size("fsdp")
    rows = blocks[0].shape[0]
    halves = []
    for half in range(2):
        order = far_bits(n)
        if half:
            order = order[::-1]
        lo = half * (rows // 2)
        have = {k: blocks[k][lo : lo + rows // 2] for k in range(n)}
        for bit in [1] + order:
            away = sorted(k for k in have if k & bit)
            got = swap(jnp.stack([have[k] for k in away]), "fsdp", bit)
            for i, k in enumerate(away):
                mine = have[k ^ bit].astype(F32) + got[i].astype(F32)
                have[k ^ bit] = mine.astype(BF)
                del have[k]
        halves.append(have[0])
    return jnp.concatenate(halves, axis=0)


def sum_all(x, axes):
    for axis in axes:
        bit = 1
        while bit < lax.axis_size(axis):
            x = x + swap(x, axis, bit)
            bit *= 2
    return x


def gelu_tanh(values):
    return jax.nn.gelu(values, approximate=True)


def rotary_tables(seq):
    half_rot = ROT_DIM // 2
    expon = jnp.arange(half_rot, dtype=F32) * (2.0 / ROT_DIM)
    freqs = ROPE_BASE ** (-expon)
    angles = jnp.arange(seq, dtype=jnp.int32).astype(F32)[:, None] * freqs[None, :]
    cosine, sine = jnp.cos(angles), jnp.sin(angles)
    zero = jnp.zeros_like(sine)
    rest = jnp.zeros((seq, HEAD_DIM - ROT_DIM), F32)
    c = jnp.concatenate([cosine, cosine, rest + 1.0], axis=1)
    up = jnp.concatenate([zero, sine, rest], axis=1)
    down = jnp.concatenate([-sine, zero, rest], axis=1)
    return tuple(jnp.concatenate([t, t], axis=1) for t in (c, up, down))


def shards(inputs, out_grad, block_order, ln_gain, ln_beta, w_in, b_in, w_out, b_out):
    n_ctx, n_fsdp = lax.axis_size("ctx"), lax.axis_size("fsdp")
    z, f = lax.axis_index("ctx"), lax.axis_index("fsdp")
    seq_in, seq_grad, blk_order = inputs[0], out_grad[0], block_order[0]
    tok_rows = seq_in.shape[0]
    seq_len = tok_rows * n_ctx
    n_blk = blk_order.shape[0]
    blk_size = seq_len // n_blk
    per = n_blk // n_ctx
    wide_d = D // n_fsdp
    shard = w_out.shape[0]
    cat_rows = shard * n_fsdp
    in_cols = w_in.shape[1]
    n_heads = HEADS // n_ctx
    wide_a, wide_m = D // n_ctx, (cat_rows - D) // n_ctx
    even, att_runs, act_runs = plan(n_fsdp, n_ctx, cat_rows)
    z_runs = [in_runs(att_runs[i], act_runs[i]) for i in range(n_ctx)]

    def turned(x):
        return jnp.concatenate(
            [lax.dynamic_slice_in_dim(x, (f ^ k) * wide_d, wide_d, 1) for k in range(n_fsdp)], axis=1
        )

    def places(j):
        rank = lax.rem(z - j + n_ctx, n_ctx)
        return [blk_order[rank * per + i] * blk_size for i in range(per)]

    def in_order(parts):
        whole = jnp.zeros((seq_len, parts[0].shape[1]), parts[0].dtype)
        for j, part in enumerate(parts):
            for i, at in enumerate(places(j)):
                whole = lax.dynamic_update_slice_in_dim(
                    whole, part[i * blk_size : (i + 1) * blk_size], at, 0
                )
        return whole

    def taker(whole):
        def take(j):
            return jnp.concatenate(
                [lax.dynamic_slice_in_dim(whole, at, blk_size, 0) for at in places(j)], axis=0
            ).astype(F32)

        return take

    centred = seq_in - jnp.mean(seq_in, axis=1, keepdims=True)
    inv_std = lax.rsqrt(jnp.mean(centred * centred, axis=1, keepdims=True) + LN_EPS)
    x_hat = centred * inv_std
    normed_own = turned((x_hat * ln_gain + ln_beta).astype(BF))
    normed = in_order(ring(normed_own))
    dy_own = seq_grad.astype(BF)
    dy = in_order(ring(dy_own))

    w_in_blocks = gather_near(pick_columns(w_in, z, z_runs))
    w_in_all = jnp.concatenate([h for pair in w_in_blocks for h in pair], axis=0)
    b_in_z = jnp.stack([jnp.concatenate([b_in[s : s + n] for s, n in runs]) for runs in z_runs])[z]

    def own_rows(whole, rank, at_f):
        pieces = []
        a_0 = jnp.clip(D - shard * at_f, 0, shard)
        n_att = [min(max(D - shard * i, 0), shard) for i in range(n_fsdp)]
        share = shard // n_ctx
        del pieces, n_att
        first = lax.dynamic_slice_in_dim(whole, rank * share, share, 0)
        mixed = [i for i in range(n_fsdp) if 0 < min(max(D - shard * i, 0), shard) < shard]
        if not mixed:
            return first
        a = D - shard * mixed[0]
        m = shard - a
        both = jnp.concatenate(
            [
                lax.dynamic_slice_in_dim(whole, rank * (a // n_ctx), a // n_ctx, 0),
                lax.dynamic_slice_in_dim(whole, a + rank * (m // n_ctx), m // n_ctx, 0),
            ],
            axis=0,
        )
        return jnp.where(at_f == mixed[0], both, first)

    if even:
        share = shard // n_ctx
        w_out_blocks = gather_near(own_rows(w_out, z, f))
        w_out_z = jnp.zeros((cat_rows // n_ctx, D), BF)
        for k, pair in enumerate(w_out_blocks):
            for half in range(2):
                w_out_z = lax.dynamic_update_slice_in_dim(
                    w_out_z, pair[half], (f ^ k) * share + half * (share // 2), 0
                )
    else:
        w_all = lax.all_gather(w_out, "fsdp", axis=0, tiled=True)
        w_out_z = jnp.concatenate(
            [
                lax.dynamic_slice_in_dim(w_all, z * wide_a, wide_a, 0),
                lax.dynamic_slice_in_dim(w_all, D + z * wide_m, wide_m, 0),
            ],
            axis=0,
        )

    project = jnp.dot(normed, w_in_all, preferred_element_type=F32) + b_in_z
    tables = rotary_tables(seq_len)
    q_b, k_b, v_b, att_b, lse = attention(project, tables, n_heads)
    pre_act = project[:, 3 * wide_a :]
    act_b = gelu_tanh(pre_act).astype(BF)
    cat_b = jnp.concatenate([att_b, act_b], axis=1)
    mixed = ring_sum(taker(jnp.dot(cat_b, w_out_z, preferred_element_type=F32)))
    out_y = seq_in + mixed + b_out

    d_cat = dot(dy, w_out_z, 1, 1)
    g_out = dot(cat_b, dy, 0, 0).astype(BF)
    d_att = d_cat[:, :wide_a].astype(BF)
    d_pre = jax.vjp(gelu_tanh, pre_act)[1](d_cat[:, wide_a:])[0]
    d_pre_b = d_pre.astype(BF)
    g_in_pre = dot(normed, d_pre_b, 0, 0).astype(BF)

    if even:
        blocks = [
            lax.dynamic_slice_in_dim(g_out, (f ^ k) * share, share, 0) for k in range(n_fsdp)
        ]
        own = scatter_near(blocks)
        g_w_out = jnp.zeros((shard, D), F32)
        mixed_f = [i for i in range(n_fsdp) if 0 < min(max(D - shard * i, 0), shard) < shard]
        a = D - shard * mixed_f[0] if mixed_f else shard
        m = shard - a
        cut = a // n_ctx
        is_mixed = (f == mixed_f[0]) if mixed_f else False
        for j, part in enumerate(ring(own)):
            rank = lax.rem(z - j + n_ctx, n_ctx)
            part = part.astype(F32)
            at_a = jnp.where(is_mixed, rank * cut, rank * share)
            at_m = jnp.where(is_mixed, a + rank * (share - cut), rank * share + cut)
            g_w_out = lax.dynamic_update_slice_in_dim(g_w_out, part[:cut], at_a, 0)
            if m:
                g_w_out = lax.dynamic_update_slice_in_dim(g_w_out, part[cut:], at_m, 0)
    else:
        spread = jnp.zeros((cat_rows, D), BF)
        spread = lax.dynamic_update_slice_in_dim(spread, g_out[:wide_a], z * wide_a, 0)
        spread = lax.dynamic_update_slice_in_dim(spread, g_out[wide_a:], D + z * wide_m, 0)
        g_w_out = lax.psum_scatter(spread.astype(F32), "fsdp", scatter_dimension=0, tiled=True)
        g_w_out = lax.psum(g_w_out, "ctx")

    dq_b, dk_b, dv_b, s_q, s_k, s_v = attention_back(
        q_b, k_b, v_b, att_b, d_att, lse, tables, n_heads
    )
    d_qkv_b = jnp.concatenate([dq_b, dk_b, dv_b], axis=1)
    g_in_qkv = dot(normed, d_qkv_b, 0, 0).astype(BF)
    d_proj_b = jnp.concatenate([d_qkv_b, d_pre_b], axis=1)
    d_norm = turned(ring_sum(taker(dot(d_proj_b, w_in_all, 1, 1))))

    def by_rank(g):
        return [g[k * wide_d : (k + 1) * wide_d] for k in range(n_fsdp)]

    own_pre = ring(scatter_near(by_rank(g_in_pre)))
    own_qkv = ring(scatter_near(by_rank(g_in_qkv)))
    g_w_in = spread_columns(
        [jnp.concatenate([a, b], axis=1) for a, b in zip(own_qkv, own_pre)], z, z_runs, in_cols
    )

    g_b_in_z = jnp.concatenate(
        [s_q.reshape(-1), s_k.reshape(-1), s_v.reshape(-1), jnp.sum(d_pre, axis=0)]
    )
    masked = jnp.where(
        jnp.arange(n_ctx)[:, None] == z, g_b_in_z[None, :], jnp.zeros((), F32)
    )
    runs = sorted((s, n, i, at) for i in range(n_ctx) for s, n, at in run_offsets(z_runs[i]))
    g_b_in = sum_all(
        jnp.concatenate([masked[i, at : at + n] for _, n, i, at in runs]), ("fsdp", "ctx")
    )
    gain_grad = d_norm * ln_gain
    d_input = seq_grad + inv_std * (
        gain_grad
        - jnp.mean(gain_grad, axis=1, keepdims=True)
        - x_hat * jnp.mean(gain_grad * x_hat, axis=1, keepdims=True)
    )
    small = sum_all(
        jnp.stack(
            [jnp.sum(seq_grad, axis=0), jnp.sum(d_norm * x_hat, axis=0), jnp.sum(d_norm, axis=0)]
        ),
        ("fsdp", "ctx"),
    )

    def own_part(vector):
        length_part = vector.shape[0] // n_fsdp
        return lax.dynamic_slice_in_dim(vector, f * length_part, length_part, 0)

    return (
        out_y[None],
        d_input[None],
        g_w_in,
        own_part(g_b_in),
        g_w_out,
        own_part(small[0]),
        own_part(small[1]),
        own_part(small[2]),
    )


def run_offsets(runs):
    at, found = 0, []
    for start, size in runs:
        found.append((start, size, at))
        at += size
    return found


def solution(mesh):
    placed = (
        P("fsdp", "ctx", None),
        P("fsdp", "ctx", None),
        P("fsdp", None),
        P(),
        P(),
        P("fsdp", None),
        P(),
        P("fsdp", None),
        P(),
    )
    return jax.shard_map(
        shards,
        mesh=mesh,
        in_specs=placed,
        out_specs=(
            P("fsdp", "ctx", None),
            P("fsdp", "ctx", None),
            P("fsdp", None),
            P("fsdp"),
            P("fsdp", None),
            P("fsdp"),
            P("fsdp"),
            P("fsdp"),
        ),
        check_vma=False,
    )
```

```python
import functools
import math

import jax
import jax.numpy as jnp
from jax import lax
from jax.experimental import pallas as pl
from jax.experimental.pallas import tpu as pltpu
from jax.sharding import PartitionSpec as P

D = 2048
HEADS = 32
HEAD_DIM = 64
ROT_DIM = 32

LN_EPS = 1e-05
NEG_BIG = -1e30
ROPE_BASE = 10000.0
BF = jnp.bfloat16
F32 = jnp.float32
VMEM_BYTES = 56 * 1024 * 1024
HBM_SPEC = pl.BlockSpec(memory_space=pltpu.HBM)


def plan(n_fsdp, n_ctx, cat_rows):
    shard = cat_rows // n_fsdp
    even = True
    att, act = [[] for _ in range(n_ctx)], [[] for _ in range(n_ctx)]
    for f in range(n_fsdp):
        a = min(max(D - shard * f, 0), shard)
        m = shard - a
        if a % (n_ctx * HEAD_DIM) or m % (n_ctx * 16):
            even = False
        for z in range(n_ctx):
            if a:
                att[z].append((shard * f + z * (a // n_ctx), a // n_ctx))
            if m:
                act[z].append((shard * f + a + z * (m // n_ctx), m // n_ctx))
    if not even:
        wide_a, wide_m = D // n_ctx, (cat_rows - D) // n_ctx
        att = [[(z * wide_a, wide_a)] for z in range(n_ctx)]
        act = [[(D + z * wide_m, wide_m)] for z in range(n_ctx)]
    return even, att, act


def in_runs(att, act):
    runs = [(part * D + s, n) for part in range(3) for s, n in att]
    return runs + [(2 * D + s, n) for s, n in act]


def key_order(n):
    return list(range(0, n, 2)) + list(range(1, n, 2))


def pick_kernel(all_runs, z_ref, src_ref, dst_ref):
    for z, runs in enumerate(all_runs):

        @pl.when(z_ref[0] == z)
        def _():
            at = 0
            for start, size in runs:
                dst_ref[:, at : at + size] = src_ref[:, start : start + size]
                at += size


def pick_columns(src, z, all_runs):
    rows, cols = src.shape
    width = sum(n for _, n in all_runs[0])
    step = min(rows, 64)
    return pl.pallas_call(
        functools.partial(pick_kernel, all_runs),
        grid_spec=pltpu.PrefetchScalarGridSpec(
            num_scalar_prefetch=1,
            grid=(rows // step,),
            in_specs=[pl.BlockSpec((step, cols), lambda i, z_ref: (i, 0))],
            out_specs=pl.BlockSpec((step, width), lambda i, z_ref: (i, 0)),
        ),
        out_shape=jax.ShapeDtypeStruct((rows, width), src.dtype),
        compiler_params=pltpu.CompilerParams(vmem_limit_bytes=VMEM_BYTES),
        name="pick_columns",
    )(z[None], src)


def spread_kernel(all_runs, n_ctx, z_ref, *refs):
    srcs, dst_ref = refs[:n_ctx], refs[-1]
    for z in range(n_ctx):

        @pl.when(z_ref[0] == z)
        def _():
            for j, src_ref in enumerate(srcs):
                at = 0
                for start, size in all_runs[(z - j) % n_ctx]:
                    dst_ref[:, start : start + size] = src_ref[:, at : at + size].astype(F32)
                    at += size


def spread_columns(whole, parts, z, all_runs, cols, first, width_out):
    rows, width = parts[0].shape
    n_ctx = len(parts)
    step = min(rows, 64)
    fresh = whole is None
    return pl.pallas_call(
        functools.partial(spread_kernel, all_runs, n_ctx),
        grid_spec=pltpu.PrefetchScalarGridSpec(
            num_scalar_prefetch=1,
            grid=(rows // step,),
            in_specs=[pl.BlockSpec((step, width), lambda i, z_ref: (i, 0))] * n_ctx
            + [pl.BlockSpec(memory_space=pl.ANY)] * (not fresh),
            out_specs=pl.BlockSpec(
                (pl.Element(step), pl.Element(width_out)), lambda i, z_ref: (i * step, first)
            ),
        ),
        out_shape=jax.ShapeDtypeStruct((rows, cols), F32),
        input_output_aliases={} if fresh else {1 + n_ctx: 0},
        compiler_params=pltpu.CompilerParams(vmem_limit_bytes=VMEM_BYTES),
        name="spread_columns",
    )(z[None], *parts, *([] if fresh else [whole]))


def norm_kernel(n_fsdp, f_ref, x_ref, g_ref, gain_ref, beta_ref, out_ref, dy_ref, hold):
    x = x_ref[...]
    centred = x - jnp.mean(x, axis=1, keepdims=True)
    inv_std = lax.rsqrt(jnp.mean(centred * centred, axis=1, keepdims=True) + LN_EPS)
    hold[...] = (centred * inv_std * gain_ref[...] + beta_ref[...]).astype(BF)
    wide = x.shape[1] // n_fsdp
    for p, k in enumerate(key_order(n_fsdp)):
        at = pl.multiple_of((f_ref[0] ^ k) * wide, wide)
        out_ref[:, p * wide : (p + 1) * wide] = hold[:, pl.ds(at, wide)]
    dy_ref[...] = g_ref[...].astype(BF)


def norm(x, g, gain, beta, f, n_fsdp):
    rows, cols = x.shape
    step = min(rows, 64)
    tile = pl.BlockSpec((step, cols), lambda i, f_ref: (i, 0))
    line = pl.BlockSpec((1, cols), lambda i, f_ref: (0, 0))
    own = jax.ShapeDtypeStruct((rows, cols), BF)
    return pl.pallas_call(
        functools.partial(norm_kernel, n_fsdp),
        grid_spec=pltpu.PrefetchScalarGridSpec(
            num_scalar_prefetch=1,
            grid=(rows // step,),
            in_specs=[tile, tile, line, line],
            out_specs=[tile, tile],
            scratch_shapes=[pltpu.VMEM((step, cols), BF)],
        ),
        out_shape=[own, own],
        compiler_params=pltpu.CompilerParams(vmem_limit_bytes=VMEM_BYTES),
        name="norm",
    )(f[None], x, g, gain[None], beta[None])


def put_kernel(cuts, fresh, at_ref, *refs):
    n = len({i for i, _, _ in cuts})
    srcs, dst, sems = refs[:n], refs[-2], refs[-1]
    del fresh
    copies = []
    for c, (i, start, size) in enumerate(cuts):
        copies.append(
            pltpu.make_async_copy(
                srcs[i].at[pl.ds(start, size)],
                dst.at[pl.ds(pl.multiple_of(at_ref[c], 16), size)],
                sems.at[c],
            )
        )
    for copy in copies:
        copy.start()
    for copy in copies:
        copy.wait()


def put(whole, pieces, rows):
    cuts, places = [], []
    for i, (_, moves) in enumerate(pieces):
        for start, size, at in moves:
            cuts.append((i, start, size))
            places.append(jnp.asarray(at, jnp.int32))
    arrays = [p for p, _ in pieces]
    fresh = whole is None
    any_spec = pl.BlockSpec(memory_space=pl.ANY)
    return pl.pallas_call(
        functools.partial(put_kernel, tuple(cuts), fresh),
        grid_spec=pltpu.PrefetchScalarGridSpec(
            num_scalar_prefetch=1,
            grid=(1,),
            in_specs=[any_spec] * len(arrays) + [HBM_SPEC] * (not fresh),
            out_specs=HBM_SPEC,
            scratch_shapes=[pltpu.SemaphoreType.DMA((len(cuts),))],
        ),
        out_shape=jax.ShapeDtypeStruct((rows, arrays[0].shape[1]), arrays[0].dtype),
        input_output_aliases={} if fresh else {1 + len(arrays): 0},
        compiler_params=pltpu.CompilerParams(vmem_limit_bytes=4 * 1024 * 1024),
        name="put",
    )(jnp.stack(places), *arrays, *([] if fresh else [whole]))


def split_kernel(n_fsdp, f_ref, src, away, home, sems):
    rows = src.shape[0] // n_fsdp
    copies = []
    for s in range(n_fsdp):
        key = f_ref[0] ^ s
        at = pl.ds(pl.multiple_of(lax.shift_right_logical(key, 1) * rows, 16), rows)
        cut = src.at[pl.ds(s * rows, rows)]
        there = pltpu.make_async_copy(cut, away.at[at], sems.at[s])
        here = pltpu.make_async_copy(cut, home.at[at], sems.at[s])
        pl.when(lax.bitwise_and(key, 1) == 1)(there.start)
        pl.when(lax.bitwise_and(key, 1) == 0)(here.start)
        copies.append(here)
    for copy in copies:
        copy.wait()


def split(whole, f, n_fsdp):
    half = jax.ShapeDtypeStruct((whole.shape[0] // 2, whole.shape[1]), whole.dtype)
    any_spec = pl.BlockSpec(memory_space=pl.ANY)
    return pl.pallas_call(
        functools.partial(split_kernel, n_fsdp),
        grid_spec=pltpu.PrefetchScalarGridSpec(
            num_scalar_prefetch=1,
            grid=(1,),
            in_specs=[any_spec],
            out_specs=[HBM_SPEC] * 2,
            scratch_shapes=[pltpu.SemaphoreType.DMA((n_fsdp,))],
        ),
        out_shape=[half, half],
        compiler_params=pltpu.CompilerParams(vmem_limit_bytes=4 * 1024 * 1024),
        name="split",
    )(f[None], whole)


def turn(u, c, s_up, s_down):
    half_rot = ROT_DIM // 2
    wide = u.shape[1]
    return (
        u * c
        + pltpu.roll(u, half_rot, 1) * s_up
        + pltpu.roll(u, wide - half_rot, 1) * s_down
    )


def dot(a, b, ca, cb):
    return lax.dot_general(a, b, (((ca,), (cb,)), ((), ())), preferred_element_type=F32)


def causal(size, keys, first):
    key_at = lax.broadcasted_iota(jnp.int32, (keys, size), 0)
    query_at = lax.broadcasted_iota(jnp.int32, (keys, size), 1) + first
    return key_at <= query_at


def att_kernel(q_ref, k_ref, v_ref, c_ref, u_ref, d_ref, qb_ref, kb_ref, vb_ref, att_ref, lse_ref):
    seq = q_ref.shape[0]
    size = math.gcd(seq, 256)
    c, su, sd = c_ref[...], u_ref[...], d_ref[...]
    qb_ref[...] = turn(q_ref[...], c, su, sd).astype(BF)
    kb_ref[...] = turn(k_ref[...], c, su, sd).astype(BF)
    vb_ref[...] = v_ref[...].astype(BF)
    scale = 1.0 / math.sqrt(HEAD_DIM)
    for i in range(seq // size):
        rows = slice(i * size, (i + 1) * size)
        keys = (i + 1) * size
        outs = []
        for h in range(2):
            lanes = slice(h * HEAD_DIM, (h + 1) * HEAD_DIM)
            s = dot(kb_ref[:keys, lanes], qb_ref[rows, lanes], 1, 1) * scale
            s = jnp.where(causal(size, keys, i * size), s, NEG_BIG)
            top = jnp.max(s, axis=0, keepdims=True)
            e = jnp.exp(s - top)
            total = jnp.sum(e, axis=0, keepdims=True)
            lse_ref[0, h : h + 1, rows] = top + jnp.log(total)
            p = (e * (1.0 / total)).astype(BF)
            outs.append(dot(p, vb_ref[:keys, lanes], 0, 0))
        att_ref[rows, :] = jnp.concatenate(outs, axis=1).astype(BF)


def attention(project, tables, n_heads):
    seq = project.shape[0]
    pairs = n_heads // 2
    wide = 2 * HEAD_DIM

    def col(base):
        return pl.BlockSpec((seq, wide), lambda p: (0, base + p))

    table = pl.BlockSpec((seq, wide), lambda p: (0, 0))
    own = jax.ShapeDtypeStruct((seq, n_heads * HEAD_DIM), BF)
    return pl.pallas_call(
        att_kernel,
        grid=(pairs,),
        in_specs=[col(0), col(pairs), col(2 * pairs), table, table, table],
        out_specs=[col(0)] * 4 + [pl.BlockSpec((1, 2, seq), lambda p: (p, 0, 0))],
        out_shape=[own] * 4 + [jax.ShapeDtypeStruct((pairs, 2, seq), F32)],
        compiler_params=pltpu.CompilerParams(vmem_limit_bytes=VMEM_BYTES),
        cost_estimate=pl.CostEstimate(
            flops=n_heads * seq * seq * 256, bytes_accessed=seq * n_heads * 64 * 20,
            transcendentals=n_heads * seq * seq // 2,
        ),
        name="attention",
    )(project, project, project, *tables)


def back_kernel(
    q_ref, k_ref, v_ref, att_ref, datt_ref, lse_ref, c_ref, u_ref, d_ref,
    dq_ref, dk_ref, dv_ref, sq_ref, sk_ref, sv_ref, aq, ak, av,
):
    seq = q_ref.shape[0]
    size = math.gcd(seq, 256)
    scale = 1.0 / math.sqrt(HEAD_DIM)
    ak[...] = jnp.zeros_like(ak)
    av[...] = jnp.zeros_like(av)
    for i in range(seq // size):
        rows = slice(i * size, (i + 1) * size)
        keys = (i + 1) * size
        dqs, dks, dvs = [], [], []
        prod = datt_ref[rows, :].astype(F32) * att_ref[rows, :].astype(F32)
        prod_t = prod.T
        for h in range(2):
            lanes = slice(h * HEAD_DIM, (h + 1) * HEAD_DIM)
            q, do = q_ref[rows, lanes], datt_ref[rows, lanes]
            k, v = k_ref[:keys, lanes], v_ref[:keys, lanes]
            delta = jnp.sum(prod_t[lanes, :], axis=0, keepdims=True)
            s = dot(k, q, 1, 1) * scale
            s = jnp.where(causal(size, keys, i * size), s, NEG_BIG)
            p = jnp.exp(s - lse_ref[0, h : h + 1, rows])
            dp = dot(v, do, 1, 1)
            ds = (p * (dp - delta) * scale).astype(BF)
            dvs.append(dot(p.astype(BF), do, 1, 0))
            dks.append(dot(ds, q, 1, 0))
            dqs.append(dot(ds, k, 0, 0))
        av[:keys, :] += jnp.concatenate(dvs, axis=1)
        ak[:keys, :] += jnp.concatenate(dks, axis=1)
        aq[rows, :] = jnp.concatenate(dqs, axis=1)
    c, su, sd = c_ref[...], -u_ref[...], -d_ref[...]
    dq = turn(aq[...], c, su, sd)
    dk = turn(ak[...], c, su, sd)
    dv = av[...]
    for g, out, tot in ((dq, dq_ref, sq_ref), (dk, dk_ref, sk_ref), (dv, dv_ref, sv_ref)):
        out[...] = g.astype(BF)
        tot[0] = jnp.sum(g, axis=0, keepdims=True)


def attention_back(q, k, v, att, d_att, lse, tables, n_heads):
    seq = q.shape[0]
    pairs = n_heads // 2
    wide = 2 * HEAD_DIM
    col = pl.BlockSpec((seq, wide), lambda p: (0, p))
    table = pl.BlockSpec((seq, wide), lambda p: (0, 0))
    own = jax.ShapeDtypeStruct((seq, n_heads * HEAD_DIM), BF)
    return pl.pallas_call(
        back_kernel,
        grid=(pairs,),
        in_specs=[col] * 5 + [pl.BlockSpec((1, 2, seq), lambda p: (p, 0, 0))] + [table] * 3,
        out_specs=[col] * 3 + [pl.BlockSpec((1, 1, wide), lambda p: (p, 0, 0))] * 3,
        out_shape=[own] * 3 + [jax.ShapeDtypeStruct((pairs, 1, wide), F32)] * 3,
        scratch_shapes=[pltpu.VMEM((seq, wide), F32)] * 3,
        compiler_params=pltpu.CompilerParams(vmem_limit_bytes=VMEM_BYTES),
        cost_estimate=pl.CostEstimate(
            flops=n_heads * seq * seq * 640, bytes_accessed=seq * n_heads * 64 * 16,
            transcendentals=n_heads * seq * seq // 2,
        ),
        name="attention_back",
    )(q, k, v, att, d_att, lse, *tables)


def after(x, *others):
    return lax.optimization_barrier((x, *others))[0]


def pass_on(x):
    n = lax.axis_size("ctx")
    return lax.ppermute(x, "ctx", [(i, (i + 1) % n) for i in range(n)])


def swap(x, axis, bit):
    n = lax.axis_size(axis)
    return lax.ppermute(x, axis, [(i, i ^ bit) for i in range(n)])


def near(x, bit):
    return swap(x, "fsdp", bit)


def far_keys(n):
    return sorted((k for k in range(2, n, 2)), key=lambda k: (k.bit_count(), k))


def top_bit(k):
    return 1 << (k.bit_length() - 1)


def low_bit(k):
    return k & -k


def halves(x):
    rows = x.shape[0] // 2
    return [x[:rows], x[rows:]]


class Line:
    def __init__(self):
        self.due = []

    def wait(self, *arrays):
        self.due += list(arrays)

    def tied(self, *xs):
        got = list(lax.optimization_barrier((*xs, *self.due)))[: len(xs)]
        self.due = got[:1]
        return got[0] if len(xs) == 1 else got


def ring_job(part, found):
    for _ in range(lax.axis_size("ctx") - 1):
        (part,) = yield [pass_on(part)]
        found.append(part)


def sum_job(take, found):
    n = lax.axis_size("ctx")
    run = take(1)
    for j in range(2, n + 1):
        (got,) = yield [pass_on(run.astype(BF))]
        run = take(j % n) + got.astype(F32)
    found.append(run)


def gather_job(shard, found):
    n = lax.axis_size("fsdp")
    have = {}
    keys = far_keys(n)
    fresh = [(0, None, shard)]
    level = 0
    while True:
        level += 1
        send = []
        for k in keys:
            if k.bit_count() != level:
                continue
            if level == 1:
                send.append((k, None, near(shard, k)))
            else:
                for h, bit in ((0, top_bit(k)), (1, low_bit(k))):
                    send.append((k, h, near(have[k ^ bit, h], bit)))
        send += [(k | 1, h, near(x, 1)) for k, h, x in fresh if not k & 1]
        if not send:
            return
        got = yield [x for _, _, x in send]
        fresh = [(k, h, x) for (k, h, _), x in zip(send, got)]
        found.extend(fresh)
        for k, h, x in fresh:
            if h is None:
                have[k, 0], have[k, 1] = halves(x)
            else:
                have[k, h] = x


def scatter_job(away, home, found):
    n = lax.axis_size("fsdp")
    (got,) = yield [near(away, 1)]
    home = home() if callable(home) else home
    rows = home.shape[0] // (n // 2)
    hold = {}
    for i, k in enumerate(range(0, n, 2)):
        for h in range(2):
            at = i * rows + h * (rows // 2)
            cut = slice(at, at + rows // 2)
            hold[k, h] = home[cut].astype(F32) + got[cut].astype(F32)
    for level in range(n.bit_length() - 2, 0, -1):
        moves = []
        for k in far_keys(n):
            if k.bit_count() != level:
                continue
            if level > 1:
                for h, bit in ((0, top_bit(k)), (1, low_bit(k))):
                    moves.append((k ^ bit, h, near(hold[k, h].astype(BF), bit)))
            else:
                whole = jnp.concatenate([hold[k, 0], hold[k, 1]], axis=0).astype(BF)
                moves.append((0, None, near(whole, k)))
        got = yield [x for _, _, x in moves]
        for (k, h, _), x in zip(moves, got):
            if h is None:
                for i, part in enumerate(halves(x)):
                    hold[k, i] = hold[k, i] + part.astype(F32)
            else:
                hold[k, h] = hold[k, h] + x.astype(F32)
    found.append(jnp.concatenate([hold[0, 0], hold[0, 1]], axis=0).astype(BF))


def total_job(x, found):
    for axis in ("fsdp", "ctx"):
        bit = 1
        while bit < lax.axis_size(axis):
            (got,) = yield [swap(x, axis, bit)]
            x = x + got
            bit *= 2
    found.append(x)


class Move:
    def __init__(self, line, job):
        self.line, self.job, self.flight = line, job, next(job)

    def step(self):
        if self.flight is None:
            return False
        got = list(lax.optimization_barrier((*self.flight, *self.line.due)))[: len(self.flight)]
        self.line.due = list(got)
        try:
            self.flight = self.job.send(got)
        except StopIteration:
            self.flight = None
        return self.flight is not None

    def end(self):
        while self.step():
            pass


def gelu_tanh(values):
    return jax.nn.gelu(values, approximate=True)


def rotary_tables(positions):
    seq = positions.shape[0]
    half_rot = ROT_DIM // 2
    expon = jnp.arange(half_rot, dtype=F32) * (2.0 / ROT_DIM)
    freqs = ROPE_BASE ** (-expon)
    angles = positions.astype(F32)[:, None] * freqs[None, :]
    cosine, sine = jnp.cos(angles), jnp.sin(angles)
    zero = jnp.zeros_like(sine)
    rest = jnp.zeros((seq, HEAD_DIM - ROT_DIM), F32)
    c = jnp.concatenate([cosine, cosine, rest + 1.0], axis=1)
    up = jnp.concatenate([zero, sine, rest], axis=1)
    down = jnp.concatenate([-sine, zero, rest], axis=1)
    return tuple(jnp.concatenate([t, t], axis=1) for t in (c, up, down))


def shards(inputs, out_grad, block_order, ln_gain, ln_beta, w_in, b_in, w_out, b_out):
    n_ctx, n_fsdp = lax.axis_size("ctx"), lax.axis_size("fsdp")
    z, f = lax.axis_index("ctx"), lax.axis_index("fsdp")
    seq_in, seq_grad, blk_order = inputs[0], out_grad[0], block_order[0]
    tok_rows = seq_in.shape[0]
    seq_len = tok_rows * n_ctx
    n_blk = blk_order.shape[0]
    blk_size = seq_len // n_blk
    per = n_blk // n_ctx
    wide_d = D // n_fsdp
    shard = w_out.shape[0]
    cat_rows = shard * n_fsdp
    in_cols = w_in.shape[1]
    n_heads = HEADS // n_ctx
    wide_a, wide_m = D // n_ctx, (cat_rows - D) // n_ctx
    even, att_runs, act_runs = plan(n_fsdp, n_ctx, cat_rows)
    z_runs = [in_runs(att_runs[i], act_runs[i]) for i in range(n_ctx)]

    def position_of(k):
        return lax.shift_right_logical(k, 1) + lax.bitwise_and(k, 1) * (n_fsdp // 2)

    def places(j):
        rank = lax.rem(z - j + n_ctx, n_ctx)
        return [blk_order[rank * per + i] * blk_size for i in range(per)]

    def taker(whole):
        def take(j):
            return jnp.concatenate(
                [lax.dynamic_slice_in_dim(whole, at, blk_size, 0) for at in places(j)], axis=0
            ).astype(F32)

        return take

    line = Line()
    rest = n_ctx - 1
    keys_at = {k: p for p, k in enumerate(key_order(n_fsdp))}
    share = shard // n_ctx
    mixed_f = [i for i in range(n_fsdp) if 0 < D - shard * i < shard]
    cut = (D - shard * mixed_f[0]) // n_ctx if mixed_f else share
    cut_m = share - cut
    is_mixed = (f == mixed_f[0]) if mixed_f else False

    def places_of(j, part):
        return (part, [(i * blk_size, blk_size, at) for i, at in enumerate(places(j))])

    def put_on(whole, pieces, rows):
        pieces = [(line.tied(pieces[0][0]), pieces[0][1])] + pieces[1:]
        whole = put(whole, pieces, rows)
        line.wait(whole)
        return whole

    def put_w_in(whole, parts):
        pieces = []
        for k, h, x in parts:
            rows = x.shape[0]
            pieces.append((x, [(0, rows, keys_at[k] * wide_d + (h or 0) * rows)]))
        return put_on(whole, pieces, D)

    def put_w_out(whole, parts):
        pieces = []
        for k, h, x in parts:
            rows = x.shape[0]
            pieces.append((x, [(0, rows, (f ^ k) * share + (h or 0) * rows)]))
        return put_on(whole, pieces, cat_rows // n_ctx)

    def own_rows(whole):
        first = lax.dynamic_slice_in_dim(whole, z * share, share, 0)
        if not cut_m:
            return first
        both = jnp.concatenate(
            [
                lax.dynamic_slice_in_dim(whole, z * cut, cut, 0),
                lax.dynamic_slice_in_dim(whole, cut * n_ctx + z * cut_m, cut_m, 0),
            ],
            axis=0,
        )
        return jnp.where(is_mixed, both, first)

    normed_parts, dy_parts, w_in_parts, w_out_parts = [], [], [], []
    w_in_own = pick_columns(w_in, z, z_runs)
    w_in_move = Move(line, gather_job(w_in_own, w_in_parts))
    line.wait(w_in_own)
    normed_own, dy_own = norm(line.tied(seq_in), seq_grad, ln_gain, ln_beta, f, n_fsdp)
    normed_ring = Move(line, ring_job(normed_own, normed_parts))
    line.wait(normed_own)
    w_in_all = put_w_in(None, [(0, None, w_in_own)])
    normed = put_on(None, [places_of(0, normed_own)], seq_len)
    tables = rotary_tables(line.tied(jnp.arange(seq_len, dtype=jnp.int32)))
    line.wait(*tables)
    b_in_z = jnp.stack([jnp.concatenate([b_in[s : s + n] for s, n in runs]) for runs in z_runs])[z]
    w_out_own = None
    if even:
        w_out_own = own_rows(line.tied(w_out))
        line.wait(w_out_own)

    def w_in_round():
        nonlocal w_in_all
        had = len(w_in_parts)
        w_in_move.step()
        if len(w_in_parts) > had:
            w_in_all = put_w_in(w_in_all, w_in_parts[had:])

    dy_ring = w_out_move = None
    for j in range(1, n_ctx):
        normed_ring.step()
        if j == rest:
            dy_ring = Move(line, ring_job(line.tied(dy_own), dy_parts))
        normed = put_on(normed, [places_of(j, normed_parts[j - 1])], seq_len)
        w_in_round()
        if j == 2 and even:
            w_out_move = Move(line, gather_job(line.tied(w_out_own), w_out_parts))
    while w_in_move.flight is not None:
        w_in_round()

    if not even:
        w_all = lax.all_gather(w_out, "fsdp", axis=0, tiled=True)
        w_out_z = jnp.concatenate(
            [
                lax.dynamic_slice_in_dim(w_all, z * wide_a, wide_a, 0),
                lax.dynamic_slice_in_dim(w_all, D + z * wide_m, wide_m, 0),
            ],
            axis=0,
        )
    wide_q = 3 * wide_a
    normed = line.tied(normed)
    qkv = jnp.dot(normed, w_in_all[:, :wide_q], preferred_element_type=F32) + b_in_z[:wide_q]
    line.wait(qkv)
    q_b, k_b, v_b, att_b, lse = attention(line.tied(qkv), tables, n_heads)
    line.wait(att_b)
    dy_ring.step()
    if even:
        w_out_move.step()
    normed_t = line.tied(normed)
    pre_act = jnp.dot(normed_t, w_in_all[:, wide_q:], preferred_element_type=F32) + b_in_z[wide_q:]
    act_b = gelu_tanh(pre_act).astype(BF)
    line.wait(act_b, pre_act)
    if even:
        w_out_move.step()
        cat_b = jnp.concatenate([line.tied(att_b), act_b], axis=1)
        line.wait(cat_b)
        w_out_move.end()
        w_out_z = put_w_out(None, [(0, None, w_out_own)] + w_out_parts)
    else:
        cat_b = jnp.concatenate([line.tied(att_b), act_b], axis=1)
    dy_ring.step()
    out_part = jnp.dot(line.tied(cat_b), w_out_z, preferred_element_type=F32)
    line.wait(out_part)
    out_sum, norm_sum = [], []
    out_move = Move(line, sum_job(taker(out_part), out_sum))

    dy_ring.end()
    dy = put_on(
        None, [places_of(j, part) for j, part in enumerate([dy_own] + dy_parts)], seq_len
    )
    d_cat = dot(line.tied(dy), w_out_z, 1, 1)
    line.wait(d_cat)
    out_move.step()
    d_cat = line.tied(d_cat)
    d_att = d_cat[:, :wide_a].astype(BF)
    d_pre = jax.vjp(gelu_tanh, pre_act)[1](d_cat[:, wide_a:])[0]
    d_pre_b = d_pre.astype(BF)
    sum_pre = jnp.sum(d_pre, axis=0)
    line.wait(d_pre_b, d_att, sum_pre)

    dq_b, dk_b, dv_b, s_q, s_k, s_v = attention_back(
        q_b, k_b, v_b, att_b, line.tied(d_att), lse, tables, n_heads
    )
    line.wait(dq_b)
    out_move.step()
    d_proj_b = jnp.concatenate([line.tied(dq_b), dk_b, dv_b, d_pre_b], axis=1)
    d_norm_part = dot(d_proj_b, w_in_all, 1, 1)
    line.wait(d_norm_part)
    norm_move = Move(line, sum_job(taker(d_norm_part), norm_sum))
    out_move.end()

    def weight_sum(left, right):
        return dot(line.tied(left), right, 0, 0).astype(BF)

    half = D // 2
    out_own, pre_own, qkv_own = [], [], []
    g_out = weight_sum(cat_b, dy)
    line.wait(g_out)
    if even:
        away, home = split(line.tied(g_out), f, n_fsdp)
        line.wait(away)
        out_scatter = Move(line, scatter_job(away, home, out_own))
    pre_away = weight_sum(normed[:, half:], d_pre_b)
    line.wait(pre_away)
    pre_scatter = Move(line, scatter_job(pre_away, lambda: pre_home, pre_own))
    norm_move.step()
    if even:
        out_scatter.step()
    pre_home = weight_sum(normed[:, :half], d_pre_b)
    line.wait(pre_home)
    qkv_away = weight_sum(normed[:, half:], d_proj_b[:, :wide_q])
    line.wait(qkv_away)
    qkv_scatter = Move(line, scatter_job(qkv_away, lambda: qkv_home, qkv_own))
    norm_move.step()
    qkv_home = weight_sum(normed[:, :half], d_proj_b[:, :wide_q])
    line.wait(qkv_home)
    if even:
        out_scatter.step()
    pre_scatter.step()
    norm_move.end()
    if even:
        out_scatter.end()
        out_parts = [out_own[0]]
        out_ring = Move(line, ring_job(out_own[0], out_parts))
    pre_scatter.step()

    seq_in_t = line.tied(seq_in)
    centred = seq_in_t - jnp.mean(seq_in_t, axis=1, keepdims=True)
    inv_std = lax.rsqrt(jnp.mean(centred * centred, axis=1, keepdims=True) + LN_EPS)
    x_hat = centred * inv_std
    d_norm = jnp.concatenate(
        [
            lax.dynamic_slice_in_dim(norm_sum[0], position_of(f ^ i) * wide_d, wide_d, 1)
            for i in range(n_fsdp)
        ],
        axis=1,
    )
    small = jnp.stack(
        [jnp.sum(seq_grad, axis=0), jnp.sum(d_norm * x_hat, axis=0), jnp.sum(d_norm, axis=0)]
    )
    gain_grad = d_norm * ln_gain
    d_input = seq_grad + inv_std * (
        gain_grad
        - jnp.mean(gain_grad, axis=1, keepdims=True)
        - x_hat * jnp.mean(gain_grad * x_hat, axis=1, keepdims=True)
    )
    out_y = seq_in + out_sum[0] + b_out

    g_b_in_z = jnp.concatenate([s_q.reshape(-1), s_k.reshape(-1), s_v.reshape(-1), sum_pre])
    masked = jnp.where(
        jnp.arange(n_ctx)[:, None] == z, g_b_in_z[None, :], jnp.zeros((), F32)
    )
    runs = sorted((s, n, i, at) for i in range(n_ctx) for s, n, at in run_offsets(z_runs[i]))
    vector = jnp.concatenate([small.reshape(-1)] + [masked[i, at : at + n] for _, n, i, at in runs])
    vectors = []
    vector_move = Move(line, total_job(vector, vectors))
    line.wait(vector, d_input, out_y)

    pre_runs = [[(s - 3 * D, n) for s, n in runs if s >= 3 * D] for runs in z_runs]
    qkv_runs = [[(s, n) for s, n in runs if s < 3 * D] for runs in z_runs]
    if even:
        out_ring.step()
    qkv_scatter.step()
    pre_scatter.end()
    pre_parts = [pre_own[0]]
    pre_ring = Move(line, ring_job(pre_own[0], pre_parts))
    if even:
        out_ring.step()
    qkv_scatter.end()
    qkv_parts = [qkv_own[0]]
    vector_move.step()
    pre_ring.step()
    if even:
        out_ring.step()
    vector_move.step()
    qkv_ring = Move(line, ring_job(qkv_own[0], qkv_parts))
    pre_ring.step()
    vector_move.step()
    pre_ring.end()
    g_w_in = spread_columns(None, pre_parts, z, pre_runs, in_cols, 3 * D, in_cols - 3 * D)
    line.wait(g_w_in)
    qkv_ring.step()
    vector_move.step()
    if even:
        g_w_out = jnp.zeros((shard, D), F32)
        for j, part in enumerate(out_parts):
            rank = lax.rem(z - j + n_ctx, n_ctx)
            part = part.astype(F32)
            at_a = jnp.where(is_mixed, rank * cut, rank * share)
            g_w_out = lax.dynamic_update_slice_in_dim(g_w_out, part[:cut], at_a, 0)
            if cut_m:
                at_m = jnp.where(is_mixed, cut * n_ctx + rank * cut_m, rank * share + cut)
                g_w_out = lax.dynamic_update_slice_in_dim(g_w_out, part[cut:], at_m, 0)
        line.wait(g_w_out)
    else:
        spread = jnp.zeros((cat_rows, D), BF)
        spread = lax.dynamic_update_slice_in_dim(spread, g_out[:wide_a], z * wide_a, 0)
        spread = lax.dynamic_update_slice_in_dim(spread, g_out[wide_a:], D + z * wide_m, 0)
        g_w_out = lax.psum_scatter(spread.astype(F32), "fsdp", scatter_dimension=0, tiled=True)
        g_w_out = lax.psum(g_w_out, "ctx")
    qkv_ring.step()
    vector_move.end()
    qkv_ring.end()
    g_w_in = spread_columns(g_w_in, qkv_parts, z, qkv_runs, in_cols, 0, 3 * D)
    small = vectors[0][: 3 * D].reshape(3, D)
    g_b_in = vectors[0][3 * D :]

    def own_part(vector):
        length_part = vector.shape[0] // n_fsdp
        return lax.dynamic_slice_in_dim(vector, f * length_part, length_part, 0)

    return (
        out_y[None],
        d_input[None],
        g_w_in,
        own_part(g_b_in),
        g_w_out,
        own_part(small[0]),
        own_part(small[1]),
        own_part(small[2]),
    )


def run_offsets(runs):
    at, found = 0, []
    for start, size in runs:
        found.append((start, size, at))
        at += size
    return found


def solution(mesh):
    placed = (
        P("fsdp", "ctx", None),
        P("fsdp", "ctx", None),
        P("fsdp", None),
        P(),
        P(),
        P("fsdp", None),
        P(),
        P("fsdp", None),
        P(),
    )
    return jax.shard_map(
        shards,
        mesh=mesh,
        in_specs=placed,
        out_specs=(
            P("fsdp", "ctx", None),
            P("fsdp", "ctx", None),
            P("fsdp", None),
            P("fsdp"),
            P("fsdp", None),
            P("fsdp"),
            P("fsdp"),
            P("fsdp"),
        ),
        check_vma=False,
    )
```

```python
import functools
import math

import jax
import jax.numpy as jnp
from jax import lax
from jax.experimental import pallas as pl
from jax.experimental.pallas import tpu as pltpu
from jax.sharding import PartitionSpec as P

D = 2048
HEADS = 32
HEAD_DIM = 64
ROT_DIM = 32

LN_EPS = 1e-05
NEG_BIG = -1e30
ROPE_BASE = 10000.0
BF = jnp.bfloat16
F32 = jnp.float32
VMEM_BYTES = 56 * 1024 * 1024
HBM_SPEC = pl.BlockSpec(memory_space=pltpu.HBM)


def plan(n_fsdp, n_ctx, cat_rows):
    shard = cat_rows // n_fsdp
    even = True
    att, act = [[] for _ in range(n_ctx)], [[] for _ in range(n_ctx)]
    for f in range(n_fsdp):
        a = min(max(D - shard * f, 0), shard)
        m = shard - a
        if a % (n_ctx * HEAD_DIM) or m % (n_ctx * 16):
            even = False
        for z in range(n_ctx):
            if a:
                att[z].append((shard * f + z * (a // n_ctx), a // n_ctx))
            if m:
                act[z].append((shard * f + a + z * (m // n_ctx), m // n_ctx))
    if not even:
        wide_a, wide_m = D // n_ctx, (cat_rows - D) // n_ctx
        att = [[(z * wide_a, wide_a)] for z in range(n_ctx)]
        act = [[(D + z * wide_m, wide_m)] for z in range(n_ctx)]
    return even, att, act


def in_runs(att, act):
    runs = [(part * D + s, n) for part in range(3) for s, n in att]
    return runs + [(2 * D + s, n) for s, n in act]


def key_order(n):
    return list(range(0, n, 2)) + list(range(1, n, 2))


def pick_kernel(all_runs, z_ref, src_ref, dst_ref):
    for z, runs in enumerate(all_runs):

        @pl.when(z_ref[0] == z)
        def _():
            at = 0
            for start, size in runs:
                dst_ref[:, at : at + size] = src_ref[:, start : start + size]
                at += size


def pick_columns(src, z, all_runs):
    rows, cols = src.shape
    width = sum(n for _, n in all_runs[0])
    step = min(rows, 64)
    return pl.pallas_call(
        functools.partial(pick_kernel, all_runs),
        grid_spec=pltpu.PrefetchScalarGridSpec(
            num_scalar_prefetch=1,
            grid=(rows // step,),
            in_specs=[pl.BlockSpec((step, cols), lambda i, z_ref: (i, 0))],
            out_specs=pl.BlockSpec((step, width), lambda i, z_ref: (i, 0)),
        ),
        out_shape=jax.ShapeDtypeStruct((rows, width), src.dtype),
        **big("pick_columns", 0, 2 * rows * (cols + width)),
    )(z[None], src)


def spread_kernel(all_runs, n_ctx, z_ref, *refs):
    srcs, dst_ref = refs[:n_ctx], refs[-1]
    for z in range(n_ctx):

        @pl.when(z_ref[0] == z)
        def _():
            for j, src_ref in enumerate(srcs):
                at = 0
                for start, size in all_runs[(z - j) % n_ctx]:
                    dst_ref[:, start : start + size] = src_ref[:, at : at + size].astype(F32)
                    at += size


def spread_columns(whole, parts, z, all_runs, cols, first, width_out):
    rows, width = parts[0].shape
    n_ctx = len(parts)
    step = min(rows, 64)
    fresh = whole is None
    return pl.pallas_call(
        functools.partial(spread_kernel, all_runs, n_ctx),
        grid_spec=pltpu.PrefetchScalarGridSpec(
            num_scalar_prefetch=1,
            grid=(rows // step,),
            in_specs=[pl.BlockSpec((step, width), lambda i, z_ref: (i, 0))] * n_ctx
            + [pl.BlockSpec(memory_space=pl.ANY)] * (not fresh),
            out_specs=pl.BlockSpec(
                (pl.Element(step), pl.Element(width_out)), lambda i, z_ref: (i * step, first)
            ),
        ),
        out_shape=jax.ShapeDtypeStruct((rows, cols), F32),
        input_output_aliases={} if fresh else {1 + n_ctx: 0},
        **big("spread_columns", 0, rows * width_out * 6),
    )(z[None], *parts, *([] if fresh else [whole]))


def norm_kernel(n_fsdp, f_ref, x_ref, g_ref, gain_ref, beta_ref, out_ref, dy_ref, hold):
    x = x_ref[...]
    centred = x - jnp.mean(x, axis=1, keepdims=True)
    inv_std = lax.rsqrt(jnp.mean(centred * centred, axis=1, keepdims=True) + LN_EPS)
    hold[...] = (centred * inv_std * gain_ref[...] + beta_ref[...]).astype(BF)
    wide = x.shape[1] // n_fsdp
    for p, k in enumerate(key_order(n_fsdp)):
        at = pl.multiple_of((f_ref[0] ^ k) * wide, wide)
        out_ref[:, p * wide : (p + 1) * wide] = hold[:, pl.ds(at, wide)]
    dy_ref[...] = g_ref[...].astype(BF)


def norm(x, g, gain, beta, f, n_fsdp):
    rows, cols = x.shape
    step = min(rows, 64)
    tile = pl.BlockSpec((step, cols), lambda i, f_ref: (i, 0))
    line = pl.BlockSpec((1, cols), lambda i, f_ref: (0, 0))
    own = jax.ShapeDtypeStruct((rows, cols), BF)
    return pl.pallas_call(
        functools.partial(norm_kernel, n_fsdp),
        grid_spec=pltpu.PrefetchScalarGridSpec(
            num_scalar_prefetch=1,
            grid=(rows // step,),
            in_specs=[tile, tile, line, line],
            out_specs=[tile, tile],
            scratch_shapes=[pltpu.VMEM((step, cols), BF)],
        ),
        out_shape=[own, own],
        **big("norm", 0, 12 * rows * cols),
    )(f[None], x, g, gain[None], beta[None])


def turn(u, c, s_up, s_down):
    half_rot = ROT_DIM // 2
    wide = u.shape[1]
    return (
        u * c
        + pltpu.roll(u, half_rot, 1) * s_up
        + pltpu.roll(u, wide - half_rot, 1) * s_down
    )


def dot(a, b, ca, cb):
    return lax.dot_general(a, b, (((ca,), (cb,)), ((), ())), preferred_element_type=F32)


def causal(size, keys, first):
    key_at = lax.broadcasted_iota(jnp.int32, (keys, size), 0)
    query_at = lax.broadcasted_iota(jnp.int32, (keys, size), 1) + first
    return key_at <= query_at


def att_kernel(q_ref, k_ref, v_ref, c_ref, u_ref, d_ref, qb_ref, kb_ref, vb_ref, att_ref, lse_ref):
    seq = q_ref.shape[0]
    size = math.gcd(seq, 256)
    c, su, sd = c_ref[...], u_ref[...], d_ref[...]
    qb_ref[...] = turn(q_ref[...], c, su, sd).astype(BF)
    kb_ref[...] = turn(k_ref[...], c, su, sd).astype(BF)
    vb_ref[...] = v_ref[...].astype(BF)
    scale = 1.0 / math.sqrt(HEAD_DIM)
    for i in range(seq // size):
        rows = slice(i * size, (i + 1) * size)
        keys = (i + 1) * size
        outs = []
        for h in range(2):
            lanes = slice(h * HEAD_DIM, (h + 1) * HEAD_DIM)
            s = dot(kb_ref[:keys, lanes], qb_ref[rows, lanes], 1, 1) * scale
            s = jnp.where(causal(size, keys, i * size), s, NEG_BIG)
            top = jnp.max(s, axis=0, keepdims=True)
            e = jnp.exp(s - top)
            total = jnp.sum(e, axis=0, keepdims=True)
            lse_ref[0, h : h + 1, rows] = top + jnp.log(total)
            p = (e * (1.0 / total)).astype(BF)
            outs.append(dot(p, vb_ref[:keys, lanes], 0, 0))
        att_ref[rows, :] = jnp.concatenate(outs, axis=1).astype(BF)


def attention(project, tables, n_heads, cat_width):
    seq = project.shape[0]
    pairs = n_heads // 2
    wide = 2 * HEAD_DIM

    def col(base):
        return pl.BlockSpec((seq, wide), lambda p: (0, base + p))

    table = pl.BlockSpec((seq, wide), lambda p: (0, 0))
    own = jax.ShapeDtypeStruct((seq, n_heads * HEAD_DIM), BF)
    return pl.pallas_call(
        att_kernel,
        grid=(pairs,),
        in_specs=[col(0), col(pairs), col(2 * pairs), table, table, table],
        out_specs=[col(0)] * 4 + [pl.BlockSpec((1, 2, seq), lambda p: (p, 0, 0))],
        out_shape=[own] * 3
        + [
            jax.ShapeDtypeStruct((seq, cat_width), BF),
            jax.ShapeDtypeStruct((pairs, 2, seq), F32),
        ],
        **big("attention", n_heads * seq * seq * 256, seq * n_heads * 64 * 20),
    )(project, project, project, *tables)


def back_kernel(
    pairs, q_ref, k_ref, v_ref, att_ref, datt_ref, lse_ref, c_ref, u_ref, d_ref, dproj_in,
    dproj_ref, sq_ref, sk_ref, sv_ref, aq, ak, av, hold, sems,
):
    del dproj_in
    seq = q_ref.shape[0]
    size = math.gcd(seq, 256)
    scale = 1.0 / math.sqrt(HEAD_DIM)
    ak[...] = jnp.zeros_like(ak)
    av[...] = jnp.zeros_like(av)
    for i in range(seq // size):
        rows = slice(i * size, (i + 1) * size)
        keys = (i + 1) * size
        dqs, dks, dvs = [], [], []
        prod = datt_ref[rows, :].astype(F32) * att_ref[rows, :].astype(F32)
        prod_t = prod.T
        for h in range(2):
            lanes = slice(h * HEAD_DIM, (h + 1) * HEAD_DIM)
            q, do = q_ref[rows, lanes], datt_ref[rows, lanes]
            k, v = k_ref[:keys, lanes], v_ref[:keys, lanes]
            delta = jnp.sum(prod_t[lanes, :], axis=0, keepdims=True)
            s = dot(k, q, 1, 1) * scale
            s = jnp.where(causal(size, keys, i * size), s, NEG_BIG)
            p = jnp.exp(s - lse_ref[0, h : h + 1, rows])
            dp = dot(v, do, 1, 1)
            ds = (p * (dp - delta) * scale).astype(BF)
            dvs.append(dot(p.astype(BF), do, 1, 0))
            dks.append(dot(ds, q, 1, 0))
            dqs.append(dot(ds, k, 0, 0))
        av[:keys, :] += jnp.concatenate(dvs, axis=1)
        ak[:keys, :] += jnp.concatenate(dks, axis=1)
        aq[rows, :] = jnp.concatenate(dqs, axis=1)
    wide = q_ref.shape[1]
    copies = []
    for i, (acc, total) in enumerate(((aq, sq_ref), (ak, sk_ref), (av, sv_ref))):
        g = acc[...]
        if i < 2:
            g = turn(g, c_ref[...], -u_ref[...], -d_ref[...])
        hold[i] = g.astype(BF)
        total[...] = jnp.sum(g, axis=0, keepdims=True)
        at = pl.multiple_of((i * pairs + pl.program_id(0)) * wide, wide)
        copies.append(
            pltpu.make_async_copy(hold.at[i], dproj_ref.at[:, pl.ds(at, wide)], sems.at[i])
        )
        copies[-1].start()
    for copy in copies:
        copy.wait()


def attention_back(q, k, v, cat, d_att, lse, tables, d_proj, n_heads):
    seq = q.shape[0]
    pairs = n_heads // 2
    wide = 2 * HEAD_DIM
    col = pl.BlockSpec((seq, wide), lambda p: (0, p))
    table = pl.BlockSpec((seq, wide), lambda p: (0, 0))
    line = pl.BlockSpec((1, wide), lambda p: (0, p))
    return pl.pallas_call(
        functools.partial(back_kernel, pairs),
        grid=(pairs,),
        in_specs=[col] * 5
        + [pl.BlockSpec((1, 2, seq), lambda p: (p, 0, 0))]
        + [table] * 3
        + [HBM_SPEC],
        out_specs=[HBM_SPEC] + [line] * 3,
        out_shape=[jax.ShapeDtypeStruct(d_proj.shape, BF)]
        + [jax.ShapeDtypeStruct((1, n_heads * HEAD_DIM), F32)] * 3,
        input_output_aliases={9: 0},
        scratch_shapes=[pltpu.VMEM((seq, wide), F32)] * 3
        + [pltpu.VMEM((3, seq, wide), BF), pltpu.SemaphoreType.DMA((3,))],
        **big("attention_back", n_heads * seq * seq * 640, seq * n_heads * 64 * 16),
    )(q, k, v, cat, d_att, lse, *tables, d_proj)


def grads_kernel(n_split, f_ref, left_ref, right_ref, *refs):
    outs, left_t = refs[:-1], refs[-1]

    @pl.when(pl.program_id(0) == 0)
    def _():
        left_t[...] = left_ref[...].T

    g = dot(left_t[...], right_ref[...], 1, 0).astype(BF)
    if len(outs) == 1:
        outs[0][...] = g
        return
    rows = g.shape[0] // n_split
    for s in range(n_split):
        key = lax.bitwise_xor(f_ref[0], s)
        at = pl.ds(pl.multiple_of(lax.shift_right_logical(key, 1) * rows, 16), rows)
        for i, out in enumerate(outs):

            @pl.when(lax.bitwise_and(key, 1) == 1 - i)
            def _():
                out[at, :] = g[s * rows : (s + 1) * rows]


def grads(left, block, wide, right, first, width, f, n_split=None):
    rows = left.shape[0]
    tile = math.gcd(512, math.gcd(width, first) if first else width)
    n_out = 2 if n_split else 1
    return pl.pallas_call(
        functools.partial(grads_kernel, n_split),
        grid_spec=pltpu.PrefetchScalarGridSpec(
            num_scalar_prefetch=1,
            grid=(width // tile,),
            in_specs=[
                pl.BlockSpec((rows, wide), lambda i, f_ref: (0, block)),
                pl.BlockSpec((rows, tile), lambda i, f_ref: (0, first // tile + i)),
            ],
            out_specs=[pl.BlockSpec((wide // n_out, tile), lambda i, f_ref: (0, i))] * n_out,
            scratch_shapes=[pltpu.VMEM((wide, rows), BF)],
        ),
        out_shape=[jax.ShapeDtypeStruct((wide // n_out, width), BF)] * n_out,
        **big("grads", 2 * rows * wide * width, 2 * rows * (wide + width) + 2 * wide * width),
    )(f[None], left, right)


def chunks(rows):
    step = math.gcd(rows, 256)
    return [slice(at, at + step) for at in range(0, rows, step)]


def gelu_parts(u):
    c = math.sqrt(2.0 / math.pi)
    square = u * u
    t = jnp.tanh(c * (u + 0.044715 * u * square))
    value = 0.5 * u * (1.0 + t)
    slope = 0.5 * (1.0 + t) + 0.5 * u * (1.0 - t * t) * (c * (1.0 + 3 * 0.044715 * square))
    return value, slope


def cost(flops, nbytes):
    return pl.CostEstimate(flops=flops, bytes_accessed=nbytes, transcendentals=0)


def big(name_of, flops, nbytes):
    return {
        "compiler_params": pltpu.CompilerParams(vmem_limit_bytes=VMEM_BYTES),
        "cost_estimate": cost(flops // 8, nbytes // 8),
        "name": name_of,
    }


def lay(parts, cuts, at_ref, base, dst):
    for c, (i, start, size) in enumerate(cuts):
        at = pl.multiple_of(at_ref[base + c], 16)
        dst[pl.ds(at, size), :] = parts[i][start : start + size, :]


def qkv_kernel(x_cuts, n_x, w_cuts, n_w, at_ref, *refs):
    xs, ws, b_ref = refs[:n_x], refs[n_x : n_x + n_w], refs[n_x + n_w]
    out_ref, x_ref, w_ref = refs[n_x + n_w + 1 :]

    @pl.when(pl.program_id(0) == 0)
    def _():
        lay(xs, x_cuts, at_ref, 0, x_ref)

    lay(ws, w_cuts, at_ref, len(x_cuts), w_ref)
    out_ref[...] = dot(x_ref[...], w_ref[...], 1, 0) + b_ref[...]


def qkv_project(xs, x_cuts, ws, w_cuts, places, b, rows, width, tile):
    deep, full = xs[0].shape[1], ws[0].shape[1]
    return pl.pallas_call(
        functools.partial(qkv_kernel, x_cuts, len(xs), w_cuts, len(ws)),
        grid_spec=pltpu.PrefetchScalarGridSpec(
            num_scalar_prefetch=1,
            grid=(width // tile,),
            in_specs=[pl.BlockSpec(x.shape, lambda i, at: (0, 0)) for x in xs]
            + [pl.BlockSpec((w.shape[0], tile), lambda i, at: (0, i)) for w in ws]
            + [pl.BlockSpec((1, tile), lambda i, at: (0, i))],
            out_specs=[
                pl.BlockSpec((rows, tile), lambda i, at: (0, i)),
                pl.BlockSpec((rows, deep), lambda i, at: (0, 0)),
                pl.BlockSpec((deep, tile), lambda i, at: (0, i)),
            ],
        ),
        out_shape=[
            jax.ShapeDtypeStruct((rows, width), F32),
            jax.ShapeDtypeStruct((rows, deep), BF),
            jax.ShapeDtypeStruct((deep, full), BF),
        ],
        **big("qkv_project", 2 * rows * deep * width, 2 * deep * (rows + width) + 4 * rows * width),
    )(places, *xs, *ws, b)


def pre_kernel(w_cuts, n_w, at_ref, x_ref, *refs):
    ws, b_ref = refs[:n_w], refs[n_w]
    slope_ref, cat_ref, w_ref = refs[-3:]
    lay(ws, w_cuts, at_ref, 0, w_ref)
    for rows in chunks(x_ref.shape[0]):
        pre = dot(x_ref[rows, :], w_ref[...], 1, 0) + b_ref[...]
        value, slope = gelu_parts(pre)
        slope_ref[rows, :] = slope
        cat_ref[rows, :] = value.astype(BF)


def pre_project(x, ws, w_cuts, places, b, cat, w_all, skip, tile):
    rows, deep = x.shape
    width = w_all.shape[1] - skip
    first, cat_first = skip // tile, (cat.shape[1] - width) // tile
    n_w = len(ws)
    return pl.pallas_call(
        functools.partial(pre_kernel, w_cuts, n_w),
        grid_spec=pltpu.PrefetchScalarGridSpec(
            num_scalar_prefetch=1,
            grid=(width // tile,),
            in_specs=[pl.BlockSpec((rows, deep), lambda i, at: (0, 0))]
            + [pl.BlockSpec((w.shape[0], tile), lambda i, at: (0, first + i)) for w in ws]
            + [pl.BlockSpec((1, tile), lambda i, at: (0, first + i))]
            + [pl.BlockSpec(memory_space=pl.ANY)] * 2,
            out_specs=[
                pl.BlockSpec((rows, tile), lambda i, at: (0, i)),
                pl.BlockSpec((rows, tile), lambda i, at: (0, cat_first + i)),
                pl.BlockSpec((deep, tile), lambda i, at: (0, first + i)),
            ],
        ),
        out_shape=[
            jax.ShapeDtypeStruct((rows, width), F32),
            jax.ShapeDtypeStruct(cat.shape, BF),
            jax.ShapeDtypeStruct(w_all.shape, BF),
        ],
        input_output_aliases={3 + n_w: 1, 4 + n_w: 2},
        **big("pre_project", 2 * rows * deep * width, 2 * deep * (rows + width) + 6 * rows * width),
    )(places, x, *ws, b, cat, w_all)


def give_shares(at_ref, acc, outs, per, blk_size):
    for j, out in enumerate(outs):
        for i in range(per):
            at = pl.multiple_of(at_ref[j * per + i], blk_size)
            out[i * blk_size : (i + 1) * blk_size, :] = acc[pl.ds(at, blk_size), :].astype(out.dtype)


def share_shapes(n_ctx, own, width):
    ups, downs = reach(n_ctx)
    kinds = [BF if j in (n_ctx - ups, downs) and j else F32 for j in range(n_ctx)]
    return [jax.ShapeDtypeStruct((own, width), kind) for kind in kinds]


def out_kernel(w_cuts, n_w, n_ctx, per, blk_size, at_ref, x_ref, *refs):
    ws, outs, w_ref, acc = refs[:n_w], refs[n_w : n_w + n_ctx], refs[-2], refs[-1]
    lay(ws, w_cuts, at_ref, n_ctx * per, w_ref)
    acc[...] = dot(x_ref[...], w_ref[...], 1, 0)
    give_shares(at_ref, acc, outs, per, blk_size)


def out_shares_of(x, ws, w_cuts, places, n_rows, n_ctx, blk_size):
    rows, deep = x.shape
    width = ws[0].shape[1]
    tile = min(512, width)
    per = n_rows // n_ctx
    own = rows // n_ctx
    col = pl.BlockSpec((own, tile), lambda i, at: (0, i))
    return pl.pallas_call(
        functools.partial(out_kernel, w_cuts, len(ws), n_ctx, per, blk_size),
        grid_spec=pltpu.PrefetchScalarGridSpec(
            num_scalar_prefetch=1,
            grid=(width // tile,),
            in_specs=[pl.BlockSpec((rows, deep), lambda i, at: (0, 0))]
            + [pl.BlockSpec((w.shape[0], tile), lambda i, at: (0, i)) for w in ws],
            out_specs=[col] * n_ctx + [pl.BlockSpec((deep, tile), lambda i, at: (0, i))],
            scratch_shapes=[pltpu.VMEM((rows, tile), F32)],
        ),
        out_shape=share_shapes(n_ctx, own, width) + [jax.ShapeDtypeStruct((deep, width), BF)],
        **big("out_shares", 2 * rows * deep * width, 2 * deep * (rows + width) + 3 * rows * width),
    )(places, x, *ws)


def norm_share_kernel(n_ctx, per, blk_size, at_ref, x_ref, w_ref, *refs):
    refs[-1][...] = dot(x_ref[...], w_ref[...], 1, 1)
    give_shares(at_ref, refs[-1], refs[:-1], per, blk_size)


def norm_shares_of(x, w, row_places, n_ctx, blk_size):
    rows, deep = x.shape
    width = w.shape[0]
    tile = min(256, width)
    per = row_places.shape[0] // n_ctx
    own = rows // n_ctx
    return pl.pallas_call(
        functools.partial(norm_share_kernel, n_ctx, per, blk_size),
        grid_spec=pltpu.PrefetchScalarGridSpec(
            num_scalar_prefetch=1,
            grid=(width // tile,),
            in_specs=[
                pl.BlockSpec((rows, deep), lambda i, at: (0, 0)),
                pl.BlockSpec((tile, deep), lambda i, at: (i, 0)),
            ],
            out_specs=[pl.BlockSpec((own, tile), lambda i, at: (0, i))] * n_ctx,
            scratch_shapes=[pltpu.VMEM((rows, tile), F32)],
        ),
        out_shape=share_shapes(n_ctx, own, width),
        **big("norm_shares", 2 * rows * deep * width, 2 * deep * (rows + width) + 3 * rows * width),
    )(row_places, x, w)


def d_cat_kernel(cuts, at_ref, g_ref, w_ref, slope_ref, datt_ref, dproj_ref, sum_ref, x_ref):
    @pl.when(pl.program_id(0) == 0)
    def _():
        lay([g_ref], cuts, at_ref, 0, x_ref)
        datt_ref[...] = dot(x_ref[...], w_ref[...], 1, 1).astype(BF)

    @pl.when(pl.program_id(0) > 0)
    def _():
        total = 0.0
        for rows in chunks(x_ref.shape[0]):
            d_pre = slope_ref[rows, :] * dot(x_ref[rows, :], w_ref[...], 1, 1)
            dproj_ref[rows, :] = d_pre.astype(BF)
            total = total + jnp.sum(d_pre, axis=0, keepdims=True)
        sum_ref[...] = total


def d_cat_parts(g, cuts, places, w, slope, wide_a):
    rows, deep = g.shape
    width = slope.shape[1]
    tile = wide_a
    total = 3 * wide_a + width

    def col(i):
        return jnp.maximum(i - 1, 0)

    return pl.pallas_call(
        functools.partial(d_cat_kernel, cuts),
        grid_spec=pltpu.PrefetchScalarGridSpec(
            num_scalar_prefetch=1,
            grid=(1 + width // tile,),
            in_specs=[
                pl.BlockSpec((rows, deep), lambda i, at: (0, 0)),
                pl.BlockSpec((tile, deep), lambda i, at: (i, 0)),
                pl.BlockSpec((rows, tile), lambda i, at: (0, col(i))),
            ],
            out_specs=[
                pl.BlockSpec((rows, tile), lambda i, at: (0, 0)),
                pl.BlockSpec((rows, tile), lambda i, at: (0, 3 + col(i))),
                pl.BlockSpec((1, tile), lambda i, at: (0, col(i))),
                pl.BlockSpec((rows, deep), lambda i, at: (0, 0)),
            ],
        ),
        out_shape=[
            jax.ShapeDtypeStruct((rows, tile), BF),
            jax.ShapeDtypeStruct((rows, total), BF),
            jax.ShapeDtypeStruct((1, width), F32),
            jax.ShapeDtypeStruct((rows, deep), BF),
        ],
        **big("d_cat_parts", 2 * rows * deep * (width + tile), 2 * deep * rows + (2 * deep + 6 * rows) * width),
    )(places, g, w, slope)


def after(x, *others):
    return lax.optimization_barrier((x, *others))[0]


def pass_on(x, hops):
    n = lax.axis_size("ctx")
    return lax.ppermute(x, "ctx", [(i, (i + hops) % n) for i in range(n)])


def reach(n):
    return n // 2, n - 1 - n // 2


def swap(x, axis, bit):
    n = lax.axis_size(axis)
    return lax.ppermute(x, axis, [(i, i ^ bit) for i in range(n)])


def near(x, bit):
    return swap(x, "fsdp", bit)


def far_keys(n):
    return sorted((k for k in range(2, n, 2)), key=lambda k: (k.bit_count(), k))


def top_bit(k):
    return 1 << (k.bit_length() - 1)


def low_bit(k):
    return k & -k


def halves(x):
    rows = x.shape[0] // 2
    return [x[:rows], x[rows:]]


class Line:
    def __init__(self):
        self.due = []

    def wait(self, *arrays):
        self.due += list(arrays)

    def tied(self, *xs):
        got = list(lax.optimization_barrier((*xs, *self.due)))[: len(xs)]
        self.due = got[:1]
        return got[0] if len(xs) == 1 else got


def ring_job(part, found):
    n = lax.axis_size("ctx")
    ups, downs = reach(n)
    found[0] = up = down = part
    for hop in range(1, ups + 1):
        if hop <= downs:
            up, down = yield [pass_on(up, 1), pass_on(down, -1)]
            found[n - hop] = down
        else:
            (up,) = yield [pass_on(up, 1)]
        found[hop] = up


def sum_job(parts, found):
    n = lax.axis_size("ctx")
    ups, downs = reach(n)
    up, down = parts[n - ups], parts[downs] if downs else None
    total = parts[0]
    for hop in range(ups):
        send = [pass_on(up.astype(BF), 1)]
        if hop < downs:
            send.append(pass_on(down.astype(BF), -1))
        got = yield send
        left = ups - 1 - hop
        if left:
            up = parts[n - left].astype(F32) + got[0].astype(F32)
        else:
            total = total + got[0].astype(F32)
        if hop < downs:
            left = downs - 1 - hop
            if left:
                down = parts[left].astype(F32) + got[1].astype(F32)
            else:
                total = total + got[1].astype(F32)
    found.append(total)


def total_job(x, found):
    for axis in ("fsdp", "ctx"):
        bit = 1
        while bit < lax.axis_size(axis):
            (got,) = yield [swap(x, axis, bit)]
            x = x + got
            bit *= 2
    found.append(x)


def gather_job(shard, found):
    n = lax.axis_size("fsdp")
    have = {}
    keys = far_keys(n)
    fresh = [(0, None, shard)]
    found.extend(fresh)
    level = 0
    while True:
        level += 1
        send = []
        for k in keys:
            if k.bit_count() != level:
                continue
            if level == 1:
                send.append((k, None, near(shard, k)))
            else:
                for h, bit in ((0, top_bit(k)), (1, low_bit(k))):
                    send.append((k, h, near(have[k ^ bit, h], bit)))
        send += [(k | 1, h, near(x, 1)) for k, h, x in fresh if not k & 1]
        if not send:
            return
        got = yield [x for _, _, x in send]
        fresh = [(k, h, x) for (k, h, _), x in zip(send, got)]
        found.extend(fresh)
        for k, h, x in fresh:
            if not k & 1:
                if h is None:
                    have[k, 0], have[k, 1] = halves(x)
                else:
                    have[k, h] = x


def gather_order(n):
    got = [(0, None)]
    fresh = list(got)
    level = 0
    while True:
        level += 1
        new = []
        for k in far_keys(n):
            if k.bit_count() == level:
                new += [(k, None)] if level == 1 else [(k, 0), (k, 1)]
        new += [(k | 1, h) for k, h in fresh if not k & 1]
        if not new:
            return got
        got += new
        fresh = new


def scatter_job(away, home, found):
    n = lax.axis_size("fsdp")
    (got,) = yield [near(away, 1)]
    home = home() if callable(home) else home
    rows = home.shape[0] // (n // 2)
    hold = {}
    for i, k in enumerate(range(0, n, 2)):
        for h in range(2):
            at = i * rows + h * (rows // 2)
            cut = slice(at, at + rows // 2)
            hold[k, h] = home[cut].astype(F32) + got[cut].astype(F32)
    for level in range(n.bit_length() - 2, 0, -1):
        moves = []
        for k in far_keys(n):
            if k.bit_count() != level:
                continue
            if level > 1:
                for h, bit in ((0, top_bit(k)), (1, low_bit(k))):
                    moves.append((k ^ bit, h, near(hold[k, h].astype(BF), bit)))
            else:
                whole = jnp.concatenate([hold[k, 0], hold[k, 1]], axis=0).astype(BF)
                moves.append((0, None, near(whole, k)))
        got = yield [x for _, _, x in moves]
        for (k, h, _), x in zip(moves, got):
            if h is None:
                for i, part in enumerate(halves(x)):
                    hold[k, i] = hold[k, i] + part.astype(F32)
            else:
                hold[k, h] = hold[k, h] + x.astype(F32)
    found.append(jnp.concatenate([hold[0, 0], hold[0, 1]], axis=0).astype(BF))


class Move:
    def __init__(self, line, job):
        self.line, self.job, self.flight = line, job, next(job)

    def step(self, *more):
        moves = [m for m in (self, *more) if m.flight is not None]
        flights = [x for m in moves for x in m.flight]
        if not moves:
            return
        got = list(lax.optimization_barrier((*flights, *self.line.due)))[: len(flights)]
        self.line.due = list(got)
        for m in moves:
            own, got = got[: len(m.flight)], got[len(m.flight) :]
            try:
                m.flight = m.job.send(own)
            except StopIteration:
                m.flight = None

    def end(self, *more):
        while self.flight is not None:
            self.step(*more)


def gelu_tanh(values):
    return jax.nn.gelu(values, approximate=True)


def rotary_tables(positions):
    seq = positions.shape[0]
    half_rot = ROT_DIM // 2
    expon = jnp.arange(half_rot, dtype=F32) * (2.0 / ROT_DIM)
    freqs = ROPE_BASE ** (-expon)
    angles = positions.astype(F32)[:, None] * freqs[None, :]
    cosine, sine = jnp.cos(angles), jnp.sin(angles)
    zero = jnp.zeros_like(sine)
    rest = jnp.zeros((seq, HEAD_DIM - ROT_DIM), F32)
    c = jnp.concatenate([cosine, cosine, rest + 1.0], axis=1)
    up = jnp.concatenate([zero, sine, rest], axis=1)
    down = jnp.concatenate([-sine, zero, rest], axis=1)
    return tuple(jnp.concatenate([t, t], axis=1) for t in (c, up, down))


def shards(inputs, out_grad, block_order, ln_gain, ln_beta, w_in, b_in, w_out, b_out):
    n_ctx, n_fsdp = lax.axis_size("ctx"), lax.axis_size("fsdp")
    z, f = lax.axis_index("ctx"), lax.axis_index("fsdp")
    seq_in, seq_grad, blk_order = inputs[0], out_grad[0], block_order[0]
    tok_rows = seq_in.shape[0]
    seq_len = tok_rows * n_ctx
    n_blk = blk_order.shape[0]
    blk_size = seq_len // n_blk
    per = n_blk // n_ctx
    wide_d = D // n_fsdp
    shard = w_out.shape[0]
    cat_rows = shard * n_fsdp
    in_cols = w_in.shape[1]
    n_heads = HEADS // n_ctx
    wide_a, wide_m = D // n_ctx, (cat_rows - D) // n_ctx
    even, att_runs, act_runs = plan(n_fsdp, n_ctx, cat_rows)
    z_runs = [in_runs(att_runs[i], act_runs[i]) for i in range(n_ctx)]

    def position_of(k):
        return lax.shift_right_logical(k, 1) + lax.bitwise_and(k, 1) * (n_fsdp // 2)

    rank_places = blk_order * blk_size
    ranks = lax.rem(z - jnp.arange(n_ctx, dtype=jnp.int32) + n_ctx, n_ctx)
    picks = (ranks[:, None] == jnp.arange(n_ctx, dtype=jnp.int32)[None, :]).astype(jnp.int32)
    row_places = jnp.sum(
        picks[:, :, None] * rank_places.reshape(1, n_ctx, per), axis=1, dtype=jnp.int32
    ).reshape(-1)

    line = Line()
    keys_at = {k: p for p, k in enumerate(key_order(n_fsdp))}
    share = shard // n_ctx
    mixed_f = [i for i in range(n_fsdp) if 0 < D - shard * i < shard]
    cut = (D - shard * mixed_f[0]) // n_ctx if mixed_f else share
    cut_m = share - cut
    is_mixed = (f == mixed_f[0]) if mixed_f else False

    def own_rows(whole):
        first = lax.dynamic_slice_in_dim(whole, z * share, share, 0)
        if not cut_m:
            return first
        both = jnp.concatenate(
            [
                lax.dynamic_slice_in_dim(whole, z * cut, cut, 0),
                lax.dynamic_slice_in_dim(whole, cut * n_ctx + z * cut_m, cut_m, 0),
            ],
            axis=0,
        )
        return jnp.where(is_mixed, both, first)

    def cuts_of(found):
        return [x for _, _, x in found], tuple((i, 0, x.shape[0]) for i, (_, _, x) in enumerate(found))

    order = gather_order(n_fsdp)
    w_at = jnp.asarray(
        [keys_at[k] * wide_d + (h or 0) * (wide_d // 2) for k, h in order], jnp.int32
    )
    o_keys = jnp.asarray([k for k, _ in order], jnp.int32)
    o_at = lax.bitwise_xor(f, o_keys) * share + jnp.asarray(
        [(h or 0) * (share // 2) for _, h in order], jnp.int32
    )
    qkv_at = jnp.concatenate([row_places, w_at])
    o_at = jnp.concatenate([row_places, o_at if even else jnp.zeros((1,), jnp.int32)])

    normed_parts, w_in_parts, w_out_parts = {}, [], []
    w_in_own = pick_columns(w_in, z, z_runs)
    w_in_move = Move(line, gather_job(w_in_own, w_in_parts))
    line.wait(w_in_own)
    normed_own, dy_own = norm(line.tied(seq_in), seq_grad, ln_gain, ln_beta, f, n_fsdp)
    normed_ring = Move(line, ring_job(normed_own, normed_parts))
    line.wait(normed_own)
    tables = rotary_tables(line.tied(jnp.arange(seq_len, dtype=jnp.int32)))
    line.wait(*tables)
    b_in_z = jnp.stack([jnp.concatenate([b_in[s : s + n] for s, n in runs]) for runs in z_runs])[z]
    b_in_z = b_in_z[None]
    w_out_own = own_rows(line.tied(w_out)) if even else w_out
    line.wait(w_out_own, b_in_z, qkv_at, o_at, w_at, rank_places, row_places)

    while normed_ring.flight is not None:
        normed_ring.step(w_in_move)
    dy_all = lax.all_gather(after(dy_own, *line.due), "ctx", axis=0, tiled=True)
    if even:
        w_out_move = Move(line, gather_job(line.tied(w_out_own), w_out_parts))
    w_in_move.end()

    wide_q = 3 * wide_a
    x_cuts = [(j, i * blk_size, blk_size) for j in range(n_ctx) for i in range(per)]
    w_arrays, w_cuts = cuts_of(w_in_parts)
    xs = [normed_parts[j] for j in range(n_ctx)]
    qkv, normed, w_in_all = qkv_project(
        [line.tied(xs[0])] + xs[1:], tuple(x_cuts), w_arrays, w_cuts, qkv_at,
        b_in_z, seq_len, wide_q, wide_a,
    )
    line.wait(qkv)
    q_b, k_b, v_b, cat_b, lse = attention(line.tied(qkv), tables, n_heads, cat_rows // n_ctx)
    line.wait(cat_b)
    if even:
        w_out_move.step()
    slope, cat_b, w_in_all = pre_project(
        line.tied(normed), w_arrays, w_cuts, w_at, b_in_z, cat_b, w_in_all, wide_q, wide_a
    )
    line.wait(cat_b)
    if even:
        w_out_move.end()
        o_arrays, o_cuts = cuts_of(w_out_parts)
    else:
        w_all = lax.all_gather(w_out, "fsdp", axis=0, tiled=True)
        w_all = jnp.concatenate(
            [
                lax.dynamic_slice_in_dim(w_all, z * wide_a, wide_a, 0),
                lax.dynamic_slice_in_dim(w_all, D + z * wide_m, wide_m, 0),
            ],
            axis=0,
        )
        o_arrays, o_cuts = [w_all], ((0, 0, cat_rows // n_ctx),)
    *out_shares, w_out_z = out_shares_of(
        line.tied(cat_b), o_arrays, o_cuts, o_at, n_ctx * per, n_ctx, blk_size
    )
    line.wait(*out_shares)
    out_sum, norm_sum = [], []
    out_move = Move(line, sum_job(line.tied(*out_shares), out_sum))

    row_cuts = tuple((0, i * blk_size, blk_size) for i in range(n_blk))
    line.wait(dy_all)
    d_att, d_proj, sum_pre, dy = d_cat_parts(
        line.tied(dy_all), row_cuts, rank_places, w_out_z, slope, wide_a
    )
    line.wait(d_att)
    away, home = grads(line.tied(cat_b), 0, cat_rows // n_ctx, dy, 0, D, f, n_fsdp)
    line.wait(away)
    out_move.step()
    out_own, pre_own, qkv_own = [], [], []
    out_moves = [Move(line, scatter_job(line.tied(away), home, out_own))] if even else []

    d_proj, *sum_qkv = attention_back(
        q_b, k_b, v_b, cat_b, line.tied(d_att), lse, tables, d_proj, n_heads
    )
    line.wait(d_proj)
    out_move.step(*out_moves)
    norm_shares = norm_shares_of(line.tied(d_proj), w_in_all, row_places, n_ctx, blk_size)
    line.wait(*norm_shares)
    out_move.end()
    if even:
        out_moves[0].step()
    norm_move = Move(line, sum_job(line.tied(*norm_shares), norm_sum))

    half = D // 2
    pre_parts, qkv_parts = {}, {}
    (pre_away,) = grads(line.tied(normed), 1, half, d_proj, wide_q, wide_m, f)
    (pre_home,) = grads(after(normed, pre_away), 0, half, d_proj, wide_q, wide_m, f)
    (qkv_away,) = grads(after(normed, pre_home), 1, half, d_proj, 0, wide_q, f)
    (qkv_home,) = grads(after(normed, qkv_away), 0, half, d_proj, 0, wide_q, f)
    line.wait(qkv_home)
    norm_move.step(*out_moves)
    if even:
        out_all = lax.all_gather(line.tied(out_own[0]), "ctx", axis=0)
    pre_scatter = Move(line, scatter_job(line.tied(pre_away), pre_home, pre_own))
    qkv_scatter = Move(line, scatter_job(line.tied(qkv_away), qkv_home, qkv_own))
    pre_scatter.step()
    pre_scatter.step()
    norm_move.end()

    seq_in_t = line.tied(seq_in)
    centred = seq_in_t - jnp.mean(seq_in_t, axis=1, keepdims=True)
    inv_std = lax.rsqrt(jnp.mean(centred * centred, axis=1, keepdims=True) + LN_EPS)
    x_hat = centred * inv_std
    d_norm = jnp.concatenate(
        [
            lax.dynamic_slice_in_dim(norm_sum[0], position_of(f ^ i) * wide_d, wide_d, 1)
            for i in range(n_fsdp)
        ],
        axis=1,
    )
    small = jnp.stack(
        [jnp.sum(seq_grad, axis=0), jnp.sum(d_norm * x_hat, axis=0), jnp.sum(d_norm, axis=0)]
    )
    gain_grad = d_norm * ln_gain
    d_input = seq_grad + inv_std * (
        gain_grad
        - jnp.mean(gain_grad, axis=1, keepdims=True)
        - x_hat * jnp.mean(gain_grad * x_hat, axis=1, keepdims=True)
    )
    out_y = seq_in + out_sum[0] + b_out

    g_b_in_z = jnp.concatenate([x[0] for x in (*sum_qkv, sum_pre)])
    masked = jnp.where(
        jnp.arange(n_ctx)[:, None] == z, g_b_in_z[None, :], jnp.zeros((), F32)
    )
    runs = sorted((s, n, i, at) for i in range(n_ctx) for s, n, at in run_offsets(z_runs[i]))
    vector = jnp.concatenate([small.reshape(-1)] + [masked[i, at : at + n] for _, n, i, at in runs])
    vectors = []
    vector_move = Move(line, total_job(vector, vectors))
    line.wait(d_input, out_y)

    pre_runs = [[(s - 3 * D, n) for s, n in runs if s >= 3 * D] for runs in z_runs]
    qkv_runs = [[(s, n) for s, n in runs if s < 3 * D] for runs in z_runs]
    pre_scatter.end(qkv_scatter, vector_move)
    pre_ring = Move(line, ring_job(line.tied(pre_own[0]), pre_parts))
    qkv_scatter.step()
    qkv_scatter.end(vector_move)
    if even:
        g_w_out = jnp.zeros((shard, D), F32)
        for rank in range(n_ctx):
            part = out_all[rank].astype(F32)
            at_a = jnp.where(is_mixed, rank * cut, rank * share)
            g_w_out = lax.dynamic_update_slice_in_dim(g_w_out, part[:cut], at_a, 0)
            if cut_m:
                at_m = jnp.where(is_mixed, cut * n_ctx + rank * cut_m, rank * share + cut)
                g_w_out = lax.dynamic_update_slice_in_dim(g_w_out, part[cut:], at_m, 0)
    else:
        blocks = jnp.concatenate([home, away], axis=0).reshape(n_fsdp, -1, D)
        g_out = jnp.concatenate(
            [lax.dynamic_index_in_dim(blocks, position_of(f ^ i), 0, False) for i in range(n_fsdp)]
        )
        spread = jnp.zeros((cat_rows, D), BF)
        spread = lax.dynamic_update_slice_in_dim(spread, g_out[:wide_a], z * wide_a, 0)
        spread = lax.dynamic_update_slice_in_dim(spread, g_out[wide_a:], D + z * wide_m, 0)
        g_w_out = lax.psum_scatter(spread.astype(F32), "fsdp", scatter_dimension=0, tiled=True)
        g_w_out = lax.psum(g_w_out, "ctx")
    pre_ring.step(vector_move)
    pre_ring.end(vector_move)
    qkv_ring = Move(line, ring_job(line.tied(qkv_own[0]), qkv_parts))
    in_turn = range(n_ctx)
    g_w_in = spread_columns(
        None,
        [line.tied(pre_parts[0])] + [pre_parts[j] for j in in_turn[1:]],
        z, pre_runs, in_cols, 3 * D, in_cols - 3 * D,
    )
    line.wait(g_w_in)
    vector_move.end(qkv_ring)
    qkv_ring.end()
    g_w_in = spread_columns(
        g_w_in, [qkv_parts[j] for j in in_turn], z, qkv_runs, in_cols, 0, 3 * D
    )
    vector = vectors[0]
    small = vector[: 3 * D].reshape(3, D)
    g_b_in = vector[3 * D :]

    def own_part(vector):
        length_part = vector.shape[0] // n_fsdp
        return lax.dynamic_slice_in_dim(vector, f * length_part, length_part, 0)

    return (
        out_y[None],
        d_input[None],
        g_w_in,
        own_part(g_b_in),
        g_w_out,
        own_part(small[0]),
        own_part(small[1]),
        own_part(small[2]),
    )


def run_offsets(runs):
    at, found = 0, []
    for start, size in runs:
        found.append((start, size, at))
        at += size
    return found


def solution(mesh):
    placed = (
        P("fsdp", "ctx", None),
        P("fsdp", "ctx", None),
        P("fsdp", None),
        P(),
        P(),
        P("fsdp", None),
        P(),
        P("fsdp", None),
        P(),
    )
    return jax.shard_map(
        shards,
        mesh=mesh,
        in_specs=placed,
        out_specs=(
            P("fsdp", "ctx", None),
            P("fsdp", "ctx", None),
            P("fsdp", None),
            P("fsdp"),
            P("fsdp", None),
            P("fsdp"),
            P("fsdp"),
            P("fsdp"),
        ),
        check_vma=False,
    )
```

```python
import functools
import math

import jax
import jax.numpy as jnp
from jax import lax
from jax.experimental import pallas as pl
from jax.experimental.pallas import tpu as pltpu
from jax.sharding import PartitionSpec as P

D = 2048
HEADS = 32
HEAD_DIM = 64
ROT_DIM = 32

LN_EPS = 1e-05
NEG_BIG = -1e30
ROPE_BASE = 10000.0
BF = jnp.bfloat16
F32 = jnp.float32
VMEM_BYTES = 56 * 1024 * 1024
HBM_SPEC = pl.BlockSpec(memory_space=pltpu.HBM)


def plan(n_fsdp, n_ctx, cat_rows):
    shard = cat_rows // n_fsdp
    even = True
    att, act = [[] for _ in range(n_ctx)], [[] for _ in range(n_ctx)]
    for f in range(n_fsdp):
        a = min(max(D - shard * f, 0), shard)
        m = shard - a
        if a % (n_ctx * HEAD_DIM) or m % (n_ctx * 16):
            even = False
        for z in range(n_ctx):
            if a:
                att[z].append((shard * f + z * (a // n_ctx), a // n_ctx))
            if m:
                act[z].append((shard * f + a + z * (m // n_ctx), m // n_ctx))
    if not even:
        wide_a, wide_m = D // n_ctx, (cat_rows - D) // n_ctx
        att = [[(z * wide_a, wide_a)] for z in range(n_ctx)]
        act = [[(D + z * wide_m, wide_m)] for z in range(n_ctx)]
    return even, att, act


def in_runs(att, act):
    runs = [(part * D + s, n) for part in range(3) for s, n in att]
    return runs + [(2 * D + s, n) for s, n in act]


def key_order(n):
    return list(range(0, n, 2)) + list(range(1, n, 2))


def pick_kernel(all_runs, z_ref, src_ref, dst_ref):
    for z, runs in enumerate(all_runs):

        @pl.when(z_ref[0] == z)
        def _():
            at = 0
            for start, size in runs:
                dst_ref[:, at : at + size] = src_ref[:, start : start + size]
                at += size


def pick_columns(src, z, all_runs):
    rows, cols = src.shape
    width = sum(n for _, n in all_runs[0])
    step = min(rows, 64)
    return pl.pallas_call(
        functools.partial(pick_kernel, all_runs),
        grid_spec=pltpu.PrefetchScalarGridSpec(
            num_scalar_prefetch=1,
            grid=(rows // step,),
            in_specs=[pl.BlockSpec((step, cols), lambda i, z_ref: (i, 0))],
            out_specs=pl.BlockSpec((step, width), lambda i, z_ref: (i, 0)),
        ),
        out_shape=jax.ShapeDtypeStruct((rows, width), src.dtype),
        **big("pick_columns", 0, 2 * rows * (cols + width)),
    )(z[None], src)


def spread_kernel(all_runs, n_ctx, z_ref, *refs):
    srcs, dst_ref = refs[:n_ctx], refs[-1]
    for z in range(n_ctx):

        @pl.when(z_ref[0] == z)
        def _():
            for j, src_ref in enumerate(srcs):
                at = 0
                for start, size in all_runs[(z - j) % n_ctx]:
                    dst_ref[:, start : start + size] = src_ref[:, at : at + size].astype(F32)
                    at += size


def spread_columns(whole, parts, z, all_runs, cols, first, width_out):
    rows, width = parts[0].shape
    n_ctx = len(parts)
    step = min(rows, 64)
    fresh = whole is None
    return pl.pallas_call(
        functools.partial(spread_kernel, all_runs, n_ctx),
        grid_spec=pltpu.PrefetchScalarGridSpec(
            num_scalar_prefetch=1,
            grid=(rows // step,),
            in_specs=[pl.BlockSpec((step, width), lambda i, z_ref: (i, 0))] * n_ctx
            + [pl.BlockSpec(memory_space=pl.ANY)] * (not fresh),
            out_specs=pl.BlockSpec(
                (pl.Element(step), pl.Element(width_out)), lambda i, z_ref: (i * step, first)
            ),
        ),
        out_shape=jax.ShapeDtypeStruct((rows, cols), F32),
        input_output_aliases={} if fresh else {1 + n_ctx: 0},
        **big("spread_columns", 0, rows * width_out * 6),
    )(z[None], *parts, *([] if fresh else [whole]))


def norm_kernel(n_fsdp, f_ref, x_ref, g_ref, gain_ref, beta_ref, out_ref, dy_ref, hold):
    x = x_ref[...]
    centred = x - jnp.mean(x, axis=1, keepdims=True)
    inv_std = lax.rsqrt(jnp.mean(centred * centred, axis=1, keepdims=True) + LN_EPS)
    hold[...] = (centred * inv_std * gain_ref[...] + beta_ref[...]).astype(BF)
    wide = x.shape[1] // n_fsdp
    for p, k in enumerate(key_order(n_fsdp)):
        at = pl.multiple_of((f_ref[0] ^ k) * wide, wide)
        out_ref[:, p * wide : (p + 1) * wide] = hold[:, pl.ds(at, wide)]
    dy_ref[...] = g_ref[...].astype(BF)


def norm(x, g, gain, beta, f, n_fsdp):
    rows, cols = x.shape
    step = min(rows, 64)
    tile = pl.BlockSpec((step, cols), lambda i, f_ref: (i, 0))
    line = pl.BlockSpec((1, cols), lambda i, f_ref: (0, 0))
    own = jax.ShapeDtypeStruct((rows, cols), BF)
    return pl.pallas_call(
        functools.partial(norm_kernel, n_fsdp),
        grid_spec=pltpu.PrefetchScalarGridSpec(
            num_scalar_prefetch=1,
            grid=(rows // step,),
            in_specs=[tile, tile, line, line],
            out_specs=[tile, tile],
            scratch_shapes=[pltpu.VMEM((step, cols), BF)],
        ),
        out_shape=[own, own],
        **big("norm", 0, 12 * rows * cols),
    )(f[None], x, g, gain[None], beta[None])


def turn(u, c, s_up, s_down):
    half_rot = ROT_DIM // 2
    wide = u.shape[1]
    return (
        u * c
        + pltpu.roll(u, half_rot, 1) * s_up
        + pltpu.roll(u, wide - half_rot, 1) * s_down
    )


def dot(a, b, ca, cb):
    return lax.dot_general(a, b, (((ca,), (cb,)), ((), ())), preferred_element_type=F32)


def causal(size, keys, first):
    key_at = lax.broadcasted_iota(jnp.int32, (keys, size), 0)
    query_at = lax.broadcasted_iota(jnp.int32, (keys, size), 1) + first
    return key_at <= query_at


def att_kernel(q_ref, k_ref, v_ref, c_ref, u_ref, d_ref, qb_ref, kb_ref, vb_ref, att_ref, lse_ref):
    seq = q_ref.shape[0]
    size = math.gcd(seq, 256)
    c, su, sd = c_ref[...], u_ref[...], d_ref[...]
    qb_ref[...] = turn(q_ref[...], c, su, sd).astype(BF)
    kb_ref[...] = turn(k_ref[...], c, su, sd).astype(BF)
    vb_ref[...] = v_ref[...].astype(BF)
    scale = 1.0 / math.sqrt(HEAD_DIM)
    for i in range(seq // size):
        rows = slice(i * size, (i + 1) * size)
        keys = (i + 1) * size
        outs = []
        for h in range(2):
            lanes = slice(h * HEAD_DIM, (h + 1) * HEAD_DIM)
            s = dot(kb_ref[:keys, lanes], qb_ref[rows, lanes], 1, 1) * scale
            s = jnp.where(causal(size, keys, i * size), s, NEG_BIG)
            top = jnp.max(s, axis=0, keepdims=True)
            e = jnp.exp(s - top)
            total = jnp.sum(e, axis=0, keepdims=True)
            lse_ref[0, h : h + 1, rows] = top + jnp.log(total)
            p = (e * (1.0 / total)).astype(BF)
            outs.append(dot(p, vb_ref[:keys, lanes], 0, 0))
        att_ref[rows, :] = jnp.concatenate(outs, axis=1).astype(BF)


def attention(project, tables, n_heads, cat_width):
    seq = project.shape[0]
    pairs = n_heads // 2
    wide = 2 * HEAD_DIM

    def col(base):
        return pl.BlockSpec((seq, wide), lambda p: (0, base + p))

    table = pl.BlockSpec((seq, wide), lambda p: (0, 0))
    own = jax.ShapeDtypeStruct((seq, n_heads * HEAD_DIM), BF)
    return pl.pallas_call(
        att_kernel,
        grid=(pairs,),
        in_specs=[col(0), col(pairs), col(2 * pairs), table, table, table],
        out_specs=[col(0)] * 4 + [pl.BlockSpec((1, 2, seq), lambda p: (p, 0, 0))],
        out_shape=[own] * 3
        + [
            jax.ShapeDtypeStruct((seq, cat_width), BF),
            jax.ShapeDtypeStruct((pairs, 2, seq), F32),
        ],
        **big("attention", n_heads * seq * seq * 256, seq * n_heads * 64 * 20),
    )(project, project, project, *tables)


def back_kernel(
    pairs, q_ref, k_ref, v_ref, att_ref, datt_ref, lse_ref, c_ref, u_ref, d_ref, dproj_in,
    dproj_ref, sq_ref, sk_ref, sv_ref, aq, ak, av, hold, sems,
):
    del dproj_in
    seq = q_ref.shape[0]
    size = math.gcd(seq, 256)
    scale = 1.0 / math.sqrt(HEAD_DIM)
    ak[...] = jnp.zeros_like(ak)
    av[...] = jnp.zeros_like(av)
    for i in range(seq // size):
        rows = slice(i * size, (i + 1) * size)
        keys = (i + 1) * size
        dqs, dks, dvs = [], [], []
        prod = datt_ref[rows, :].astype(F32) * att_ref[rows, :].astype(F32)
        prod_t = prod.T
        for h in range(2):
            lanes = slice(h * HEAD_DIM, (h + 1) * HEAD_DIM)
            q, do = q_ref[rows, lanes], datt_ref[rows, lanes]
            k, v = k_ref[:keys, lanes], v_ref[:keys, lanes]
            delta = jnp.sum(prod_t[lanes, :], axis=0, keepdims=True)
            s = dot(k, q, 1, 1) * scale
            s = jnp.where(causal(size, keys, i * size), s, NEG_BIG)
            p = jnp.exp(s - lse_ref[0, h : h + 1, rows])
            dp = dot(v, do, 1, 1)
            ds = (p * (dp - delta) * scale).astype(BF)
            dvs.append(dot(p.astype(BF), do, 1, 0))
            dks.append(dot(ds, q, 1, 0))
            dqs.append(dot(ds, k, 0, 0))
        av[:keys, :] += jnp.concatenate(dvs, axis=1)
        ak[:keys, :] += jnp.concatenate(dks, axis=1)
        aq[rows, :] = jnp.concatenate(dqs, axis=1)
    wide = q_ref.shape[1]
    copies = []
    for i, (acc, total) in enumerate(((aq, sq_ref), (ak, sk_ref), (av, sv_ref))):
        g = acc[...]
        if i < 2:
            g = turn(g, c_ref[...], -u_ref[...], -d_ref[...])
        hold[i] = g.astype(BF)
        total[...] = jnp.sum(g, axis=0, keepdims=True)
        at = pl.multiple_of((i * pairs + pl.program_id(0)) * wide, wide)
        copies.append(
            pltpu.make_async_copy(hold.at[i], dproj_ref.at[:, pl.ds(at, wide)], sems.at[i])
        )
        copies[-1].start()
    for copy in copies:
        copy.wait()


def attention_back(q, k, v, cat, d_att, lse, tables, d_proj, n_heads):
    seq = q.shape[0]
    pairs = n_heads // 2
    wide = 2 * HEAD_DIM
    col = pl.BlockSpec((seq, wide), lambda p: (0, p))
    table = pl.BlockSpec((seq, wide), lambda p: (0, 0))
    line = pl.BlockSpec((1, wide), lambda p: (0, p))
    return pl.pallas_call(
        functools.partial(back_kernel, pairs),
        grid=(pairs,),
        in_specs=[col] * 5
        + [pl.BlockSpec((1, 2, seq), lambda p: (p, 0, 0))]
        + [table] * 3
        + [HBM_SPEC],
        out_specs=[HBM_SPEC] + [line] * 3,
        out_shape=[jax.ShapeDtypeStruct(d_proj.shape, BF)]
        + [jax.ShapeDtypeStruct((1, n_heads * HEAD_DIM), F32)] * 3,
        input_output_aliases={9: 0},
        scratch_shapes=[pltpu.VMEM((seq, wide), F32)] * 3
        + [pltpu.VMEM((3, seq, wide), BF), pltpu.SemaphoreType.DMA((3,))],
        **big("attention_back", n_heads * seq * seq * 640, seq * n_heads * 64 * 16),
    )(q, k, v, cat, d_att, lse, *tables, d_proj)


def grads_kernel(n_split, n_late, f_ref, left_ref, right_ref, *refs):
    outs, left_t = refs[n_late:-1], refs[-1]

    @pl.when(pl.program_id(0) == 0)
    def _():
        left_t[...] = left_ref[...].T

    g = dot(left_t[...], right_ref[...], 1, 0).astype(BF)
    if len(outs) == 1:
        outs[0][...] = g
        return
    rows = g.shape[0] // n_split
    for s in range(n_split):
        key = lax.bitwise_xor(f_ref[0], s)
        at = pl.ds(pl.multiple_of(lax.shift_right_logical(key, 1) * rows, 16), rows)
        for i, out in enumerate(outs):

            @pl.when(lax.bitwise_and(key, 1) == 1 - i)
            def _():
                out[at, :] = g[s * rows : (s + 1) * rows]


def grads(left, block, wide, right, first, width, f, n_split=None, late=()):
    rows = left.shape[0]
    tile = math.gcd(512, math.gcd(width, first) if first else width)
    n_out = 2 if n_split else 1
    return pl.pallas_call(
        functools.partial(grads_kernel, n_split, len(late)),
        grid_spec=pltpu.PrefetchScalarGridSpec(
            num_scalar_prefetch=1,
            grid=(width // tile,),
            in_specs=[
                pl.BlockSpec((rows, wide), lambda i, f_ref: (0, block)),
                pl.BlockSpec((rows, tile), lambda i, f_ref: (0, first // tile + i)),
            ]
            + [pl.BlockSpec(memory_space=pl.ANY)] * len(late),
            out_specs=[pl.BlockSpec((wide // n_out, tile), lambda i, f_ref: (0, i))] * n_out,
            scratch_shapes=[pltpu.VMEM((wide, rows), BF)],
        ),
        out_shape=[jax.ShapeDtypeStruct((wide // n_out, width), BF)] * n_out,
        **big("grads", 2 * rows * wide * width, 2 * rows * (wide + width) + 2 * wide * width),
    )(f[None], left, right, *late)


def chunks(rows):
    step = math.gcd(rows, 256)
    return [slice(at, at + step) for at in range(0, rows, step)]


def gelu_parts(u):
    c = math.sqrt(2.0 / math.pi)
    square = u * u
    t = jnp.tanh(c * (u + 0.044715 * u * square))
    value = 0.5 * u * (1.0 + t)
    slope = 0.5 * (1.0 + t) + 0.5 * u * (1.0 - t * t) * (c * (1.0 + 3 * 0.044715 * square))
    return value, slope


def cost(flops, nbytes):
    return pl.CostEstimate(flops=flops, bytes_accessed=nbytes, transcendentals=0)


def big(name_of, flops, nbytes):
    return {
        "compiler_params": pltpu.CompilerParams(vmem_limit_bytes=VMEM_BYTES),
        "cost_estimate": cost(flops // 64, nbytes // 64),
        "name": name_of,
    }


def lay(parts, cuts, at_ref, base, dst):
    for c, (i, start, size) in enumerate(cuts):
        at = pl.multiple_of(at_ref[base + c], 16)
        dst[pl.ds(at, size), :] = parts[i][start : start + size, :]


def qkv_kernel(x_cuts, n_x, w_cuts, n_w, at_ref, *refs):
    xs, ws, b_ref = refs[:n_x], refs[n_x : n_x + n_w], refs[n_x + n_w]
    out_ref, x_ref, w_ref = refs[n_x + n_w + 1 :]

    @pl.when(pl.program_id(0) == 0)
    def _():
        lay(xs, x_cuts, at_ref, 0, x_ref)

    lay(ws, w_cuts, at_ref, len(x_cuts), w_ref)
    out_ref[...] = dot(x_ref[...], w_ref[...], 1, 0) + b_ref[...]


def qkv_project(xs, x_cuts, ws, w_cuts, places, b, rows, width, tile):
    deep, full = xs[0].shape[1], ws[0].shape[1]
    return pl.pallas_call(
        functools.partial(qkv_kernel, x_cuts, len(xs), w_cuts, len(ws)),
        grid_spec=pltpu.PrefetchScalarGridSpec(
            num_scalar_prefetch=1,
            grid=(width // tile,),
            in_specs=[pl.BlockSpec(x.shape, lambda i, at: (0, 0)) for x in xs]
            + [pl.BlockSpec((w.shape[0], tile), lambda i, at: (0, i)) for w in ws]
            + [pl.BlockSpec((1, tile), lambda i, at: (0, i))],
            out_specs=[
                pl.BlockSpec((rows, tile), lambda i, at: (0, i)),
                pl.BlockSpec((rows, deep), lambda i, at: (0, 0)),
                pl.BlockSpec((deep, tile), lambda i, at: (0, i)),
            ],
        ),
        out_shape=[
            jax.ShapeDtypeStruct((rows, width), F32),
            jax.ShapeDtypeStruct((rows, deep), BF),
            jax.ShapeDtypeStruct((deep, full), BF),
        ],
        **big("qkv_project", 2 * rows * deep * width, 2 * deep * (rows + width) + 4 * rows * width),
    )(places, *xs, *ws, b)


def pre_kernel(w_cuts, n_w, at_ref, x_ref, *refs):
    ws, b_ref = refs[:n_w], refs[n_w]
    slope_ref, cat_ref, w_ref = refs[-3:]
    lay(ws, w_cuts, at_ref, 0, w_ref)
    for rows in chunks(x_ref.shape[0]):
        pre = dot(x_ref[rows, :], w_ref[...], 1, 0) + b_ref[...]
        value, slope = gelu_parts(pre)
        slope_ref[rows, :] = slope
        cat_ref[rows, :] = value.astype(BF)


def pre_project(x, ws, w_cuts, places, b, cat, w_all, skip, tile):
    rows, deep = x.shape
    width = w_all.shape[1] - skip
    first, cat_first = skip // tile, (cat.shape[1] - width) // tile
    n_w = len(ws)
    return pl.pallas_call(
        functools.partial(pre_kernel, w_cuts, n_w),
        grid_spec=pltpu.PrefetchScalarGridSpec(
            num_scalar_prefetch=1,
            grid=(width // tile,),
            in_specs=[pl.BlockSpec((rows, deep), lambda i, at: (0, 0))]
            + [pl.BlockSpec((w.shape[0], tile), lambda i, at: (0, first + i)) for w in ws]
            + [pl.BlockSpec((1, tile), lambda i, at: (0, first + i))]
            + [pl.BlockSpec(memory_space=pl.ANY)] * 2,
            out_specs=[
                pl.BlockSpec((rows, tile), lambda i, at: (0, i)),
                pl.BlockSpec((rows, tile), lambda i, at: (0, cat_first + i)),
                pl.BlockSpec((deep, tile), lambda i, at: (0, first + i)),
            ],
        ),
        out_shape=[
            jax.ShapeDtypeStruct((rows, width), F32),
            jax.ShapeDtypeStruct(cat.shape, BF),
            jax.ShapeDtypeStruct(w_all.shape, BF),
        ],
        input_output_aliases={3 + n_w: 1, 4 + n_w: 2},
        **big("pre_project", 2 * rows * deep * width, 2 * deep * (rows + width) + 6 * rows * width),
    )(places, x, *ws, b, cat, w_all)


def by_rank(at_ref, acc, out, blk_size):
    for i in range(acc.shape[0] // blk_size):
        at = pl.multiple_of(at_ref[i], blk_size)
        out[i * blk_size : (i + 1) * blk_size, :] = acc[pl.ds(at, blk_size), :].astype(out.dtype)


def out_kernel(w_cuts, n_w, n_blk, blk_size, at_ref, x_ref, *refs):
    ws, out_ref, w_ref, acc = refs[:n_w], refs[-3], refs[-2], refs[-1]
    lay(ws, w_cuts, at_ref, n_blk, w_ref)
    acc[...] = dot(x_ref[...], w_ref[...], 1, 0)
    by_rank(at_ref, acc, out_ref, blk_size)


def out_project(x, ws, w_cuts, places, n_blk, blk_size):
    rows, deep = x.shape
    width = ws[0].shape[1]
    tile = min(512, width)
    return pl.pallas_call(
        functools.partial(out_kernel, w_cuts, len(ws), n_blk, blk_size),
        grid_spec=pltpu.PrefetchScalarGridSpec(
            num_scalar_prefetch=1,
            grid=(width // tile,),
            in_specs=[pl.BlockSpec((rows, deep), lambda i, at: (0, 0))]
            + [pl.BlockSpec((w.shape[0], tile), lambda i, at: (0, i)) for w in ws],
            out_specs=[
                pl.BlockSpec((rows, tile), lambda i, at: (0, i)),
                pl.BlockSpec((deep, tile), lambda i, at: (0, i)),
            ],
            scratch_shapes=[pltpu.VMEM((rows, tile), F32)],
        ),
        out_shape=[
            jax.ShapeDtypeStruct((rows, width), BF),
            jax.ShapeDtypeStruct((deep, width), BF),
        ],
        **big("out_project", 2 * rows * deep * width, 2 * deep * (rows + width) + 3 * rows * width),
    )(places, x, *ws)


def norm_kernel_back(blk_size, at_ref, x_ref, w_ref, out_ref, acc):
    acc[...] = dot(x_ref[...], w_ref[...], 1, 1)
    by_rank(at_ref, acc, out_ref, blk_size)


def norm_back(x, w, places, blk_size):
    rows, deep = x.shape
    width = w.shape[0]
    tile = min(256, width)
    return pl.pallas_call(
        functools.partial(norm_kernel_back, blk_size),
        grid_spec=pltpu.PrefetchScalarGridSpec(
            num_scalar_prefetch=1,
            grid=(width // tile,),
            in_specs=[
                pl.BlockSpec((rows, deep), lambda i, at: (0, 0)),
                pl.BlockSpec((tile, deep), lambda i, at: (i, 0)),
            ],
            out_specs=pl.BlockSpec((rows, tile), lambda i, at: (0, i)),
            scratch_shapes=[pltpu.VMEM((rows, tile), F32)],
        ),
        out_shape=jax.ShapeDtypeStruct((rows, width), BF),
        **big("norm_back", 2 * rows * deep * width, 2 * deep * (rows + width) + 3 * rows * width),
    )(places, x, w)


def d_cat_kernel(cuts, at_ref, g_ref, w_ref, slope_ref, datt_ref, dproj_ref, sum_ref, x_ref):
    @pl.when(pl.program_id(0) == 0)
    def _():
        lay([g_ref], cuts, at_ref, 0, x_ref)
        datt_ref[...] = dot(x_ref[...], w_ref[...], 1, 1).astype(BF)

    @pl.when(pl.program_id(0) > 0)
    def _():
        total = 0.0
        for rows in chunks(x_ref.shape[0]):
            d_pre = slope_ref[rows, :] * dot(x_ref[rows, :], w_ref[...], 1, 1)
            dproj_ref[rows, :] = d_pre.astype(BF)
            total = total + jnp.sum(d_pre, axis=0, keepdims=True)
        sum_ref[...] = total


def d_cat_parts(g, places, w, slope, wide_a):
    rows, deep = g.shape
    width = slope.shape[1]
    tile = wide_a
    total = 3 * wide_a + width
    blk = rows // places.shape[0]
    cuts = tuple((0, i * blk, blk) for i in range(places.shape[0]))

    def col(i):
        return jnp.maximum(i - 1, 0)

    return pl.pallas_call(
        functools.partial(d_cat_kernel, cuts),
        grid_spec=pltpu.PrefetchScalarGridSpec(
            num_scalar_prefetch=1,
            grid=(1 + width // tile,),
            in_specs=[
                pl.BlockSpec((rows, deep), lambda i, at: (0, 0)),
                pl.BlockSpec((tile, deep), lambda i, at: (i, 0)),
                pl.BlockSpec((rows, tile), lambda i, at: (0, col(i))),
            ],
            out_specs=[
                pl.BlockSpec((rows, tile), lambda i, at: (0, 0)),
                pl.BlockSpec((rows, tile), lambda i, at: (0, 3 + col(i))),
                pl.BlockSpec((1, tile), lambda i, at: (0, col(i))),
                pl.BlockSpec((rows, deep), lambda i, at: (0, 0)),
            ],
        ),
        out_shape=[
            jax.ShapeDtypeStruct((rows, tile), BF),
            jax.ShapeDtypeStruct((rows, total), BF),
            jax.ShapeDtypeStruct((1, width), F32),
            jax.ShapeDtypeStruct((rows, deep), BF),
        ],
        **big("d_cat_parts", 2 * rows * deep * (width + tile), 2 * deep * rows + (2 * deep + 6 * rows) * width),
    )(places, g, w, slope)


def join_kernel(n_parts, sizes, at_ref, *refs):
    dst = refs[-1]
    for j in range(n_parts):
        first = 0
        for i, size in enumerate(sizes):
            at = pl.multiple_of(at_ref[j * len(sizes) + i], 16)
            dst[pl.ds(at, size), :] = refs[j][first : first + size, :].astype(F32)
            first += size


def join_rows(parts, places, sizes):
    rows, width = parts[0].shape
    tile = min(512, width)
    return pl.pallas_call(
        functools.partial(join_kernel, len(parts), sizes),
        grid_spec=pltpu.PrefetchScalarGridSpec(
            num_scalar_prefetch=1,
            grid=(width // tile,),
            in_specs=[pl.BlockSpec((rows, tile), lambda i, at: (0, i))] * len(parts),
            out_specs=pl.BlockSpec((rows * len(parts), tile), lambda i, at: (0, i)),
        ),
        out_shape=jax.ShapeDtypeStruct((rows * len(parts), width), F32),
        **big("join_rows", 0, 6 * rows * len(parts) * width),
    )(places, *parts)


def after(x, *others):
    return lax.optimization_barrier((x, *others))[0]


def pass_on(x, hops):
    n = lax.axis_size("ctx")
    return lax.ppermute(x, "ctx", [(i, (i + hops) % n) for i in range(n)])


def reach(n):
    return n // 2, n - 1 - n // 2


def swap(x, axis, bit):
    n = lax.axis_size(axis)
    return lax.ppermute(x, axis, [(i, i ^ bit) for i in range(n)])


def near(x, bit):
    return swap(x, "fsdp", bit)


def far_keys(n):
    return sorted((k for k in range(2, n, 2)), key=lambda k: (k.bit_count(), k))


def top_bit(k):
    return 1 << (k.bit_length() - 1)


def low_bit(k):
    return k & -k


def halves(x):
    rows = x.shape[0] // 2
    return [x[:rows], x[rows:]]


class Line:
    def __init__(self):
        self.due = []

    def wait(self, *arrays):
        self.due += list(arrays)

    def tied(self, *xs):
        got = list(lax.optimization_barrier((*xs, *self.due)))[: len(xs)]
        self.due = got[:1]
        return got[0] if len(xs) == 1 else got


def ring_job(part, found):
    n = lax.axis_size("ctx")
    ups, downs = reach(n)
    found[0] = up = down = part
    for hop in range(1, ups + 1):
        if hop <= downs:
            up, down = yield [pass_on(up, 1), pass_on(down, -1)]
            found[n - hop] = down
        else:
            (up,) = yield [pass_on(up, 1)]
        found[hop] = up


def total_job(x, found):
    for axis in ("fsdp", "ctx"):
        bit = 1
        while bit < lax.axis_size(axis):
            (got,) = yield [swap(x, axis, bit)]
            x = x + got
            bit *= 2
    found.append(x)


def gather_job(shard, found):
    n = lax.axis_size("fsdp")
    have = {}
    keys = far_keys(n)
    fresh = [(0, None, shard)]
    found.extend(fresh)
    level = 0
    while True:
        level += 1
        send = []
        for k in keys:
            if k.bit_count() != level:
                continue
            if level == 1:
                send.append((k, None, near(shard, k)))
            else:
                for h, bit in ((0, top_bit(k)), (1, low_bit(k))):
                    send.append((k, h, near(have[k ^ bit, h], bit)))
        send += [(k | 1, h, near(x, 1)) for k, h, x in fresh if not k & 1]
        if not send:
            return
        got = yield [x for _, _, x in send]
        fresh = [(k, h, x) for (k, h, _), x in zip(send, got)]
        found.extend(fresh)
        for k, h, x in fresh:
            if not k & 1:
                if h is None:
                    have[k, 0], have[k, 1] = halves(x)
                else:
                    have[k, h] = x


def gather_order(n):
    got = [(0, None)]
    fresh = list(got)
    level = 0
    while True:
        level += 1
        new = []
        for k in far_keys(n):
            if k.bit_count() == level:
                new += [(k, None)] if level == 1 else [(k, 0), (k, 1)]
        new += [(k | 1, h) for k, h in fresh if not k & 1]
        if not new:
            return got
        got += new
        fresh = new


def scatter_job(away, home, found):
    n = lax.axis_size("fsdp")
    (got,) = yield [near(away, 1)]
    home = home() if callable(home) else home
    rows = home.shape[0] // (n // 2)
    hold = {}
    for i, k in enumerate(range(0, n, 2)):
        for h in range(2):
            at = i * rows + h * (rows // 2)
            cut = slice(at, at + rows // 2)
            hold[k, h] = home[cut].astype(F32) + got[cut].astype(F32)
    for level in range(n.bit_length() - 2, 0, -1):
        moves = []
        for k in far_keys(n):
            if k.bit_count() != level:
                continue
            if level > 1:
                for h, bit in ((0, top_bit(k)), (1, low_bit(k))):
                    moves.append((k ^ bit, h, near(hold[k, h].astype(BF), bit)))
            else:
                whole = jnp.concatenate([hold[k, 0], hold[k, 1]], axis=0).astype(BF)
                moves.append((0, None, near(whole, k)))
        got = yield [x for _, _, x in moves]
        for (k, h, _), x in zip(moves, got):
            if h is None:
                for i, part in enumerate(halves(x)):
                    hold[k, i] = hold[k, i] + part.astype(F32)
            else:
                hold[k, h] = hold[k, h] + x.astype(F32)
    found.append(jnp.concatenate([hold[0, 0], hold[0, 1]], axis=0).astype(BF))


class Move:
    def __init__(self, line, job):
        self.line, self.job, self.flight = line, job, next(job)

    def step(self, *more):
        moves = [m for m in (self, *more) if m.flight is not None]
        flights = [x for m in moves for x in m.flight]
        if not moves:
            return
        got = list(lax.optimization_barrier((*flights, *self.line.due)))[: len(flights)]
        self.line.due = list(got)
        for m in moves:
            own, got = got[: len(m.flight)], got[len(m.flight) :]
            try:
                m.flight = m.job.send(own)
            except StopIteration:
                m.flight = None

    def end(self, *more):
        while self.flight is not None:
            self.step(*more)


def gelu_tanh(values):
    return jax.nn.gelu(values, approximate=True)


def rotary_tables(positions):
    seq = positions.shape[0]
    half_rot = ROT_DIM // 2
    expon = jnp.arange(half_rot, dtype=F32) * (2.0 / ROT_DIM)
    freqs = ROPE_BASE ** (-expon)
    angles = positions.astype(F32)[:, None] * freqs[None, :]
    cosine, sine = jnp.cos(angles), jnp.sin(angles)
    zero = jnp.zeros_like(sine)
    rest = jnp.zeros((seq, HEAD_DIM - ROT_DIM), F32)
    c = jnp.concatenate([cosine, cosine, rest + 1.0], axis=1)
    up = jnp.concatenate([zero, sine, rest], axis=1)
    down = jnp.concatenate([-sine, zero, rest], axis=1)
    return tuple(jnp.concatenate([t, t], axis=1) for t in (c, up, down))


def shards(inputs, out_grad, block_order, ln_gain, ln_beta, w_in, b_in, w_out, b_out):
    n_ctx, n_fsdp = lax.axis_size("ctx"), lax.axis_size("fsdp")
    z, f = lax.axis_index("ctx"), lax.axis_index("fsdp")
    seq_in, seq_grad, blk_order = inputs[0], out_grad[0], block_order[0]
    tok_rows = seq_in.shape[0]
    seq_len = tok_rows * n_ctx
    n_blk = blk_order.shape[0]
    blk_size = seq_len // n_blk
    per = n_blk // n_ctx
    wide_d = D // n_fsdp
    shard = w_out.shape[0]
    cat_rows = shard * n_fsdp
    in_cols = w_in.shape[1]
    n_heads = HEADS // n_ctx
    wide_a, wide_m = D // n_ctx, (cat_rows - D) // n_ctx
    even, att_runs, act_runs = plan(n_fsdp, n_ctx, cat_rows)
    z_runs = [in_runs(att_runs[i], act_runs[i]) for i in range(n_ctx)]

    def position_of(k):
        return lax.shift_right_logical(k, 1) + lax.bitwise_and(k, 1) * (n_fsdp // 2)

    rank_places = blk_order * blk_size
    ranks = lax.rem(z - jnp.arange(n_ctx, dtype=jnp.int32) + n_ctx, n_ctx)
    picks = (ranks[:, None] == jnp.arange(n_ctx, dtype=jnp.int32)[None, :]).astype(jnp.int32)
    row_places = jnp.sum(
        picks[:, :, None] * rank_places.reshape(1, n_ctx, per), axis=1, dtype=jnp.int32
    ).reshape(-1)

    line = Line()
    keys_at = {k: p for p, k in enumerate(key_order(n_fsdp))}
    share = shard // n_ctx
    mixed_f = [i for i in range(n_fsdp) if 0 < D - shard * i < shard]
    cut = (D - shard * mixed_f[0]) // n_ctx if mixed_f else share
    cut_m = share - cut
    is_mixed = (f == mixed_f[0]) if mixed_f else False

    def own_rows(whole):
        first = lax.dynamic_slice_in_dim(whole, z * share, share, 0)
        if not cut_m:
            return first
        both = jnp.concatenate(
            [
                lax.dynamic_slice_in_dim(whole, z * cut, cut, 0),
                lax.dynamic_slice_in_dim(whole, cut * n_ctx + z * cut_m, cut_m, 0),
            ],
            axis=0,
        )
        return jnp.where(is_mixed, both, first)

    def cuts_of(found):
        return [x for _, _, x in found], tuple((i, 0, x.shape[0]) for i, (_, _, x) in enumerate(found))

    order = gather_order(n_fsdp)
    w_at = jnp.asarray(
        [keys_at[k] * wide_d + (h or 0) * (wide_d // 2) for k, h in order], jnp.int32
    )
    o_keys = jnp.asarray([k for k, _ in order], jnp.int32)
    o_at = lax.bitwise_xor(f, o_keys) * share + jnp.asarray(
        [(h or 0) * (share // 2) for _, h in order], jnp.int32
    )
    qkv_at = jnp.concatenate([row_places, w_at])
    o_at = jnp.concatenate([rank_places, o_at if even else jnp.zeros((1,), jnp.int32)])

    normed_parts, w_in_parts, w_out_parts = {}, [], []
    w_in_own = pick_columns(w_in, z, z_runs)
    w_in_move = Move(line, gather_job(w_in_own, w_in_parts))
    line.wait(w_in_own)
    normed_own, dy_own = norm(line.tied(seq_in), seq_grad, ln_gain, ln_beta, f, n_fsdp)
    normed_ring = Move(line, ring_job(normed_own, normed_parts))
    line.wait(normed_own)
    tables = rotary_tables(line.tied(jnp.arange(seq_len, dtype=jnp.int32)))
    line.wait(*tables)
    b_in_z = jnp.stack([jnp.concatenate([b_in[s : s + n] for s, n in runs]) for runs in z_runs])[z]
    b_in_z = b_in_z[None]
    w_out_own = own_rows(line.tied(w_out)) if even else w_out
    line.wait(w_out_own, b_in_z, qkv_at, o_at, w_at, rank_places, row_places)

    while normed_ring.flight is not None:
        normed_ring.step(w_in_move)
    dy_all = lax.all_gather(after(dy_own, *line.due), "ctx", axis=0, tiled=True)
    if even:
        w_out_move = Move(line, gather_job(line.tied(w_out_own), w_out_parts))
    w_in_move.end()

    wide_q = 3 * wide_a
    x_cuts = [(j, i * blk_size, blk_size) for j in range(n_ctx) for i in range(per)]
    w_arrays, w_cuts = cuts_of(w_in_parts)
    xs = [normed_parts[j] for j in range(n_ctx)]
    qkv, normed, w_in_all = qkv_project(
        [line.tied(xs[0])] + xs[1:], tuple(x_cuts), w_arrays, w_cuts, qkv_at,
        b_in_z, seq_len, wide_q, wide_a,
    )
    line.wait(qkv)
    q_b, k_b, v_b, cat_b, lse = attention(line.tied(qkv), tables, n_heads, cat_rows // n_ctx)
    line.wait(cat_b)
    if even:
        w_out_move.step()
    slope, cat_b, w_in_all = pre_project(
        line.tied(normed), w_arrays, w_cuts, w_at, b_in_z, cat_b, w_in_all, wide_q, wide_a
    )
    line.wait(cat_b)
    if even:
        w_out_move.end()
        o_arrays, o_cuts = cuts_of(w_out_parts)
    else:
        w_all = lax.all_gather(w_out, "fsdp", axis=0, tiled=True)
        w_all = jnp.concatenate(
            [
                lax.dynamic_slice_in_dim(w_all, z * wide_a, wide_a, 0),
                lax.dynamic_slice_in_dim(w_all, D + z * wide_m, wide_m, 0),
            ],
            axis=0,
        )
        o_arrays, o_cuts = [w_all], ((0, 0, cat_rows // n_ctx),)
    out_part, w_out_z = out_project(line.tied(cat_b), o_arrays, o_cuts, o_at, n_blk, blk_size)
    line.wait(out_part)

    def ctx_sum(x):
        return lax.psum_scatter(x, "ctx", scatter_dimension=0, tiled=True)

    out_sum = ctx_sum(out_part)

    line.wait(dy_all)
    d_att, d_proj, sum_pre, dy = d_cat_parts(
        line.tied(dy_all), rank_places, w_out_z, slope, wide_a
    )
    line.wait(d_att)
    d_proj, *sum_qkv = attention_back(
        q_b, k_b, v_b, cat_b, line.tied(d_att), lse, tables, d_proj, n_heads
    )
    line.wait(d_proj)
    norm_part = norm_back(line.tied(d_proj), w_in_all, rank_places, blk_size)
    line.wait(norm_part)
    norm_sum = ctx_sum(norm_part)

    half = D // 2
    out_own, pre_own, qkv_own = [], [], []
    out_parts, pre_parts, qkv_parts = {}, {}, {}
    away, home = grads(line.tied(cat_b), 0, cat_rows // n_ctx, dy, 0, D, f, n_fsdp)
    line.wait(away)
    out_scatter = Move(line, scatter_job(line.tied(away), home, out_own)) if even else None
    (pre_away,) = grads(line.tied(normed), 1, half, d_proj, wide_q, wide_m, f)
    line.wait(pre_away)
    if even:
        out_scatter.step()
    (pre_home,) = grads(line.tied(normed), 0, half, d_proj, wide_q, wide_m, f, late=(out_sum,))
    line.wait(pre_home)
    (qkv_away,) = grads(line.tied(normed), 1, half, d_proj, 0, wide_q, f)
    line.wait(qkv_away)
    if even:
        out_scatter.step()
    pre_scatter = Move(line, scatter_job(line.tied(pre_away), pre_home, pre_own))
    (qkv_home,) = grads(line.tied(normed), 0, half, d_proj, 0, wide_q, f)
    line.wait(qkv_home)
    if even:
        out_scatter.step(pre_scatter)
        out_ring = Move(line, ring_job(line.tied(out_own[0]), out_parts))
    else:
        pre_scatter.step()
    qkv_scatter = Move(line, scatter_job(line.tied(qkv_away), qkv_home, qkv_own))
    pre_scatter.step()

    norm_sum = line.tied(norm_sum)

    seq_in_t = line.tied(seq_in)
    centred = seq_in_t - jnp.mean(seq_in_t, axis=1, keepdims=True)
    inv_std = lax.rsqrt(jnp.mean(centred * centred, axis=1, keepdims=True) + LN_EPS)
    x_hat = centred * inv_std
    d_norm = jnp.concatenate(
        [
            lax.dynamic_slice_in_dim(norm_sum.astype(F32), position_of(f ^ i) * wide_d, wide_d, 1)
            for i in range(n_fsdp)
        ],
        axis=1,
    )
    small = jnp.stack(
        [jnp.sum(seq_grad, axis=0), jnp.sum(d_norm * x_hat, axis=0), jnp.sum(d_norm, axis=0)]
    )
    gain_grad = d_norm * ln_gain
    d_input = seq_grad + inv_std * (
        gain_grad
        - jnp.mean(gain_grad, axis=1, keepdims=True)
        - x_hat * jnp.mean(gain_grad * x_hat, axis=1, keepdims=True)
    )
    out_y = seq_in + out_sum.astype(F32) + b_out

    g_b_in_z = jnp.concatenate([x[0] for x in (*sum_qkv, sum_pre)])
    masked = jnp.where(
        jnp.arange(n_ctx)[:, None] == z, g_b_in_z[None, :], jnp.zeros((), F32)
    )
    runs = sorted((s, n, i, at) for i in range(n_ctx) for s, n, at in run_offsets(z_runs[i]))
    vector = jnp.concatenate([small.reshape(-1)] + [masked[i, at : at + n] for _, n, i, at in runs])
    line.wait(d_input)

    pre_runs = [[(s - 3 * D, n) for s, n in runs if s >= 3 * D] for runs in z_runs]
    qkv_runs = [[(s, n) for s, n in runs if s < 3 * D] for runs in z_runs]
    if even:
        out_ring.step(pre_scatter, qkv_scatter)
    else:
        pre_scatter.step(qkv_scatter)
    pre_scatter.end()
    pre_ring = Move(line, ring_job(line.tied(pre_own[0]), pre_parts))
    vectors = []
    if even:
        out_ring.end(qkv_scatter)
    vector_move = Move(line, total_job(line.tied(vector), vectors))
    if even:
        at = []
        for j in range(n_ctx):
            rank = lax.rem(z - j + n_ctx, n_ctx)
            at.append(jnp.where(is_mixed, rank * cut, rank * share))
            if cut_m:
                at.append(jnp.where(is_mixed, cut * n_ctx + rank * cut_m, rank * share + cut))
        g_w_out = join_rows(
            [line.tied(out_parts[0])] + [out_parts[j] for j in range(1, n_ctx)],
            jnp.stack(at).astype(jnp.int32),
            (cut, cut_m) if cut_m else (cut,),
        )
        line.wait(g_w_out)
    else:
        blocks = jnp.concatenate([home, away], axis=0).reshape(n_fsdp, -1, D)
        g_out = jnp.concatenate(
            [lax.dynamic_index_in_dim(blocks, position_of(f ^ i), 0, False) for i in range(n_fsdp)]
        )
        spread = jnp.zeros((cat_rows, D), BF)
        spread = lax.dynamic_update_slice_in_dim(spread, g_out[:wide_a], z * wide_a, 0)
        spread = lax.dynamic_update_slice_in_dim(spread, g_out[wide_a:], D + z * wide_m, 0)
        g_w_out = lax.psum_scatter(spread.astype(F32), "fsdp", scatter_dimension=0, tiled=True)
        g_w_out = lax.psum(g_w_out, "ctx")
    pre_ring.step(qkv_scatter, vector_move)
    qkv_scatter.end()
    qkv_ring = Move(line, ring_job(line.tied(qkv_own[0]), qkv_parts))
    pre_ring.end(vector_move)
    vector_move.step()
    in_turn = range(n_ctx)
    g_w_in = spread_columns(
        None,
        [line.tied(pre_parts[0])] + [pre_parts[j] for j in in_turn[1:]],
        z, pre_runs, in_cols, 3 * D, in_cols - 3 * D,
    )
    line.wait(g_w_in)
    qkv_ring.step(vector_move)
    qkv_ring.end(vector_move)
    vector_move.end()
    g_w_in = spread_columns(
        g_w_in, [qkv_parts[j] for j in in_turn], z, qkv_runs, in_cols, 0, 3 * D
    )
    vector = vectors[0]
    small = vector[: 3 * D].reshape(3, D)
    g_b_in = vector[3 * D :]

    def own_part(vector):
        length_part = vector.shape[0] // n_fsdp
        return lax.dynamic_slice_in_dim(vector, f * length_part, length_part, 0)

    return (
        out_y[None],
        d_input[None],
        g_w_in,
        own_part(g_b_in),
        g_w_out,
        own_part(small[0]),
        own_part(small[1]),
        own_part(small[2]),
    )


def run_offsets(runs):
    at, found = 0, []
    for start, size in runs:
        found.append((start, size, at))
        at += size
    return found


def solution(mesh):
    placed = (
        P("fsdp", "ctx", None),
        P("fsdp", "ctx", None),
        P("fsdp", None),
        P(),
        P(),
        P("fsdp", None),
        P(),
        P("fsdp", None),
        P(),
    )
    return jax.shard_map(
        shards,
        mesh=mesh,
        in_specs=placed,
        out_specs=(
            P("fsdp", "ctx", None),
            P("fsdp", "ctx", None),
            P("fsdp", None),
            P("fsdp"),
            P("fsdp", None),
            P("fsdp"),
            P("fsdp"),
            P("fsdp"),
        ),
        check_vma=False,
    )
```

```python
import functools
import math

import jax
import jax.numpy as jnp
from jax import lax
from jax.experimental import pallas as pl
from jax.experimental.pallas import tpu as pltpu
from jax.sharding import PartitionSpec as P

D = 2048
HEADS = 32
HEAD_DIM = 64
ROT_DIM = 32

LN_EPS = 1e-05
NEG_BIG = -1e30
ROPE_BASE = 10000.0
BF = jnp.bfloat16
F32 = jnp.float32
VMEM_BYTES = 56 * 1024 * 1024
HBM_SPEC = pl.BlockSpec(memory_space=pltpu.HBM)


def plan(n_fsdp, n_ctx, cat_rows):
    shard = cat_rows // n_fsdp
    even = True
    att, act = [[] for _ in range(n_ctx)], [[] for _ in range(n_ctx)]
    for f in range(n_fsdp):
        a = min(max(D - shard * f, 0), shard)
        m = shard - a
        if a % (n_ctx * HEAD_DIM) or m % (n_ctx * 16):
            even = False
        for z in range(n_ctx):
            if a:
                att[z].append((shard * f + z * (a // n_ctx), a // n_ctx))
            if m:
                act[z].append((shard * f + a + z * (m // n_ctx), m // n_ctx))
    if not even:
        wide_a, wide_m = D // n_ctx, (cat_rows - D) // n_ctx
        att = [[(z * wide_a, wide_a)] for z in range(n_ctx)]
        act = [[(D + z * wide_m, wide_m)] for z in range(n_ctx)]
    return even, att, act


def in_runs(att, act):
    runs = [(part * D + s, n) for part in range(3) for s, n in att]
    return runs + [(2 * D + s, n) for s, n in act]


def key_order(n):
    return list(range(0, n, 2)) + list(range(1, n, 2))


def pick_kernel(all_runs, z_ref, src_ref, dst_ref):
    for z, runs in enumerate(all_runs):

        @pl.when(z_ref[0] == z)
        def _():
            at = 0
            for start, size in runs:
                dst_ref[:, at : at + size] = src_ref[:, start : start + size]
                at += size


def pick_columns(src, z, all_runs):
    rows, cols = src.shape
    width = sum(n for _, n in all_runs[0])
    step = min(rows, 128)
    return pl.pallas_call(
        functools.partial(pick_kernel, all_runs),
        grid_spec=pltpu.PrefetchScalarGridSpec(
            num_scalar_prefetch=1,
            grid=(rows // step,),
            in_specs=[pl.BlockSpec((step, cols), lambda i, z_ref: (i, 0))],
            out_specs=pl.BlockSpec((step, width), lambda i, z_ref: (i, 0)),
        ),
        out_shape=jax.ShapeDtypeStruct((rows, width), src.dtype),
        **big("pick_columns", 0, 2 * rows * (cols + width)),
    )(z[None], src)


def spread_kernel(all_runs, n_ctx, z_ref, *refs):
    srcs, dst_ref = refs[:n_ctx], refs[-1]
    for z in range(n_ctx):

        @pl.when(z_ref[0] == z)
        def _():
            for j, src_ref in enumerate(srcs):
                at = 0
                for start, size in all_runs[(z - j) % n_ctx]:
                    dst_ref[:, start : start + size] = src_ref[:, at : at + size].astype(F32)
                    at += size


def spread_columns(whole, parts, z, all_runs, cols, first, width_out):
    rows, width = parts[0].shape
    n_ctx = len(parts)
    step = min(rows, 128)
    fresh = whole is None
    return pl.pallas_call(
        functools.partial(spread_kernel, all_runs, n_ctx),
        grid_spec=pltpu.PrefetchScalarGridSpec(
            num_scalar_prefetch=1,
            grid=(rows // step,),
            in_specs=[pl.BlockSpec((step, width), lambda i, z_ref: (i, 0))] * n_ctx
            + [pl.BlockSpec(memory_space=pl.ANY)] * (not fresh),
            out_specs=pl.BlockSpec(
                (pl.Element(step), pl.Element(width_out)), lambda i, z_ref: (i * step, first)
            ),
        ),
        out_shape=jax.ShapeDtypeStruct((rows, cols), F32),
        input_output_aliases={} if fresh else {1 + n_ctx: 0},
        **big("spread_columns", 0, rows * width_out * 6),
    )(z[None], *parts, *([] if fresh else [whole]))


def norm_kernel(n_fsdp, f_ref, x_ref, g_ref, gain_ref, beta_ref, out_ref, dy_ref, hold):
    x = x_ref[...]
    centred = x - jnp.mean(x, axis=1, keepdims=True)
    inv_std = lax.rsqrt(jnp.mean(centred * centred, axis=1, keepdims=True) + LN_EPS)
    hold[...] = (centred * inv_std * gain_ref[...] + beta_ref[...]).astype(BF)
    wide = x.shape[1] // n_fsdp
    for p, k in enumerate(key_order(n_fsdp)):
        at = pl.multiple_of((f_ref[0] ^ k) * wide, wide)
        out_ref[:, p * wide : (p + 1) * wide] = hold[:, pl.ds(at, wide)]
    dy_ref[...] = g_ref[...].astype(BF)


def norm(x, g, gain, beta, f, n_fsdp):
    rows, cols = x.shape
    step = min(rows, 128)
    tile = pl.BlockSpec((step, cols), lambda i, f_ref: (i, 0))
    line = pl.BlockSpec((1, cols), lambda i, f_ref: (0, 0))
    own = jax.ShapeDtypeStruct((rows, cols), BF)
    return pl.pallas_call(
        functools.partial(norm_kernel, n_fsdp),
        grid_spec=pltpu.PrefetchScalarGridSpec(
            num_scalar_prefetch=1,
            grid=(rows // step,),
            in_specs=[tile, tile, line, line],
            out_specs=[tile, tile],
            scratch_shapes=[pltpu.VMEM((step, cols), BF)],
        ),
        out_shape=[own, own],
        **big("norm", 0, 12 * rows * cols),
    )(f[None], x, g, gain[None], beta[None])


def turn(u, c, s_up, s_down):
    half_rot = ROT_DIM // 2
    wide = u.shape[1]
    return (
        u * c
        + pltpu.roll(u, half_rot, 1) * s_up
        + pltpu.roll(u, wide - half_rot, 1) * s_down
    )


def dot(a, b, ca, cb):
    return lax.dot_general(a, b, (((ca,), (cb,)), ((), ())), preferred_element_type=F32)


def causal(size, keys, first):
    key_at = lax.broadcasted_iota(jnp.int32, (keys, size), 0)
    query_at = lax.broadcasted_iota(jnp.int32, (keys, size), 1) + first
    return key_at <= query_at


def att_kernel(q_ref, k_ref, v_ref, c_ref, u_ref, d_ref, qb_ref, kb_ref, vb_ref, att_ref, lse_ref):
    seq = q_ref.shape[0]
    size = math.gcd(seq, 256)
    c, su, sd = c_ref[...], u_ref[...], d_ref[...]
    qb_ref[...] = turn(q_ref[...], c, su, sd).astype(BF)
    kb_ref[...] = turn(k_ref[...], c, su, sd).astype(BF)
    vb_ref[...] = v_ref[...].astype(BF)
    scale = 1.0 / math.sqrt(HEAD_DIM)
    for i in range(seq // size):
        rows = slice(i * size, (i + 1) * size)
        keys = (i + 1) * size
        outs = []
        for h in range(2):
            lanes = slice(h * HEAD_DIM, (h + 1) * HEAD_DIM)
            s = dot(kb_ref[:keys, lanes], qb_ref[rows, lanes], 1, 1) * scale
            s = jnp.where(causal(size, keys, i * size), s, NEG_BIG)
            top = jnp.max(s, axis=0, keepdims=True)
            e = jnp.exp(s - top)
            total = jnp.sum(e, axis=0, keepdims=True)
            lse_ref[0, h : h + 1, rows] = top + jnp.log(total)
            p = (e * (1.0 / total)).astype(BF)
            outs.append(dot(p, vb_ref[:keys, lanes], 0, 0))
        att_ref[rows, :] = jnp.concatenate(outs, axis=1).astype(BF)


def attention(project, tables, n_heads, cat_width):
    seq = project.shape[0]
    pairs = n_heads // 2
    wide = 2 * HEAD_DIM

    def col(base):
        return pl.BlockSpec((seq, wide), lambda p: (0, base + p))

    table = pl.BlockSpec((seq, wide), lambda p: (0, 0))
    own = jax.ShapeDtypeStruct((seq, n_heads * HEAD_DIM), BF)
    return pl.pallas_call(
        att_kernel,
        grid=(pairs,),
        in_specs=[col(0), col(pairs), col(2 * pairs), table, table, table],
        out_specs=[col(0)] * 4 + [pl.BlockSpec((1, 2, seq), lambda p: (p, 0, 0))],
        out_shape=[own] * 3
        + [
            jax.ShapeDtypeStruct((seq, cat_width), BF),
            jax.ShapeDtypeStruct((pairs, 2, seq), F32),
        ],
        **big("attention", n_heads * seq * seq * 256, seq * n_heads * 64 * 20),
    )(project, project, project, *tables)


def back_kernel(
    pairs, q_ref, k_ref, v_ref, att_ref, datt_ref, lse_ref, c_ref, u_ref, d_ref, dproj_in,
    dproj_ref, sq_ref, sk_ref, sv_ref, aq, ak, av, hold, sems,
):
    del dproj_in
    seq = q_ref.shape[0]
    size = math.gcd(seq, 256)
    scale = 1.0 / math.sqrt(HEAD_DIM)
    ak[...] = jnp.zeros_like(ak)
    av[...] = jnp.zeros_like(av)
    for i in range(seq // size):
        rows = slice(i * size, (i + 1) * size)
        keys = (i + 1) * size
        dqs, dks, dvs = [], [], []
        prod = datt_ref[rows, :].astype(F32) * att_ref[rows, :].astype(F32)
        prod_t = prod.T
        for h in range(2):
            lanes = slice(h * HEAD_DIM, (h + 1) * HEAD_DIM)
            q, do = q_ref[rows, lanes], datt_ref[rows, lanes]
            k, v = k_ref[:keys, lanes], v_ref[:keys, lanes]
            delta = jnp.sum(prod_t[lanes, :], axis=0, keepdims=True)
            s = dot(k, q, 1, 1) * scale
            s = jnp.where(causal(size, keys, i * size), s, NEG_BIG)
            p = jnp.exp(s - lse_ref[0, h : h + 1, rows])
            dp = dot(v, do, 1, 1)
            ds = (p * (dp - delta) * scale).astype(BF)
            dvs.append(dot(p.astype(BF), do, 1, 0))
            dks.append(dot(ds, q, 1, 0))
            dqs.append(dot(ds, k, 0, 0))
        av[:keys, :] += jnp.concatenate(dvs, axis=1)
        ak[:keys, :] += jnp.concatenate(dks, axis=1)
        aq[rows, :] = jnp.concatenate(dqs, axis=1)
    wide = q_ref.shape[1]
    copies = []
    for i, (acc, total) in enumerate(((aq, sq_ref), (ak, sk_ref), (av, sv_ref))):
        g = acc[...]
        if i < 2:
            g = turn(g, c_ref[...], -u_ref[...], -d_ref[...])
        hold[i] = g.astype(BF)
        total[...] = jnp.sum(g, axis=0, keepdims=True)
        at = pl.multiple_of((i * pairs + pl.program_id(0)) * wide, wide)
        copies.append(
            pltpu.make_async_copy(hold.at[i], dproj_ref.at[:, pl.ds(at, wide)], sems.at[i])
        )
        copies[-1].start()
    for copy in copies:
        copy.wait()


def attention_back(q, k, v, cat, d_att, lse, tables, d_proj, n_heads):
    seq = q.shape[0]
    pairs = n_heads // 2
    wide = 2 * HEAD_DIM
    col = pl.BlockSpec((seq, wide), lambda p: (0, p))
    table = pl.BlockSpec((seq, wide), lambda p: (0, 0))
    line = pl.BlockSpec((1, wide), lambda p: (0, p))
    return pl.pallas_call(
        functools.partial(back_kernel, pairs),
        grid=(pairs,),
        in_specs=[col] * 5
        + [pl.BlockSpec((1, 2, seq), lambda p: (p, 0, 0))]
        + [table] * 3
        + [HBM_SPEC],
        out_specs=[HBM_SPEC] + [line] * 3,
        out_shape=[jax.ShapeDtypeStruct(d_proj.shape, BF)]
        + [jax.ShapeDtypeStruct((1, n_heads * HEAD_DIM), F32)] * 3,
        input_output_aliases={9: 0},
        scratch_shapes=[pltpu.VMEM((seq, wide), F32)] * 3
        + [pltpu.VMEM((3, seq, wide), BF), pltpu.SemaphoreType.DMA((3,))],
        **big("attention_back", n_heads * seq * seq * 640, seq * n_heads * 64 * 16),
    )(q, k, v, cat, d_att, lse, *tables, d_proj)


def grads_kernel(n_split, n_late, f_ref, left_ref, right_ref, *refs):
    outs, left_t = refs[n_late:-1], refs[-1]

    @pl.when(pl.program_id(0) == 0)
    def _():
        left_t[...] = left_ref[...].T

    g = dot(left_t[...], right_ref[...], 1, 0).astype(BF)
    if len(outs) == 1:
        outs[0][...] = g
        return
    rows = g.shape[0] // n_split
    for s in range(n_split):
        key = lax.bitwise_xor(f_ref[0], s)
        at = pl.ds(pl.multiple_of(lax.shift_right_logical(key, 1) * rows, 16), rows)
        for i, out in enumerate(outs):

            @pl.when(lax.bitwise_and(key, 1) == 1 - i)
            def _():
                out[at, :] = g[s * rows : (s + 1) * rows]


def grads(left, block, wide, right, first, width, f, n_split=None, late=()):
    rows = left.shape[0]
    tile = math.gcd(512, math.gcd(width, first) if first else width)
    n_out = 2 if n_split else 1
    return pl.pallas_call(
        functools.partial(grads_kernel, n_split, len(late)),
        grid_spec=pltpu.PrefetchScalarGridSpec(
            num_scalar_prefetch=1,
            grid=(width // tile,),
            in_specs=[
                pl.BlockSpec((rows, wide), lambda i, f_ref: (0, block)),
                pl.BlockSpec((rows, tile), lambda i, f_ref: (0, first // tile + i)),
            ]
            + [pl.BlockSpec(memory_space=pl.ANY)] * len(late),
            out_specs=[pl.BlockSpec((wide // n_out, tile), lambda i, f_ref: (0, i))] * n_out,
            scratch_shapes=[pltpu.VMEM((wide, rows), BF)],
        ),
        out_shape=[jax.ShapeDtypeStruct((wide // n_out, width), BF)] * n_out,
        **big("grads", 2 * rows * wide * width, 2 * rows * (wide + width) + 2 * wide * width),
    )(f[None], left, right, *late)


def chunks(rows):
    step = math.gcd(rows, 256)
    return [slice(at, at + step) for at in range(0, rows, step)]


def gelu_parts(u):
    c = math.sqrt(2.0 / math.pi)
    square = u * u
    t = jnp.tanh(c * (u + 0.044715 * u * square))
    value = 0.5 * u * (1.0 + t)
    slope = 0.5 * (1.0 + t) + 0.5 * u * (1.0 - t * t) * (c * (1.0 + 3 * 0.044715 * square))
    return value, slope


def cost(flops, nbytes):
    return pl.CostEstimate(flops=flops, bytes_accessed=nbytes, transcendentals=0)


def big(name_of, flops, nbytes):
    return {
        "compiler_params": pltpu.CompilerParams(vmem_limit_bytes=VMEM_BYTES),
        "cost_estimate": cost(flops // 64, nbytes // 64),
        "name": name_of,
    }


def lay(parts, cuts, at_ref, base, dst):
    for c, (i, start, size) in enumerate(cuts):
        at = pl.multiple_of(at_ref[base + c], 16)
        dst[pl.ds(at, size), :] = parts[i][start : start + size, :]


def qkv_kernel(x_cuts, n_x, w_cuts, n_w, at_ref, *refs):
    xs, ws, b_ref = refs[:n_x], refs[n_x : n_x + n_w], refs[n_x + n_w]
    out_ref, x_ref, w_ref = refs[n_x + n_w + 1 :]

    @pl.when(pl.program_id(0) == 0)
    def _():
        lay(xs, x_cuts, at_ref, 0, x_ref)

    lay(ws, w_cuts, at_ref, len(x_cuts), w_ref)
    out_ref[...] = dot(x_ref[...], w_ref[...], 1, 0) + b_ref[...]


def qkv_project(xs, x_cuts, ws, w_cuts, places, b, rows, width, tile):
    deep, full = xs[0].shape[1], ws[0].shape[1]
    return pl.pallas_call(
        functools.partial(qkv_kernel, x_cuts, len(xs), w_cuts, len(ws)),
        grid_spec=pltpu.PrefetchScalarGridSpec(
            num_scalar_prefetch=1,
            grid=(width // tile,),
            in_specs=[pl.BlockSpec(x.shape, lambda i, at: (0, 0)) for x in xs]
            + [pl.BlockSpec((w.shape[0], tile), lambda i, at: (0, i)) for w in ws]
            + [pl.BlockSpec((1, tile), lambda i, at: (0, i))],
            out_specs=[
                pl.BlockSpec((rows, tile), lambda i, at: (0, i)),
                pl.BlockSpec((rows, deep), lambda i, at: (0, 0)),
                pl.BlockSpec((deep, tile), lambda i, at: (0, i)),
            ],
        ),
        out_shape=[
            jax.ShapeDtypeStruct((rows, width), F32),
            jax.ShapeDtypeStruct((rows, deep), BF),
            jax.ShapeDtypeStruct((deep, full), BF),
        ],
        **big("qkv_project", 2 * rows * deep * width, 2 * deep * (rows + width) + 4 * rows * width),
    )(places, *xs, *ws, b)


def pre_kernel(w_cuts, n_w, at_ref, x_ref, *refs):
    ws, b_ref = refs[:n_w], refs[n_w]
    pre_ref, cat_ref, w_ref = refs[-3:]
    lay(ws, w_cuts, at_ref, 0, w_ref)
    for rows in chunks(x_ref.shape[0]):
        pre = dot(x_ref[rows, :], w_ref[...], 1, 0) + b_ref[...]
        pre_ref[rows, :] = pre
        cat_ref[rows, :] = gelu_parts(pre)[0].astype(BF)


def pre_project(x, ws, w_cuts, places, b, cat, w_all, skip, tile):
    rows, deep = x.shape
    width = w_all.shape[1] - skip
    first, cat_first = skip // tile, (cat.shape[1] - width) // tile
    n_w = len(ws)
    return pl.pallas_call(
        functools.partial(pre_kernel, w_cuts, n_w),
        grid_spec=pltpu.PrefetchScalarGridSpec(
            num_scalar_prefetch=1,
            grid=(width // tile,),
            in_specs=[pl.BlockSpec((rows, deep), lambda i, at: (0, 0))]
            + [pl.BlockSpec((w.shape[0], tile), lambda i, at: (0, first + i)) for w in ws]
            + [pl.BlockSpec((1, tile), lambda i, at: (0, first + i))]
            + [pl.BlockSpec(memory_space=pl.ANY)] * 2,
            out_specs=[
                pl.BlockSpec((rows, tile), lambda i, at: (0, i)),
                pl.BlockSpec((rows, tile), lambda i, at: (0, cat_first + i)),
                pl.BlockSpec((deep, tile), lambda i, at: (0, first + i)),
            ],
        ),
        out_shape=[
            jax.ShapeDtypeStruct((rows, width), F32),
            jax.ShapeDtypeStruct(cat.shape, BF),
            jax.ShapeDtypeStruct(w_all.shape, BF),
        ],
        input_output_aliases={3 + n_w: 1, 4 + n_w: 2},
        **big("pre_project", 2 * rows * deep * width, 2 * deep * (rows + width) + 6 * rows * width),
    )(places, x, *ws, b, cat, w_all)


def by_rank(at_ref, acc, out, blk_size):
    for i in range(acc.shape[0] // blk_size):
        at = pl.multiple_of(at_ref[i], blk_size)
        out[i * blk_size : (i + 1) * blk_size, :] = acc[pl.ds(at, blk_size), :].astype(out.dtype)


def out_kernel(w_cuts, n_w, n_blk, blk_size, at_ref, x_ref, *refs):
    ws, out_ref, w_ref, acc = refs[:n_w], refs[-3], refs[-2], refs[-1]
    lay(ws, w_cuts, at_ref, n_blk, w_ref)
    acc[...] = dot(x_ref[...], w_ref[...], 1, 0)
    by_rank(at_ref, acc, out_ref, blk_size)


def out_project(x, ws, w_cuts, places, n_blk, blk_size):
    rows, deep = x.shape
    width = ws[0].shape[1]
    tile = min(512, width)
    return pl.pallas_call(
        functools.partial(out_kernel, w_cuts, len(ws), n_blk, blk_size),
        grid_spec=pltpu.PrefetchScalarGridSpec(
            num_scalar_prefetch=1,
            grid=(width // tile,),
            in_specs=[pl.BlockSpec((rows, deep), lambda i, at: (0, 0))]
            + [pl.BlockSpec((w.shape[0], tile), lambda i, at: (0, i)) for w in ws],
            out_specs=[
                pl.BlockSpec((rows, tile), lambda i, at: (0, i)),
                pl.BlockSpec((deep, tile), lambda i, at: (0, i)),
            ],
            scratch_shapes=[pltpu.VMEM((rows, tile), F32)],
        ),
        out_shape=[
            jax.ShapeDtypeStruct((rows, width), BF),
            jax.ShapeDtypeStruct((deep, width), BF),
        ],
        **big("out_project", 2 * rows * deep * width, 2 * deep * (rows + width) + 3 * rows * width),
    )(places, x, *ws)


def norm_kernel_back(blk_size, at_ref, x_ref, w_ref, out_ref, acc):
    acc[...] = dot(x_ref[...], w_ref[...], 1, 1)
    by_rank(at_ref, acc, out_ref, blk_size)


def norm_back(x, w, places, blk_size):
    rows, deep = x.shape
    width = w.shape[0]
    tile = min(256, width)
    return pl.pallas_call(
        functools.partial(norm_kernel_back, blk_size),
        grid_spec=pltpu.PrefetchScalarGridSpec(
            num_scalar_prefetch=1,
            grid=(width // tile,),
            in_specs=[
                pl.BlockSpec((rows, deep), lambda i, at: (0, 0)),
                pl.BlockSpec((tile, deep), lambda i, at: (i, 0)),
            ],
            out_specs=pl.BlockSpec((rows, tile), lambda i, at: (0, i)),
            scratch_shapes=[pltpu.VMEM((rows, tile), F32)],
        ),
        out_shape=jax.ShapeDtypeStruct((rows, width), BF),
        **big("norm_back", 2 * rows * deep * width, 2 * deep * (rows + width) + 3 * rows * width),
    )(places, x, w)


def d_cat_kernel(cuts, at_ref, g_ref, w_ref, pre_ref, datt_ref, dproj_ref, sum_ref, x_ref):
    @pl.when(pl.program_id(0) == 0)
    def _():
        lay([g_ref], cuts, at_ref, 0, x_ref)
        datt_ref[...] = dot(x_ref[...], w_ref[...], 1, 1).astype(BF)

    @pl.when(pl.program_id(0) > 0)
    def _():
        total = 0.0
        for rows in chunks(x_ref.shape[0]):
            d_pre = gelu_parts(pre_ref[rows, :])[1] * dot(x_ref[rows, :], w_ref[...], 1, 1)
            dproj_ref[rows, :] = d_pre.astype(BF)
            total = total + jnp.sum(d_pre, axis=0, keepdims=True)
        sum_ref[...] = total


def d_cat_parts(g, places, w, pre_act, wide_a):
    rows, deep = g.shape
    width = pre_act.shape[1]
    tile = wide_a
    total = 3 * wide_a + width
    blk = rows // places.shape[0]
    cuts = tuple((0, i * blk, blk) for i in range(places.shape[0]))

    def col(i):
        return jnp.maximum(i - 1, 0)

    return pl.pallas_call(
        functools.partial(d_cat_kernel, cuts),
        grid_spec=pltpu.PrefetchScalarGridSpec(
            num_scalar_prefetch=1,
            grid=(1 + width // tile,),
            in_specs=[
                pl.BlockSpec((rows, deep), lambda i, at: (0, 0)),
                pl.BlockSpec((tile, deep), lambda i, at: (i, 0)),
                pl.BlockSpec((rows, tile), lambda i, at: (0, col(i))),
            ],
            out_specs=[
                pl.BlockSpec((rows, tile), lambda i, at: (0, 0)),
                pl.BlockSpec((rows, tile), lambda i, at: (0, 3 + col(i))),
                pl.BlockSpec((1, tile), lambda i, at: (0, col(i))),
                pl.BlockSpec((rows, deep), lambda i, at: (0, 0)),
            ],
        ),
        out_shape=[
            jax.ShapeDtypeStruct((rows, tile), BF),
            jax.ShapeDtypeStruct((rows, total), BF),
            jax.ShapeDtypeStruct((1, width), F32),
            jax.ShapeDtypeStruct((rows, deep), BF),
        ],
        **big("d_cat_parts", 2 * rows * deep * (width + tile), 2 * deep * rows + (2 * deep + 6 * rows) * width),
    )(places, g, w, pre_act)


def join_kernel(n_parts, sizes, at_ref, *refs):
    dst = refs[-1]
    for j in range(n_parts):
        first = 0
        for i, size in enumerate(sizes):
            at = pl.multiple_of(at_ref[j * len(sizes) + i], 16)
            dst[pl.ds(at, size), :] = refs[j][first : first + size, :].astype(F32)
            first += size


def join_rows(parts, places, sizes):
    rows, width = parts[0].shape
    tile = min(512, width)
    return pl.pallas_call(
        functools.partial(join_kernel, len(parts), sizes),
        grid_spec=pltpu.PrefetchScalarGridSpec(
            num_scalar_prefetch=1,
            grid=(width // tile,),
            in_specs=[pl.BlockSpec((rows, tile), lambda i, at: (0, i))] * len(parts),
            out_specs=pl.BlockSpec((rows * len(parts), tile), lambda i, at: (0, i)),
        ),
        out_shape=jax.ShapeDtypeStruct((rows * len(parts), width), F32),
        **big("join_rows", 0, 6 * rows * len(parts) * width),
    )(places, *parts)


def after(x, *others):
    return lax.optimization_barrier((x, *others))[0]


def pass_on(x, hops):
    n = lax.axis_size("ctx")
    return lax.ppermute(x, "ctx", [(i, (i + hops) % n) for i in range(n)])


def reach(n):
    return n // 2, n - 1 - n // 2


def swap(x, axis, bit):
    n = lax.axis_size(axis)
    return lax.ppermute(x, axis, [(i, i ^ bit) for i in range(n)])


def near(x, bit):
    return swap(x, "fsdp", bit)


def far_keys(n):
    return sorted((k for k in range(2, n, 2)), key=lambda k: (k.bit_count(), k))


def top_bit(k):
    return 1 << (k.bit_length() - 1)


def low_bit(k):
    return k & -k


def halves(x):
    rows = x.shape[0] // 2
    return [x[:rows], x[rows:]]


class Line:
    def __init__(self):
        self.due = []

    def wait(self, *arrays):
        self.due += list(arrays)

    def tied(self, *xs):
        got = list(lax.optimization_barrier((*xs, *self.due)))[: len(xs)]
        self.due = got[:1]
        return got[0] if len(xs) == 1 else got


def ring_job(part, found):
    n = lax.axis_size("ctx")
    ups, downs = reach(n)
    found[0] = up = down = part
    for hop in range(1, ups + 1):
        if hop <= downs:
            up, down = yield [pass_on(up, 1), pass_on(down, -1)]
            found[n - hop] = down
        else:
            (up,) = yield [pass_on(up, 1)]
        found[hop] = up


def total_job(x, found):
    for axis in ("fsdp", "ctx"):
        bit = 1
        while bit < lax.axis_size(axis):
            (got,) = yield [swap(x, axis, bit)]
            x = x + got
            bit *= 2
    found.append(x)


def gather_job(shard, found):
    n = lax.axis_size("fsdp")
    have = {}
    keys = far_keys(n)
    fresh = [(0, None, shard)]
    found.extend(fresh)
    level = 0
    while True:
        level += 1
        send = []
        for k in keys:
            if k.bit_count() != level:
                continue
            if level == 1:
                send.append((k, None, near(shard, k)))
            else:
                for h, bit in ((0, top_bit(k)), (1, low_bit(k))):
                    send.append((k, h, near(have[k ^ bit, h], bit)))
        send += [(k | 1, h, near(x, 1)) for k, h, x in fresh if not k & 1]
        if not send:
            return
        got = yield [x for _, _, x in send]
        fresh = [(k, h, x) for (k, h, _), x in zip(send, got)]
        found.extend(fresh)
        for k, h, x in fresh:
            if not k & 1:
                if h is None:
                    have[k, 0], have[k, 1] = halves(x)
                else:
                    have[k, h] = x


def gather_order(n):
    got = [(0, None)]
    fresh = list(got)
    level = 0
    while True:
        level += 1
        new = []
        for k in far_keys(n):
            if k.bit_count() == level:
                new += [(k, None)] if level == 1 else [(k, 0), (k, 1)]
        new += [(k | 1, h) for k, h in fresh if not k & 1]
        if not new:
            return got
        got += new
        fresh = new


def scatter_job(away, home, found):
    n = lax.axis_size("fsdp")
    (got,) = yield [near(away, 1)]
    home = home() if callable(home) else home
    rows = home.shape[0] // (n // 2)
    hold = {}
    for i, k in enumerate(range(0, n, 2)):
        for h in range(2):
            at = i * rows + h * (rows // 2)
            cut = slice(at, at + rows // 2)
            hold[k, h] = home[cut].astype(F32) + got[cut].astype(F32)
    for level in range(n.bit_length() - 2, 0, -1):
        moves = []
        for k in far_keys(n):
            if k.bit_count() != level:
                continue
            if level > 1:
                for h, bit in ((0, top_bit(k)), (1, low_bit(k))):
                    moves.append((k ^ bit, h, near(hold[k, h].astype(BF), bit)))
            else:
                whole = jnp.concatenate([hold[k, 0], hold[k, 1]], axis=0).astype(BF)
                moves.append((0, None, near(whole, k)))
        got = yield [x for _, _, x in moves]
        for (k, h, _), x in zip(moves, got):
            if h is None:
                for i, part in enumerate(halves(x)):
                    hold[k, i] = hold[k, i] + part.astype(F32)
            else:
                hold[k, h] = hold[k, h] + x.astype(F32)
    found.append(jnp.concatenate([hold[0, 0], hold[0, 1]], axis=0).astype(BF))


class Move:
    def __init__(self, line, job):
        self.line, self.job, self.flight = line, job, next(job)

    def step(self, *more):
        moves = [m for m in (self, *more) if m.flight is not None]
        flights = [x for m in moves for x in m.flight]
        if not moves:
            return
        got = list(lax.optimization_barrier((*flights, *self.line.due)))[: len(flights)]
        self.line.due = list(got)
        for m in moves:
            own, got = got[: len(m.flight)], got[len(m.flight) :]
            try:
                m.flight = m.job.send(own)
            except StopIteration:
                m.flight = None

    def end(self, *more):
        while self.flight is not None:
            self.step(*more)


def gelu_tanh(values):
    return jax.nn.gelu(values, approximate=True)


def rotary_tables(positions):
    seq = positions.shape[0]
    half_rot = ROT_DIM // 2
    expon = jnp.arange(half_rot, dtype=F32) * (2.0 / ROT_DIM)
    freqs = ROPE_BASE ** (-expon)
    angles = positions.astype(F32)[:, None] * freqs[None, :]
    cosine, sine = jnp.cos(angles), jnp.sin(angles)
    zero = jnp.zeros_like(sine)
    rest = jnp.zeros((seq, HEAD_DIM - ROT_DIM), F32)
    c = jnp.concatenate([cosine, cosine, rest + 1.0], axis=1)
    up = jnp.concatenate([zero, sine, rest], axis=1)
    down = jnp.concatenate([-sine, zero, rest], axis=1)
    return tuple(jnp.concatenate([t, t], axis=1) for t in (c, up, down))


def shards(inputs, out_grad, block_order, ln_gain, ln_beta, w_in, b_in, w_out, b_out):
    n_ctx, n_fsdp = lax.axis_size("ctx"), lax.axis_size("fsdp")
    z, f = lax.axis_index("ctx"), lax.axis_index("fsdp")
    seq_in, seq_grad, blk_order = inputs[0], out_grad[0], block_order[0]
    tok_rows = seq_in.shape[0]
    seq_len = tok_rows * n_ctx
    n_blk = blk_order.shape[0]
    blk_size = seq_len // n_blk
    per = n_blk // n_ctx
    wide_d = D // n_fsdp
    shard = w_out.shape[0]
    cat_rows = shard * n_fsdp
    in_cols = w_in.shape[1]
    n_heads = HEADS // n_ctx
    wide_a, wide_m = D // n_ctx, (cat_rows - D) // n_ctx
    even, att_runs, act_runs = plan(n_fsdp, n_ctx, cat_rows)
    z_runs = [in_runs(att_runs[i], act_runs[i]) for i in range(n_ctx)]

    def position_of(k):
        return lax.shift_right_logical(k, 1) + lax.bitwise_and(k, 1) * (n_fsdp // 2)

    rank_places = blk_order * blk_size
    ranks = lax.rem(z - jnp.arange(n_ctx, dtype=jnp.int32) + n_ctx, n_ctx)
    picks = (ranks[:, None] == jnp.arange(n_ctx, dtype=jnp.int32)[None, :]).astype(jnp.int32)
    row_places = jnp.sum(
        picks[:, :, None] * rank_places.reshape(1, n_ctx, per), axis=1, dtype=jnp.int32
    ).reshape(-1)

    line = Line()
    keys_at = {k: p for p, k in enumerate(key_order(n_fsdp))}
    share = shard // n_ctx
    mixed_f = [i for i in range(n_fsdp) if 0 < D - shard * i < shard]
    cut = (D - shard * mixed_f[0]) // n_ctx if mixed_f else share
    cut_m = share - cut
    is_mixed = (f == mixed_f[0]) if mixed_f else False

    def own_rows(whole):
        first = lax.dynamic_slice_in_dim(whole, z * share, share, 0)
        if not cut_m:
            return first
        both = jnp.concatenate(
            [
                lax.dynamic_slice_in_dim(whole, z * cut, cut, 0),
                lax.dynamic_slice_in_dim(whole, cut * n_ctx + z * cut_m, cut_m, 0),
            ],
            axis=0,
        )
        return jnp.where(is_mixed, both, first)

    def cuts_of(found):
        return [x for _, _, x in found], tuple((i, 0, x.shape[0]) for i, (_, _, x) in enumerate(found))

    order = gather_order(n_fsdp)
    w_at = jnp.asarray(
        [keys_at[k] * wide_d + (h or 0) * (wide_d // 2) for k, h in order], jnp.int32
    )
    o_keys = jnp.asarray([k for k, _ in order], jnp.int32)
    o_at = lax.bitwise_xor(f, o_keys) * share + jnp.asarray(
        [(h or 0) * (share // 2) for _, h in order], jnp.int32
    )
    qkv_at = jnp.concatenate([row_places, w_at])
    o_at = jnp.concatenate([rank_places, o_at if even else jnp.zeros((1,), jnp.int32)])

    normed_parts, w_in_parts, w_out_parts = {}, [], []
    w_in_own = pick_columns(w_in, z, z_runs)
    w_in_move = Move(line, gather_job(w_in_own, w_in_parts))
    line.wait(w_in_own)
    normed_own, dy_own = norm(line.tied(seq_in), seq_grad, ln_gain, ln_beta, f, n_fsdp)
    normed_ring = Move(line, ring_job(normed_own, normed_parts))
    line.wait(normed_own)
    tables = rotary_tables(line.tied(jnp.arange(seq_len, dtype=jnp.int32)))
    line.wait(*tables)
    b_in_z = jnp.stack([jnp.concatenate([b_in[s : s + n] for s, n in runs]) for runs in z_runs])[z]
    b_in_z = b_in_z[None]
    w_out_own = own_rows(line.tied(w_out)) if even else w_out
    line.wait(w_out_own, b_in_z, qkv_at, o_at, w_at, rank_places, row_places)

    while normed_ring.flight is not None:
        normed_ring.step(w_in_move)
    dy_all = lax.all_gather(after(dy_own, *line.due), "ctx", axis=0, tiled=True)
    w_in_move.end()
    if even:
        w_out_move = Move(line, gather_job(line.tied(w_out_own), w_out_parts))

    wide_q = 3 * wide_a
    x_cuts = [(j, i * blk_size, blk_size) for j in range(n_ctx) for i in range(per)]
    w_arrays, w_cuts = cuts_of(w_in_parts)
    xs = [normed_parts[j] for j in range(n_ctx)]
    qkv, normed, w_in_all = qkv_project(
        [line.tied(xs[0])] + xs[1:], tuple(x_cuts), w_arrays, w_cuts, qkv_at,
        b_in_z, seq_len, wide_q, wide_a,
    )
    line.wait(qkv)
    q_b, k_b, v_b, cat_b, lse = attention(line.tied(qkv), tables, n_heads, cat_rows // n_ctx)
    line.wait(cat_b)
    if even:
        w_out_move.step()
    pre_act, cat_b, w_in_all = pre_project(
        line.tied(normed), w_arrays, w_cuts, w_at, b_in_z, cat_b, w_in_all, wide_q, wide_a
    )
    line.wait(cat_b)
    if even:
        w_out_move.end()
        o_arrays, o_cuts = cuts_of(w_out_parts)
    else:
        w_all = lax.all_gather(w_out, "fsdp", axis=0, tiled=True)
        w_all = jnp.concatenate(
            [
                lax.dynamic_slice_in_dim(w_all, z * wide_a, wide_a, 0),
                lax.dynamic_slice_in_dim(w_all, D + z * wide_m, wide_m, 0),
            ],
            axis=0,
        )
        o_arrays, o_cuts = [w_all], ((0, 0, cat_rows // n_ctx),)
    out_part, w_out_z = out_project(line.tied(cat_b), o_arrays, o_cuts, o_at, n_blk, blk_size)
    line.wait(out_part)

    def ctx_sum(x):
        return lax.psum_scatter(x, "ctx", scatter_dimension=0, tiled=True)

    out_sum = ctx_sum(out_part)

    line.wait(dy_all)
    d_att, d_proj, sum_pre, dy = d_cat_parts(
        line.tied(dy_all), rank_places, w_out_z, pre_act, wide_a
    )
    line.wait(d_att)
    d_proj, *sum_qkv = attention_back(
        q_b, k_b, v_b, cat_b, line.tied(d_att), lse, tables, d_proj, n_heads
    )
    line.wait(d_proj)
    norm_part = norm_back(line.tied(d_proj), w_in_all, rank_places, blk_size)
    line.wait(norm_part)
    norm_sum = ctx_sum(norm_part)

    half = D // 2
    out_own, pre_own, qkv_own = [], [], []
    out_parts, pre_parts, qkv_parts = {}, {}, {}
    away, home = grads(line.tied(cat_b), 0, cat_rows // n_ctx, dy, 0, D, f, n_fsdp)
    line.wait(away)
    out_scatter = Move(line, scatter_job(line.tied(away), home, out_own)) if even else None
    (pre_away,) = grads(line.tied(normed), 1, half, d_proj, wide_q, wide_m, f)
    line.wait(pre_away)
    if even:
        out_scatter.step()
    (pre_home,) = grads(line.tied(normed), 0, half, d_proj, wide_q, wide_m, f, late=(out_sum,))
    line.wait(pre_home)
    (qkv_away,) = grads(line.tied(normed), 1, half, d_proj, 0, wide_q, f)
    line.wait(qkv_away)
    if even:
        out_scatter.step()
    pre_scatter = Move(line, scatter_job(line.tied(pre_away), pre_home, pre_own))
    (qkv_home,) = grads(line.tied(normed), 0, half, d_proj, 0, wide_q, f)
    line.wait(qkv_home)
    if even:
        out_scatter.step(pre_scatter)
        out_ring = Move(line, ring_job(line.tied(out_own[0]), out_parts))
    else:
        pre_scatter.step()
    qkv_scatter = Move(line, scatter_job(line.tied(qkv_away), qkv_home, qkv_own))
    pre_scatter.step()

    norm_sum = line.tied(norm_sum)

    seq_in_t = line.tied(seq_in)
    centred = seq_in_t - jnp.mean(seq_in_t, axis=1, keepdims=True)
    inv_std = lax.rsqrt(jnp.mean(centred * centred, axis=1, keepdims=True) + LN_EPS)
    x_hat = centred * inv_std
    d_norm = jnp.concatenate(
        [
            lax.dynamic_slice_in_dim(norm_sum.astype(F32), position_of(f ^ i) * wide_d, wide_d, 1)
            for i in range(n_fsdp)
        ],
        axis=1,
    )
    small = jnp.stack(
        [jnp.sum(seq_grad, axis=0), jnp.sum(d_norm * x_hat, axis=0), jnp.sum(d_norm, axis=0)]
    )
    gain_grad = d_norm * ln_gain
    d_input = seq_grad + inv_std * (
        gain_grad
        - jnp.mean(gain_grad, axis=1, keepdims=True)
        - x_hat * jnp.mean(gain_grad * x_hat, axis=1, keepdims=True)
    )
    out_y = seq_in + out_sum.astype(F32) + b_out

    g_b_in_z = jnp.concatenate([x[0] for x in (*sum_qkv, sum_pre)])
    masked = jnp.where(
        jnp.arange(n_ctx)[:, None] == z, g_b_in_z[None, :], jnp.zeros((), F32)
    )
    runs = sorted((s, n, i, at) for i in range(n_ctx) for s, n, at in run_offsets(z_runs[i]))
    vector = jnp.concatenate([small.reshape(-1)] + [masked[i, at : at + n] for _, n, i, at in runs])
    line.wait(d_input)

    pre_runs = [[(s - 3 * D, n) for s, n in runs if s >= 3 * D] for runs in z_runs]
    qkv_runs = [[(s, n) for s, n in runs if s < 3 * D] for runs in z_runs]
    if even:
        out_ring.step(pre_scatter, qkv_scatter)
    else:
        pre_scatter.step(qkv_scatter)
    pre_scatter.end()
    pre_ring = Move(line, ring_job(line.tied(pre_own[0]), pre_parts))
    vectors = []
    if even:
        out_ring.end(qkv_scatter)
    vector_move = Move(line, total_job(line.tied(vector), vectors))
    if even:
        at = []
        for j in range(n_ctx):
            rank = lax.rem(z - j + n_ctx, n_ctx)
            at.append(jnp.where(is_mixed, rank * cut, rank * share))
            if cut_m:
                at.append(jnp.where(is_mixed, cut * n_ctx + rank * cut_m, rank * share + cut))
        g_w_out = join_rows(
            [line.tied(out_parts[0])] + [out_parts[j] for j in range(1, n_ctx)],
            jnp.stack(at).astype(jnp.int32),
            (cut, cut_m) if cut_m else (cut,),
        )
        line.wait(g_w_out)
    else:
        blocks = jnp.concatenate([home, away], axis=0).reshape(n_fsdp, -1, D)
        g_out = jnp.concatenate(
            [lax.dynamic_index_in_dim(blocks, position_of(f ^ i), 0, False) for i in range(n_fsdp)]
        )
        spread = jnp.zeros((cat_rows, D), BF)
        spread = lax.dynamic_update_slice_in_dim(spread, g_out[:wide_a], z * wide_a, 0)
        spread = lax.dynamic_update_slice_in_dim(spread, g_out[wide_a:], D + z * wide_m, 0)
        g_w_out = lax.psum_scatter(spread.astype(F32), "fsdp", scatter_dimension=0, tiled=True)
        g_w_out = lax.psum(g_w_out, "ctx")
    pre_ring.step(qkv_scatter, vector_move)
    qkv_scatter.end()
    qkv_ring = Move(line, ring_job(line.tied(qkv_own[0]), qkv_parts))
    pre_ring.end(vector_move)
    vector_move.step()
    in_turn = range(n_ctx)
    g_w_in = spread_columns(
        None,
        [line.tied(pre_parts[0])] + [pre_parts[j] for j in in_turn[1:]],
        z, pre_runs, in_cols, 3 * D, in_cols - 3 * D,
    )
    line.wait(g_w_in)
    qkv_ring.step(vector_move)
    qkv_ring.end(vector_move)
    vector_move.end()
    g_w_in = spread_columns(
        g_w_in, [qkv_parts[j] for j in in_turn], z, qkv_runs, in_cols, 0, 3 * D
    )
    vector = vectors[0]
    small = vector[: 3 * D].reshape(3, D)
    g_b_in = vector[3 * D :]

    def own_part(vector):
        length_part = vector.shape[0] // n_fsdp
        return lax.dynamic_slice_in_dim(vector, f * length_part, length_part, 0)

    return (
        out_y[None],
        d_input[None],
        g_w_in,
        own_part(g_b_in),
        g_w_out,
        own_part(small[0]),
        own_part(small[1]),
        own_part(small[2]),
    )


def run_offsets(runs):
    at, found = 0, []
    for start, size in runs:
        found.append((start, size, at))
        at += size
    return found


def solution(mesh):
    placed = (
        P("fsdp", "ctx", None),
        P("fsdp", "ctx", None),
        P("fsdp", None),
        P(),
        P(),
        P("fsdp", None),
        P(),
        P("fsdp", None),
        P(),
    )
    return jax.shard_map(
        shards,
        mesh=mesh,
        in_specs=placed,
        out_specs=(
            P("fsdp", "ctx", None),
            P("fsdp", "ctx", None),
            P("fsdp", None),
            P("fsdp"),
            P("fsdp", None),
            P("fsdp"),
            P("fsdp"),
            P("fsdp"),
        ),
        check_vma=False,
    )
```

```python
import functools
import math

import jax
import jax.numpy as jnp
from jax import lax
from jax.experimental import pallas as pl
from jax.experimental.pallas import tpu as pltpu
from jax.sharding import PartitionSpec as P

D = 2048
HEADS = 32
HEAD_DIM = 64
ROT_DIM = 32

LN_EPS = 1e-05
NEG_BIG = -1e30
ROPE_BASE = 10000.0
BF = jnp.bfloat16
F32 = jnp.float32
VMEM_BYTES = 56 * 1024 * 1024
HBM_SPEC = pl.BlockSpec(memory_space=pltpu.HBM)


def plan(n_fsdp, n_ctx, cat_rows):
    shard = cat_rows // n_fsdp
    even = True
    att, act = [[] for _ in range(n_ctx)], [[] for _ in range(n_ctx)]
    for f in range(n_fsdp):
        a = min(max(D - shard * f, 0), shard)
        m = shard - a
        if a % (n_ctx * HEAD_DIM) or m % (n_ctx * 16):
            even = False
        for z in range(n_ctx):
            if a:
                att[z].append((shard * f + z * (a // n_ctx), a // n_ctx))
            if m:
                act[z].append((shard * f + a + z * (m // n_ctx), m // n_ctx))
    if not even:
        wide_a, wide_m = D // n_ctx, (cat_rows - D) // n_ctx
        att = [[(z * wide_a, wide_a)] for z in range(n_ctx)]
        act = [[(D + z * wide_m, wide_m)] for z in range(n_ctx)]
    return even, att, act


def in_runs(att, act):
    runs = [(part * D + s, n) for part in range(3) for s, n in att]
    return runs + [(2 * D + s, n) for s, n in act]


def key_order(n):
    return list(range(0, n, 2)) + list(range(1, n, 2))


def pick_kernel(all_runs, z_ref, src_ref, dst_ref):
    for z, runs in enumerate(all_runs):

        @pl.when(z_ref[0] == z)
        def _():
            at = 0
            for start, size in runs:
                dst_ref[:, at : at + size] = src_ref[:, start : start + size]
                at += size


def pick_columns(src, z, all_runs):
    rows, cols = src.shape
    width = sum(n for _, n in all_runs[0])
    step = min(rows, 128)
    return pl.pallas_call(
        functools.partial(pick_kernel, all_runs),
        grid_spec=pltpu.PrefetchScalarGridSpec(
            num_scalar_prefetch=1,
            grid=(rows // step,),
            in_specs=[pl.BlockSpec((step, cols), lambda i, z_ref: (i, 0))],
            out_specs=pl.BlockSpec((step, width), lambda i, z_ref: (i, 0)),
        ),
        out_shape=jax.ShapeDtypeStruct((rows, width), src.dtype),
        **big("pick_columns", 0, 2 * rows * (cols + width)),
    )(z[None], src)


def spread_kernel(all_runs, n_ctx, z_ref, *refs):
    srcs, dst_ref = refs[:n_ctx], refs[-1]
    for z in range(n_ctx):

        @pl.when(z_ref[0] == z)
        def _():
            for j, src_ref in enumerate(srcs):
                at = 0
                for start, size in all_runs[(z - j) % n_ctx]:
                    dst_ref[:, start : start + size] = src_ref[:, at : at + size].astype(F32)
                    at += size


def spread_columns(whole, parts, z, all_runs, cols, first, width_out):
    rows, width = parts[0].shape
    n_ctx = len(parts)
    step = min(rows, 128)
    fresh = whole is None
    return pl.pallas_call(
        functools.partial(spread_kernel, all_runs, n_ctx),
        grid_spec=pltpu.PrefetchScalarGridSpec(
            num_scalar_prefetch=1,
            grid=(rows // step,),
            in_specs=[pl.BlockSpec((step, width), lambda i, z_ref: (i, 0))] * n_ctx
            + [pl.BlockSpec(memory_space=pl.ANY)] * (not fresh),
            out_specs=pl.BlockSpec(
                (pl.Element(step), pl.Element(width_out)), lambda i, z_ref: (i * step, first)
            ),
        ),
        out_shape=jax.ShapeDtypeStruct((rows, cols), F32),
        input_output_aliases={} if fresh else {1 + n_ctx: 0},
        **big("spread_columns", 0, rows * width_out * 6),
    )(z[None], *parts, *([] if fresh else [whole]))


def norm_kernel(n_fsdp, f_ref, x_ref, g_ref, gain_ref, beta_ref, out_ref, dy_ref, hold):
    x = x_ref[...]
    centred = x - jnp.mean(x, axis=1, keepdims=True)
    inv_std = lax.rsqrt(jnp.mean(centred * centred, axis=1, keepdims=True) + LN_EPS)
    hold[...] = (centred * inv_std * gain_ref[...] + beta_ref[...]).astype(BF)
    wide = x.shape[1] // n_fsdp
    for p, k in enumerate(key_order(n_fsdp)):
        at = pl.multiple_of((f_ref[0] ^ k) * wide, wide)
        out_ref[:, p * wide : (p + 1) * wide] = hold[:, pl.ds(at, wide)]
    dy_ref[...] = g_ref[...].astype(BF)


def norm(x, g, gain, beta, f, n_fsdp):
    rows, cols = x.shape
    step = min(rows, 128)
    tile = pl.BlockSpec((step, cols), lambda i, f_ref: (i, 0))
    line = pl.BlockSpec((1, cols), lambda i, f_ref: (0, 0))
    own = jax.ShapeDtypeStruct((rows, cols), BF)
    return pl.pallas_call(
        functools.partial(norm_kernel, n_fsdp),
        grid_spec=pltpu.PrefetchScalarGridSpec(
            num_scalar_prefetch=1,
            grid=(rows // step,),
            in_specs=[tile, tile, line, line],
            out_specs=[tile, tile],
            scratch_shapes=[pltpu.VMEM((step, cols), BF)],
        ),
        out_shape=[own, own],
        **big("norm", 0, 12 * rows * cols),
    )(f[None], x, g, gain[None], beta[None])


def turn(u, c, s_up, s_down):
    half_rot = ROT_DIM // 2
    wide = u.shape[1]
    return (
        u * c
        + pltpu.roll(u, half_rot, 1) * s_up
        + pltpu.roll(u, wide - half_rot, 1) * s_down
    )


def dot(a, b, ca, cb):
    return lax.dot_general(a, b, (((ca,), (cb,)), ((), ())), preferred_element_type=F32)


def causal(s):
    keys, size = s.shape
    key_at = lax.broadcasted_iota(jnp.int32, (size, size), 0)
    query_at = lax.broadcasted_iota(jnp.int32, (size, size), 1)
    own = jnp.where(key_at <= query_at, s[keys - size :], NEG_BIG)
    return own if keys == size else jnp.concatenate([s[: keys - size], own], axis=0)


def att_kernel(q_ref, k_ref, v_ref, c_ref, u_ref, d_ref, qb_ref, kb_ref, vb_ref, att_ref, lse_ref):
    seq = q_ref.shape[0]
    size = math.gcd(seq, 256)
    c, su, sd = c_ref[...], u_ref[...], d_ref[...]
    qb_ref[...] = turn(q_ref[...], c, su, sd).astype(BF)
    kb_ref[...] = turn(k_ref[...], c, su, sd).astype(BF)
    vb_ref[...] = v_ref[...].astype(BF)
    scale = jnp.asarray(1.0 / math.sqrt(HEAD_DIM), BF)
    for i in range(seq // size):
        rows = slice(i * size, (i + 1) * size)
        keys = (i + 1) * size
        outs = []
        for h in range(2):
            lanes = slice(h * HEAD_DIM, (h + 1) * HEAD_DIM)
            s = causal(dot(kb_ref[:keys, lanes], qb_ref[rows, lanes] * scale, 1, 1))
            top = jnp.max(s, axis=0, keepdims=True)
            e = jnp.exp(s - top)
            total = jnp.sum(e, axis=0, keepdims=True)
            lse_ref[0, h : h + 1, rows] = top + jnp.log(total)
            p = (e * (1.0 / total)).astype(BF)
            outs.append(dot(p, vb_ref[:keys, lanes], 0, 0))
        att_ref[rows, :] = jnp.concatenate(outs, axis=1).astype(BF)


def attention(project, tables, n_heads, cat_width):
    seq = project.shape[0]
    pairs = n_heads // 2
    wide = 2 * HEAD_DIM

    def col(base):
        return pl.BlockSpec((seq, wide), lambda p: (0, base + p))

    table = pl.BlockSpec((seq, wide), lambda p: (0, 0))
    own = jax.ShapeDtypeStruct((seq, n_heads * HEAD_DIM), BF)
    return pl.pallas_call(
        att_kernel,
        grid=(pairs,),
        in_specs=[col(0), col(pairs), col(2 * pairs), table, table, table],
        out_specs=[col(0)] * 4 + [pl.BlockSpec((1, 2, seq), lambda p: (p, 0, 0))],
        out_shape=[own] * 3
        + [
            jax.ShapeDtypeStruct((seq, cat_width), BF),
            jax.ShapeDtypeStruct((pairs, 2, seq), F32),
        ],
        **big("attention", n_heads * seq * seq * 256, seq * n_heads * 64 * 20),
    )(project, project, project, *tables)


def back_kernel(
    pairs, q_ref, k_ref, v_ref, att_ref, datt_ref, lse_ref, c_ref, u_ref, d_ref, dproj_in,
    dproj_ref, sq_ref, sk_ref, sv_ref, aq, ak, av, hold, sems,
):
    del dproj_in
    seq = q_ref.shape[0]
    size = math.gcd(seq, 256)
    scale = jnp.asarray(1.0 / math.sqrt(HEAD_DIM), BF)
    ak[...] = jnp.zeros_like(ak)
    av[...] = jnp.zeros_like(av)
    for i in range(seq // size):
        rows = slice(i * size, (i + 1) * size)
        keys = (i + 1) * size
        dqs, dks, dvs = [], [], []
        prod = datt_ref[rows, :].astype(F32) * att_ref[rows, :].astype(F32)
        prod_t = prod.T
        for h in range(2):
            lanes = slice(h * HEAD_DIM, (h + 1) * HEAD_DIM)
            q, do = q_ref[rows, lanes], datt_ref[rows, lanes]
            k, v = k_ref[:keys, lanes], v_ref[:keys, lanes]
            delta = jnp.sum(prod_t[lanes, :], axis=0, keepdims=True)
            q = q * scale
            s = causal(dot(k, q, 1, 1))
            p = jnp.exp(s - lse_ref[0, h : h + 1, rows])
            dp = dot(v, do, 1, 1)
            ds = (p * (dp - delta)).astype(BF)
            dvs.append(dot(p.astype(BF), do, 1, 0))
            dks.append(dot(ds, q, 1, 0))
            dqs.append(dot(k, ds, 0, 0).T * scale.astype(F32))
        av[:keys, :] += jnp.concatenate(dvs, axis=1)
        ak[:keys, :] += jnp.concatenate(dks, axis=1)
        aq[rows, :] = jnp.concatenate(dqs, axis=1)
    wide = q_ref.shape[1]
    copies = []
    for i, (acc, total) in enumerate(((aq, sq_ref), (ak, sk_ref), (av, sv_ref))):
        g = acc[...]
        if i < 2:
            g = turn(g, c_ref[...], -u_ref[...], -d_ref[...])
        hold[i] = g.astype(BF)
        total[...] = jnp.sum(g, axis=0, keepdims=True)
        at = pl.multiple_of((i * pairs + pl.program_id(0)) * wide, wide)
        copies.append(
            pltpu.make_async_copy(hold.at[i], dproj_ref.at[:, pl.ds(at, wide)], sems.at[i])
        )
        copies[-1].start()
    for copy in copies:
        copy.wait()


def attention_back(q, k, v, cat, d_att, lse, tables, d_proj, n_heads):
    seq = q.shape[0]
    pairs = n_heads // 2
    wide = 2 * HEAD_DIM
    col = pl.BlockSpec((seq, wide), lambda p: (0, p))
    table = pl.BlockSpec((seq, wide), lambda p: (0, 0))
    line = pl.BlockSpec((1, wide), lambda p: (0, p))
    return pl.pallas_call(
        functools.partial(back_kernel, pairs),
        grid=(pairs,),
        in_specs=[col] * 5
        + [pl.BlockSpec((1, 2, seq), lambda p: (p, 0, 0))]
        + [table] * 3
        + [HBM_SPEC],
        out_specs=[HBM_SPEC] + [line] * 3,
        out_shape=[jax.ShapeDtypeStruct(d_proj.shape, BF)]
        + [jax.ShapeDtypeStruct((1, n_heads * HEAD_DIM), F32)] * 3,
        input_output_aliases={9: 0},
        scratch_shapes=[pltpu.VMEM((seq, wide), F32)] * 3
        + [pltpu.VMEM((3, seq, wide), BF), pltpu.SemaphoreType.DMA((3,))],
        **big("attention_back", n_heads * seq * seq * 640, seq * n_heads * 64 * 16),
    )(q, k, v, cat, d_att, lse, *tables, d_proj)


def grads_kernel(n_split, n_late, f_ref, left_ref, right_ref, *refs):
    outs = refs[n_late:]
    g = dot(left_ref[...], right_ref[...], 0, 0).astype(BF)
    if len(outs) == 1:
        outs[0][...] = g
        return
    rows = g.shape[0] // n_split
    for s in range(n_split):
        key = lax.bitwise_xor(f_ref[0], s)
        at = pl.ds(pl.multiple_of(lax.shift_right_logical(key, 1) * rows, 16), rows)
        for i, out in enumerate(outs):

            @pl.when(lax.bitwise_and(key, 1) == 1 - i)
            def _():
                out[at, :] = g[s * rows : (s + 1) * rows]


def grads(left, block, wide, right, first, width, f, n_split=None, late=()):
    rows = left.shape[0]
    tile = math.gcd(512, math.gcd(width, first) if first else width)
    n_out = 2 if n_split else 1
    return pl.pallas_call(
        functools.partial(grads_kernel, n_split, len(late)),
        grid_spec=pltpu.PrefetchScalarGridSpec(
            num_scalar_prefetch=1,
            grid=(width // tile,),
            in_specs=[
                pl.BlockSpec((rows, wide), lambda i, f_ref: (0, block)),
                pl.BlockSpec((rows, tile), lambda i, f_ref: (0, first // tile + i)),
            ]
            + [pl.BlockSpec(memory_space=pl.ANY)] * len(late),
            out_specs=[pl.BlockSpec((wide // n_out, tile), lambda i, f_ref: (0, i))] * n_out,
        ),
        out_shape=[jax.ShapeDtypeStruct((wide // n_out, width), BF)] * n_out,
        **big("grads", 2 * rows * wide * width, 2 * rows * (wide + width) + 2 * wide * width),
    )(f[None], left, right, *late)


def chunks(rows):
    step = math.gcd(rows, 256)
    return [slice(at, at + step) for at in range(0, rows, step)]


def gelu_parts(u):
    c = math.sqrt(2.0 / math.pi)
    square = u * u
    t = jnp.tanh(c * (u + 0.044715 * u * square))
    value = 0.5 * u * (1.0 + t)
    slope = 0.5 * (1.0 + t) + 0.5 * u * (1.0 - t * t) * (c * (1.0 + 3 * 0.044715 * square))
    return value, slope


def cost(flops, nbytes):
    return pl.CostEstimate(flops=flops, bytes_accessed=nbytes, transcendentals=0)


def big(name_of, flops, nbytes):
    return {
        "compiler_params": pltpu.CompilerParams(vmem_limit_bytes=VMEM_BYTES),
        "cost_estimate": cost(flops // 64, nbytes // 64),
        "name": name_of,
    }


def lay(parts, cuts, at_ref, base, dst):
    for c, (i, start, size) in enumerate(cuts):
        at = pl.multiple_of(at_ref[base + c], 16)
        dst[pl.ds(at, size), :] = parts[i][start : start + size, :]


def qkv_kernel(x_cuts, n_x, w_cuts, n_w, at_ref, *refs):
    xs, ws, b_ref = refs[:n_x], refs[n_x : n_x + n_w], refs[n_x + n_w]
    out_ref, x_ref, w_ref = refs[n_x + n_w + 1 :]

    @pl.when(pl.program_id(0) == 0)
    def _():
        lay(xs, x_cuts, at_ref, 0, x_ref)

    lay(ws, w_cuts, at_ref, len(x_cuts), w_ref)
    out_ref[...] = dot(x_ref[...], w_ref[...], 1, 0) + b_ref[...]


def qkv_project(xs, x_cuts, ws, w_cuts, places, b, rows, width, tile):
    deep, full = xs[0].shape[1], ws[0].shape[1]
    return pl.pallas_call(
        functools.partial(qkv_kernel, x_cuts, len(xs), w_cuts, len(ws)),
        grid_spec=pltpu.PrefetchScalarGridSpec(
            num_scalar_prefetch=1,
            grid=(width // tile,),
            in_specs=[pl.BlockSpec(x.shape, lambda i, at: (0, 0)) for x in xs]
            + [pl.BlockSpec((w.shape[0], tile), lambda i, at: (0, i)) for w in ws]
            + [pl.BlockSpec((1, tile), lambda i, at: (0, i))],
            out_specs=[
                pl.BlockSpec((rows, tile), lambda i, at: (0, i)),
                pl.BlockSpec((rows, deep), lambda i, at: (0, 0)),
                pl.BlockSpec((deep, tile), lambda i, at: (0, i)),
            ],
        ),
        out_shape=[
            jax.ShapeDtypeStruct((rows, width), F32),
            jax.ShapeDtypeStruct((rows, deep), BF),
            jax.ShapeDtypeStruct((deep, full), BF),
        ],
        **big("qkv_project", 2 * rows * deep * width, 2 * deep * (rows + width) + 4 * rows * width),
    )(places, *xs, *ws, b)


def pre_kernel(w_cuts, n_w, at_ref, x_ref, *refs):
    ws, b_ref = refs[:n_w], refs[n_w]
    pre_ref, cat_ref, w_ref = refs[-3:]
    lay(ws, w_cuts, at_ref, 0, w_ref)
    for rows in chunks(x_ref.shape[0]):
        pre = dot(x_ref[rows, :], w_ref[...], 1, 0) + b_ref[...]
        pre_ref[rows, :] = pre
        cat_ref[rows, :] = gelu_parts(pre)[0].astype(BF)


def pre_project(x, ws, w_cuts, places, b, cat, w_all, skip, tile):
    rows, deep = x.shape
    width = w_all.shape[1] - skip
    first, cat_first = skip // tile, (cat.shape[1] - width) // tile
    n_w = len(ws)
    return pl.pallas_call(
        functools.partial(pre_kernel, w_cuts, n_w),
        grid_spec=pltpu.PrefetchScalarGridSpec(
            num_scalar_prefetch=1,
            grid=(width // tile,),
            in_specs=[pl.BlockSpec((rows, deep), lambda i, at: (0, 0))]
            + [pl.BlockSpec((w.shape[0], tile), lambda i, at: (0, first + i)) for w in ws]
            + [pl.BlockSpec((1, tile), lambda i, at: (0, first + i))]
            + [pl.BlockSpec(memory_space=pl.ANY)] * 2,
            out_specs=[
                pl.BlockSpec((rows, tile), lambda i, at: (0, i)),
                pl.BlockSpec((rows, tile), lambda i, at: (0, cat_first + i)),
                pl.BlockSpec((deep, tile), lambda i, at: (0, first + i)),
            ],
        ),
        out_shape=[
            jax.ShapeDtypeStruct((rows, width), F32),
            jax.ShapeDtypeStruct(cat.shape, BF),
            jax.ShapeDtypeStruct(w_all.shape, BF),
        ],
        input_output_aliases={3 + n_w: 1, 4 + n_w: 2},
        **big("pre_project", 2 * rows * deep * width, 2 * deep * (rows + width) + 6 * rows * width),
    )(places, x, *ws, b, cat, w_all)


def by_rank(at_ref, x_ref, w, side, out, blk_size):
    for rows in chunks(x_ref.shape[0]):
        part = dot(x_ref[rows, :], w[...], 1, side).astype(out.dtype)
        for at in range(0, part.shape[0], blk_size):
            to = pl.multiple_of(at_ref[(rows.start + at) // blk_size], blk_size)
            out[pl.ds(to, blk_size), :] = part[at : at + blk_size]


def out_kernel(w_cuts, n_w, n_blk, blk_size, at_ref, x_ref, *refs):
    ws, out_ref, w_ref = refs[:n_w], refs[-2], refs[-1]
    lay(ws, w_cuts, at_ref, n_blk, w_ref)
    by_rank(at_ref, x_ref, w_ref, 0, out_ref, blk_size)


def out_project(x, ws, w_cuts, places, n_blk, blk_size):
    rows, deep = x.shape
    width = ws[0].shape[1]
    tile = min(512, width)
    return pl.pallas_call(
        functools.partial(out_kernel, w_cuts, len(ws), n_blk, blk_size),
        grid_spec=pltpu.PrefetchScalarGridSpec(
            num_scalar_prefetch=1,
            grid=(width // tile,),
            in_specs=[pl.BlockSpec((rows, deep), lambda i, at: (0, 0))]
            + [pl.BlockSpec((w.shape[0], tile), lambda i, at: (0, i)) for w in ws],
            out_specs=[
                pl.BlockSpec((rows, tile), lambda i, at: (0, i)),
                pl.BlockSpec((deep, tile), lambda i, at: (0, i)),
            ],
        ),
        out_shape=[
            jax.ShapeDtypeStruct((rows, width), BF),
            jax.ShapeDtypeStruct((deep, width), BF),
        ],
        **big("out_project", 2 * rows * deep * width, 2 * deep * (rows + width) + 3 * rows * width),
    )(places, x, *ws)


def norm_kernel_back(blk_size, at_ref, x_ref, w_ref, out_ref):
    by_rank(at_ref, x_ref, w_ref, 1, out_ref, blk_size)


def norm_back(x, w, places, blk_size):
    rows, deep = x.shape
    width = w.shape[0]
    tile = min(256, width)
    return pl.pallas_call(
        functools.partial(norm_kernel_back, blk_size),
        grid_spec=pltpu.PrefetchScalarGridSpec(
            num_scalar_prefetch=1,
            grid=(width // tile,),
            in_specs=[
                pl.BlockSpec((rows, deep), lambda i, at: (0, 0)),
                pl.BlockSpec((tile, deep), lambda i, at: (i, 0)),
            ],
            out_specs=pl.BlockSpec((rows, tile), lambda i, at: (0, i)),
        ),
        out_shape=jax.ShapeDtypeStruct((rows, width), BF),
        **big("norm_back", 2 * rows * deep * width, 2 * deep * (rows + width) + 3 * rows * width),
    )(places, x, w)


def d_cat_kernel(cuts, at_ref, g_ref, w_ref, pre_ref, datt_ref, dproj_ref, sum_ref, x_ref):
    @pl.when(pl.program_id(0) == 0)
    def _():
        lay([g_ref], cuts, at_ref, 0, x_ref)
        datt_ref[...] = dot(x_ref[...], w_ref[...], 1, 1).astype(BF)

    @pl.when(pl.program_id(0) > 0)
    def _():
        total = 0.0
        for rows in chunks(x_ref.shape[0]):
            d_pre = gelu_parts(pre_ref[rows, :])[1] * dot(x_ref[rows, :], w_ref[...], 1, 1)
            dproj_ref[rows, :] = d_pre.astype(BF)
            total = total + jnp.sum(d_pre, axis=0, keepdims=True)
        sum_ref[...] = total


def d_cat_parts(g, places, w, pre_act, wide_a):
    rows, deep = g.shape
    width = pre_act.shape[1]
    tile = wide_a
    total = 3 * wide_a + width
    blk = rows // places.shape[0]
    cuts = tuple((0, i * blk, blk) for i in range(places.shape[0]))

    def col(i):
        return jnp.maximum(i - 1, 0)

    return pl.pallas_call(
        functools.partial(d_cat_kernel, cuts),
        grid_spec=pltpu.PrefetchScalarGridSpec(
            num_scalar_prefetch=1,
            grid=(1 + width // tile,),
            in_specs=[
                pl.BlockSpec((rows, deep), lambda i, at: (0, 0)),
                pl.BlockSpec((tile, deep), lambda i, at: (i, 0)),
                pl.BlockSpec((rows, tile), lambda i, at: (0, col(i))),
            ],
            out_specs=[
                pl.BlockSpec((rows, tile), lambda i, at: (0, 0)),
                pl.BlockSpec((rows, tile), lambda i, at: (0, 3 + col(i))),
                pl.BlockSpec((1, tile), lambda i, at: (0, col(i))),
                pl.BlockSpec((rows, deep), lambda i, at: (0, 0)),
            ],
        ),
        out_shape=[
            jax.ShapeDtypeStruct((rows, tile), BF),
            jax.ShapeDtypeStruct((rows, total), BF),
            jax.ShapeDtypeStruct((1, width), F32),
            jax.ShapeDtypeStruct((rows, deep), BF),
        ],
        **big("d_cat_parts", 2 * rows * deep * (width + tile), 2 * deep * rows + (2 * deep + 6 * rows) * width),
    )(places, g, w, pre_act)


def join_kernel(n_parts, sizes, at_ref, *refs):
    dst = refs[-1]
    for j in range(n_parts):
        first = 0
        for i, size in enumerate(sizes):
            at = pl.multiple_of(at_ref[j * len(sizes) + i], 16)
            dst[pl.ds(at, size), :] = refs[j][first : first + size, :].astype(F32)
            first += size


def join_rows(parts, places, sizes):
    rows, width = parts[0].shape
    tile = min(512, width)
    return pl.pallas_call(
        functools.partial(join_kernel, len(parts), sizes),
        grid_spec=pltpu.PrefetchScalarGridSpec(
            num_scalar_prefetch=1,
            grid=(width // tile,),
            in_specs=[pl.BlockSpec((rows, tile), lambda i, at: (0, i))] * len(parts),
            out_specs=pl.BlockSpec((rows * len(parts), tile), lambda i, at: (0, i)),
        ),
        out_shape=jax.ShapeDtypeStruct((rows * len(parts), width), F32),
        **big("join_rows", 0, 6 * rows * len(parts) * width),
    )(places, *parts)


def after(x, *others):
    return lax.optimization_barrier((x, *others))[0]


def pass_on(x, hops):
    n = lax.axis_size("ctx")
    return lax.ppermute(x, "ctx", [(i, (i + hops) % n) for i in range(n)])


def reach(n):
    return n // 2, n - 1 - n // 2


def swap(x, axis, bit):
    n = lax.axis_size(axis)
    return lax.ppermute(x, axis, [(i, i ^ bit) for i in range(n)])


def near(x, bit):
    return swap(x, "fsdp", bit)


def far_keys(n):
    return sorted((k for k in range(2, n, 2)), key=lambda k: (k.bit_count(), k))


def top_bit(k):
    return 1 << (k.bit_length() - 1)


def low_bit(k):
    return k & -k


def halves(x):
    rows = x.shape[0] // 2
    return [x[:rows], x[rows:]]


class Line:
    def __init__(self):
        self.due = []

    def wait(self, *arrays):
        self.due += list(arrays)

    def tied(self, *xs):
        got = list(lax.optimization_barrier((*xs, *self.due)))[: len(xs)]
        self.due = got[:1]
        return got[0] if len(xs) == 1 else got


def ring_job(part, found):
    n = lax.axis_size("ctx")
    ups, downs = reach(n)
    found[0] = up = down = part
    for hop in range(1, ups + 1):
        if hop <= downs:
            up, down = yield [pass_on(up, 1), pass_on(down, -1)]
            found[n - hop] = down
        else:
            (up,) = yield [pass_on(up, 1)]
        found[hop] = up


def total_job(x, found):
    for axis in ("fsdp", "ctx"):
        bit = 1
        while bit < lax.axis_size(axis):
            (got,) = yield [swap(x, axis, bit)]
            x = x + got
            bit *= 2
    found.append(x)


def gather_job(shard, found):
    n = lax.axis_size("fsdp")
    have = {}
    keys = far_keys(n)
    fresh = [(0, None, shard)]
    found.extend(fresh)
    level = 0
    while True:
        level += 1
        send = []
        for k in keys:
            if k.bit_count() != level:
                continue
            if level == 1:
                send.append((k, None, near(shard, k)))
            else:
                for h, bit in ((0, top_bit(k)), (1, low_bit(k))):
                    send.append((k, h, near(have[k ^ bit, h], bit)))
        send += [(k | 1, h, near(x, 1)) for k, h, x in fresh if not k & 1]
        if not send:
            return
        got = yield [x for _, _, x in send]
        fresh = [(k, h, x) for (k, h, _), x in zip(send, got)]
        found.extend(fresh)
        for k, h, x in fresh:
            if not k & 1:
                if h is None:
                    have[k, 0], have[k, 1] = halves(x)
                else:
                    have[k, h] = x


def gather_order(n):
    got = [(0, None)]
    fresh = list(got)
    level = 0
    while True:
        level += 1
        new = []
        for k in far_keys(n):
            if k.bit_count() == level:
                new += [(k, None)] if level == 1 else [(k, 0), (k, 1)]
        new += [(k | 1, h) for k, h in fresh if not k & 1]
        if not new:
            return got
        got += new
        fresh = new


def scatter_job(away, home, found):
    n = lax.axis_size("fsdp")
    (got,) = yield [near(away, 1)]
    home = home() if callable(home) else home
    rows = home.shape[0] // (n // 2)
    hold = {}
    for i, k in enumerate(range(0, n, 2)):
        for h in range(2):
            at = i * rows + h * (rows // 2)
            cut = slice(at, at + rows // 2)
            hold[k, h] = home[cut].astype(F32) + got[cut].astype(F32)
    for level in range(n.bit_length() - 2, 0, -1):
        moves = []
        for k in far_keys(n):
            if k.bit_count() != level:
                continue
            if level > 1:
                for h, bit in ((0, top_bit(k)), (1, low_bit(k))):
                    moves.append((k ^ bit, h, near(hold[k, h].astype(BF), bit)))
            else:
                whole = jnp.concatenate([hold[k, 0], hold[k, 1]], axis=0).astype(BF)
                moves.append((0, None, near(whole, k)))
        got = yield [x for _, _, x in moves]
        for (k, h, _), x in zip(moves, got):
            if h is None:
                for i, part in enumerate(halves(x)):
                    hold[k, i] = hold[k, i] + part.astype(F32)
            else:
                hold[k, h] = hold[k, h] + x.astype(F32)
    found.append(jnp.concatenate([hold[0, 0], hold[0, 1]], axis=0).astype(BF))


class Move:
    def __init__(self, line, job):
        self.line, self.job, self.flight = line, job, next(job)

    def step(self, *more):
        moves = [m for m in (self, *more) if m.flight is not None]
        flights = [x for m in moves for x in m.flight]
        if not moves:
            return
        got = list(lax.optimization_barrier((*flights, *self.line.due)))[: len(flights)]
        self.line.due = list(got)
        for m in moves:
            own, got = got[: len(m.flight)], got[len(m.flight) :]
            try:
                m.flight = m.job.send(own)
            except StopIteration:
                m.flight = None

    def end(self, *more):
        while self.flight is not None:
            self.step(*more)


def gelu_tanh(values):
    return jax.nn.gelu(values, approximate=True)


def rotary_tables(positions):
    seq = positions.shape[0]
    half_rot = ROT_DIM // 2
    expon = jnp.arange(half_rot, dtype=F32) * (2.0 / ROT_DIM)
    freqs = ROPE_BASE ** (-expon)
    angles = positions.astype(F32)[:, None] * freqs[None, :]
    cosine, sine = jnp.cos(angles), jnp.sin(angles)
    zero = jnp.zeros_like(sine)
    rest = jnp.zeros((seq, HEAD_DIM - ROT_DIM), F32)
    c = jnp.concatenate([cosine, cosine, rest + 1.0], axis=1)
    up = jnp.concatenate([zero, sine, rest], axis=1)
    down = jnp.concatenate([-sine, zero, rest], axis=1)
    return tuple(jnp.concatenate([t, t], axis=1) for t in (c, up, down))


def shards(inputs, out_grad, block_order, ln_gain, ln_beta, w_in, b_in, w_out, b_out):
    n_ctx, n_fsdp = lax.axis_size("ctx"), lax.axis_size("fsdp")
    z, f = lax.axis_index("ctx"), lax.axis_index("fsdp")
    seq_in, seq_grad, blk_order = inputs[0], out_grad[0], block_order[0]
    tok_rows = seq_in.shape[0]
    seq_len = tok_rows * n_ctx
    n_blk = blk_order.shape[0]
    blk_size = seq_len // n_blk
    per = n_blk // n_ctx
    wide_d = D // n_fsdp
    shard = w_out.shape[0]
    cat_rows = shard * n_fsdp
    in_cols = w_in.shape[1]
    n_heads = HEADS // n_ctx
    wide_a, wide_m = D // n_ctx, (cat_rows - D) // n_ctx
    even, att_runs, act_runs = plan(n_fsdp, n_ctx, cat_rows)
    z_runs = [in_runs(att_runs[i], act_runs[i]) for i in range(n_ctx)]

    def position_of(k):
        return lax.shift_right_logical(k, 1) + lax.bitwise_and(k, 1) * (n_fsdp // 2)

    rank_places = blk_order * blk_size
    blocks_at = jnp.arange(n_blk, dtype=jnp.int32)
    slots = jnp.sum(
        (blk_order[None, :] == blocks_at[:, None]).astype(jnp.int32) * blocks_at[None, :],
        axis=1, dtype=jnp.int32,
    ) * blk_size
    ranks = lax.rem(z - jnp.arange(n_ctx, dtype=jnp.int32) + n_ctx, n_ctx)
    picks = (ranks[:, None] == jnp.arange(n_ctx, dtype=jnp.int32)[None, :]).astype(jnp.int32)
    row_places = jnp.sum(
        picks[:, :, None] * rank_places.reshape(1, n_ctx, per), axis=1, dtype=jnp.int32
    ).reshape(-1)

    line = Line()
    keys_at = {k: p for p, k in enumerate(key_order(n_fsdp))}
    share = shard // n_ctx
    mixed_f = [i for i in range(n_fsdp) if 0 < D - shard * i < shard]
    cut = (D - shard * mixed_f[0]) // n_ctx if mixed_f else share
    cut_m = share - cut
    is_mixed = (f == mixed_f[0]) if mixed_f else False

    def own_rows(whole):
        first = lax.dynamic_slice_in_dim(whole, z * share, share, 0)
        if not cut_m:
            return first
        both = jnp.concatenate(
            [
                lax.dynamic_slice_in_dim(whole, z * cut, cut, 0),
                lax.dynamic_slice_in_dim(whole, cut * n_ctx + z * cut_m, cut_m, 0),
            ],
            axis=0,
        )
        return jnp.where(is_mixed, both, first)

    def cuts_of(found):
        return [x for _, _, x in found], tuple((i, 0, x.shape[0]) for i, (_, _, x) in enumerate(found))

    order = gather_order(n_fsdp)
    w_at = jnp.asarray(
        [keys_at[k] * wide_d + (h or 0) * (wide_d // 2) for k, h in order], jnp.int32
    )
    o_keys = jnp.asarray([k for k, _ in order], jnp.int32)
    o_at = lax.bitwise_xor(f, o_keys) * share + jnp.asarray(
        [(h or 0) * (share // 2) for _, h in order], jnp.int32
    )
    qkv_at = jnp.concatenate([row_places, w_at])
    o_at = jnp.concatenate([slots, o_at if even else jnp.zeros((1,), jnp.int32)])

    normed_parts, w_in_parts, w_out_parts = {}, [], []
    w_in_own = pick_columns(w_in, z, z_runs)
    w_in_move = Move(line, gather_job(w_in_own, w_in_parts))
    line.wait(w_in_own)
    normed_own, dy_own = norm(line.tied(seq_in), seq_grad, ln_gain, ln_beta, f, n_fsdp)
    normed_ring = Move(line, ring_job(normed_own, normed_parts))
    line.wait(normed_own)
    tables = rotary_tables(line.tied(jnp.arange(seq_len, dtype=jnp.int32)))
    line.wait(*tables)
    b_in_z = jnp.stack([jnp.concatenate([b_in[s : s + n] for s, n in runs]) for runs in z_runs])[z]
    b_in_z = b_in_z[None]
    w_out_own = own_rows(line.tied(w_out)) if even else w_out
    line.wait(w_out_own, b_in_z, qkv_at, o_at, w_at, rank_places, slots)

    while normed_ring.flight is not None:
        normed_ring.step(w_in_move)
    dy_all = lax.all_gather(after(dy_own, *line.due), "ctx", axis=0, tiled=True)
    w_in_move.end()
    if even:
        w_out_move = Move(line, gather_job(line.tied(w_out_own), w_out_parts))

    wide_q = 3 * wide_a
    x_cuts = [(j, i * blk_size, blk_size) for j in range(n_ctx) for i in range(per)]
    w_arrays, w_cuts = cuts_of(w_in_parts)
    xs = [normed_parts[j] for j in range(n_ctx)]
    qkv, normed, w_in_all = qkv_project(
        [line.tied(xs[0])] + xs[1:], tuple(x_cuts), w_arrays, w_cuts, qkv_at,
        b_in_z, seq_len, wide_q, wide_a,
    )
    line.wait(qkv)
    q_b, k_b, v_b, cat_b, lse = attention(line.tied(qkv), tables, n_heads, cat_rows // n_ctx)
    line.wait(cat_b)
    if even:
        w_out_move.step()
    pre_act, cat_b, w_in_all = pre_project(
        line.tied(normed), w_arrays, w_cuts, w_at, b_in_z, cat_b, w_in_all, wide_q, wide_a
    )
    line.wait(cat_b)
    if even:
        w_out_move.end()
        o_arrays, o_cuts = cuts_of(w_out_parts)
    else:
        w_all = lax.all_gather(w_out, "fsdp", axis=0, tiled=True)
        w_all = jnp.concatenate(
            [
                lax.dynamic_slice_in_dim(w_all, z * wide_a, wide_a, 0),
                lax.dynamic_slice_in_dim(w_all, D + z * wide_m, wide_m, 0),
            ],
            axis=0,
        )
        o_arrays, o_cuts = [w_all], ((0, 0, cat_rows // n_ctx),)
    out_part, w_out_z = out_project(line.tied(cat_b), o_arrays, o_cuts, o_at, n_blk, blk_size)
    line.wait(out_part)

    def ctx_sum(x):
        return lax.psum_scatter(x, "ctx", scatter_dimension=0, tiled=True)

    out_sum = ctx_sum(out_part)

    line.wait(dy_all)
    d_att, d_proj, sum_pre, dy = d_cat_parts(
        line.tied(dy_all), rank_places, w_out_z, pre_act, wide_a
    )
    line.wait(d_att)
    d_proj, *sum_qkv = attention_back(
        q_b, k_b, v_b, cat_b, line.tied(d_att), lse, tables, d_proj, n_heads
    )
    line.wait(d_proj)
    norm_part = norm_back(line.tied(d_proj), w_in_all, slots, blk_size)
    line.wait(norm_part)
    norm_sum = ctx_sum(norm_part)

    half = D // 2
    out_own, pre_own, qkv_own = [], [], []
    out_parts, pre_parts, qkv_parts = {}, {}, {}
    away, home = grads(line.tied(cat_b), 0, cat_rows // n_ctx, dy, 0, D, f, n_fsdp)
    line.wait(away)
    out_scatter = Move(line, scatter_job(line.tied(away), home, out_own)) if even else None
    (pre_away,) = grads(line.tied(normed), 1, half, d_proj, wide_q, wide_m, f)
    line.wait(pre_away)
    if even:
        out_scatter.step()
    (pre_home,) = grads(line.tied(normed), 0, half, d_proj, wide_q, wide_m, f, late=(out_sum,))
    line.wait(pre_home)
    (qkv_away,) = grads(line.tied(normed), 1, half, d_proj, 0, wide_q, f)
    line.wait(qkv_away)
    if even:
        out_scatter.step()
    pre_scatter = Move(line, scatter_job(line.tied(pre_away), pre_home, pre_own))
    (qkv_home,) = grads(line.tied(normed), 0, half, d_proj, 0, wide_q, f)
    line.wait(qkv_home)
    if even:
        out_scatter.step(pre_scatter)
        out_ring = Move(line, ring_job(line.tied(out_own[0]), out_parts))
    else:
        pre_scatter.step()
    qkv_scatter = Move(line, scatter_job(line.tied(qkv_away), qkv_home, qkv_own))
    pre_scatter.step()

    norm_sum = line.tied(norm_sum)

    seq_in_t = line.tied(seq_in)
    centred = seq_in_t - jnp.mean(seq_in_t, axis=1, keepdims=True)
    inv_std = lax.rsqrt(jnp.mean(centred * centred, axis=1, keepdims=True) + LN_EPS)
    x_hat = centred * inv_std
    d_norm = jnp.concatenate(
        [
            lax.dynamic_slice_in_dim(norm_sum.astype(F32), position_of(f ^ i) * wide_d, wide_d, 1)
            for i in range(n_fsdp)
        ],
        axis=1,
    )
    small = jnp.stack(
        [jnp.sum(seq_grad, axis=0), jnp.sum(d_norm * x_hat, axis=0), jnp.sum(d_norm, axis=0)]
    )
    gain_grad = d_norm * ln_gain
    d_input = seq_grad + inv_std * (
        gain_grad
        - jnp.mean(gain_grad, axis=1, keepdims=True)
        - x_hat * jnp.mean(gain_grad * x_hat, axis=1, keepdims=True)
    )
    out_y = seq_in + out_sum.astype(F32) + b_out

    g_b_in_z = jnp.concatenate([x[0] for x in (*sum_qkv, sum_pre)])
    masked = jnp.where(
        jnp.arange(n_ctx)[:, None] == z, g_b_in_z[None, :], jnp.zeros((), F32)
    )
    runs = sorted((s, n, i, at) for i in range(n_ctx) for s, n, at in run_offsets(z_runs[i]))
    vector = jnp.concatenate([small.reshape(-1)] + [masked[i, at : at + n] for _, n, i, at in runs])
    line.wait(d_input)

    pre_runs = [[(s - 3 * D, n) for s, n in runs if s >= 3 * D] for runs in z_runs]
    qkv_runs = [[(s, n) for s, n in runs if s < 3 * D] for runs in z_runs]
    if even:
        out_ring.step(pre_scatter, qkv_scatter)
    else:
        pre_scatter.step(qkv_scatter)
    pre_scatter.end()
    pre_ring = Move(line, ring_job(line.tied(pre_own[0]), pre_parts))
    vectors = []
    if even:
        out_ring.end(qkv_scatter)
    vector_move = Move(line, total_job(line.tied(vector), vectors))
    if even:
        at = []
        for j in range(n_ctx):
            rank = lax.rem(z - j + n_ctx, n_ctx)
            at.append(jnp.where(is_mixed, rank * cut, rank * share))
            if cut_m:
                at.append(jnp.where(is_mixed, cut * n_ctx + rank * cut_m, rank * share + cut))
        g_w_out = join_rows(
            [line.tied(out_parts[0])] + [out_parts[j] for j in range(1, n_ctx)],
            jnp.stack(at).astype(jnp.int32),
            (cut, cut_m) if cut_m else (cut,),
        )
        line.wait(g_w_out)
    else:
        blocks = jnp.concatenate([home, away], axis=0).reshape(n_fsdp, -1, D)
        g_out = jnp.concatenate(
            [lax.dynamic_index_in_dim(blocks, position_of(f ^ i), 0, False) for i in range(n_fsdp)]
        )
        spread = jnp.zeros((cat_rows, D), BF)
        spread = lax.dynamic_update_slice_in_dim(spread, g_out[:wide_a], z * wide_a, 0)
        spread = lax.dynamic_update_slice_in_dim(spread, g_out[wide_a:], D + z * wide_m, 0)
        g_w_out = lax.psum_scatter(spread.astype(F32), "fsdp", scatter_dimension=0, tiled=True)
        g_w_out = lax.psum(g_w_out, "ctx")
    pre_ring.step(qkv_scatter, vector_move)
    qkv_scatter.end()
    qkv_ring = Move(line, ring_job(line.tied(qkv_own[0]), qkv_parts))
    pre_ring.end(vector_move)
    vector_move.step()
    in_turn = range(n_ctx)
    g_w_in = spread_columns(
        None,
        [line.tied(pre_parts[0])] + [pre_parts[j] for j in in_turn[1:]],
        z, pre_runs, in_cols, 3 * D, in_cols - 3 * D,
    )
    line.wait(g_w_in)
    qkv_ring.step(vector_move)
    qkv_ring.end(vector_move)
    vector_move.end()
    g_w_in = spread_columns(
        g_w_in, [qkv_parts[j] for j in in_turn], z, qkv_runs, in_cols, 0, 3 * D
    )
    vector = vectors[0]
    small = vector[: 3 * D].reshape(3, D)
    g_b_in = vector[3 * D :]

    def own_part(vector):
        length_part = vector.shape[0] // n_fsdp
        return lax.dynamic_slice_in_dim(vector, f * length_part, length_part, 0)

    return (
        out_y[None],
        d_input[None],
        g_w_in,
        own_part(g_b_in),
        g_w_out,
        own_part(small[0]),
        own_part(small[1]),
        own_part(small[2]),
    )


def run_offsets(runs):
    at, found = 0, []
    for start, size in runs:
        found.append((start, size, at))
        at += size
    return found


def solution(mesh):
    placed = (
        P("fsdp", "ctx", None),
        P("fsdp", "ctx", None),
        P("fsdp", None),
        P(),
        P(),
        P("fsdp", None),
        P(),
        P("fsdp", None),
        P(),
    )
    return jax.shard_map(
        shards,
        mesh=mesh,
        in_specs=placed,
        out_specs=(
            P("fsdp", "ctx", None),
            P("fsdp", "ctx", None),
            P("fsdp", None),
            P("fsdp"),
            P("fsdp", None),
            P("fsdp"),
            P("fsdp"),
            P("fsdp"),
        ),
        check_vma=False,
    )
```

```python
import functools
import math

import jax
import jax.numpy as jnp
from jax import lax
from jax.experimental import pallas as pl
from jax.experimental.pallas import tpu as pltpu
from jax.sharding import PartitionSpec as P

D = 2048
HEADS = 32
HEAD_DIM = 64
ROT_DIM = 32

LN_EPS = 1e-05
NEG_BIG = -1e30
ROPE_BASE = 10000.0
BF = jnp.bfloat16
F32 = jnp.float32
VMEM_BYTES = 56 * 1024 * 1024
HBM_SPEC = pl.BlockSpec(memory_space=pltpu.HBM)


def plan(n_fsdp, n_ctx, cat_rows):
    shard = cat_rows // n_fsdp
    even = True
    att, act = [[] for _ in range(n_ctx)], [[] for _ in range(n_ctx)]
    for f in range(n_fsdp):
        a = min(max(D - shard * f, 0), shard)
        m = shard - a
        if a % (n_ctx * HEAD_DIM) or m % (n_ctx * 16):
            even = False
        for z in range(n_ctx):
            if a:
                att[z].append((shard * f + z * (a // n_ctx), a // n_ctx))
            if m:
                act[z].append((shard * f + a + z * (m // n_ctx), m // n_ctx))
    if not even:
        wide_a, wide_m = D // n_ctx, (cat_rows - D) // n_ctx
        att = [[(z * wide_a, wide_a)] for z in range(n_ctx)]
        act = [[(D + z * wide_m, wide_m)] for z in range(n_ctx)]
    return even, att, act


def in_runs(att, act):
    runs = [(part * D + s, n) for part in range(3) for s, n in att]
    return runs + [(2 * D + s, n) for s, n in act]


def key_order(n):
    return list(range(0, n, 2)) + list(range(1, n, 2))


def pick_kernel(all_runs, z_ref, src_ref, dst_ref):
    for z, runs in enumerate(all_runs):

        @pl.when(z_ref[0] == z)
        def _():
            at = 0
            for start, size in runs:
                dst_ref[:, at : at + size] = src_ref[:, start : start + size]
                at += size


def pick_columns(src, z, all_runs):
    rows, cols = src.shape
    width = sum(n for _, n in all_runs[0])
    step = min(rows, 128)
    return pl.pallas_call(
        functools.partial(pick_kernel, all_runs),
        grid_spec=pltpu.PrefetchScalarGridSpec(
            num_scalar_prefetch=1,
            grid=(rows // step,),
            in_specs=[pl.BlockSpec((step, cols), lambda i, z_ref: (i, 0))],
            out_specs=pl.BlockSpec((step, width), lambda i, z_ref: (i, 0)),
        ),
        out_shape=jax.ShapeDtypeStruct((rows, width), src.dtype),
        **big("pick_columns", 0, 2 * rows * (cols + width)),
    )(z[None], src)


def spread_kernel(all_runs, n_ctx, z_ref, *refs):
    srcs, dst_ref = refs[:n_ctx], refs[-1]
    for z in range(n_ctx):

        @pl.when(z_ref[0] == z)
        def _():
            for j, src_ref in enumerate(srcs):
                at = 0
                for start, size in all_runs[(z - j) % n_ctx]:
                    dst_ref[:, start : start + size] = src_ref[:, at : at + size].astype(F32)
                    at += size


def spread_columns(whole, parts, z, all_runs, cols, first, width_out):
    rows, width = parts[0].shape
    n_ctx = len(parts)
    step = min(rows, 128)
    fresh = whole is None
    return pl.pallas_call(
        functools.partial(spread_kernel, all_runs, n_ctx),
        grid_spec=pltpu.PrefetchScalarGridSpec(
            num_scalar_prefetch=1,
            grid=(rows // step,),
            in_specs=[pl.BlockSpec((step, width), lambda i, z_ref: (i, 0))] * n_ctx
            + [pl.BlockSpec(memory_space=pl.ANY)] * (not fresh),
            out_specs=pl.BlockSpec(
                (pl.Element(step), pl.Element(width_out)), lambda i, z_ref: (i * step, first)
            ),
        ),
        out_shape=jax.ShapeDtypeStruct((rows, cols), F32),
        input_output_aliases={} if fresh else {1 + n_ctx: 0},
        **big("spread_columns", 0, rows * width_out * 6),
    )(z[None], *parts, *([] if fresh else [whole]))


def norm_kernel(n_fsdp, f_ref, x_ref, g_ref, gain_ref, beta_ref, out_ref, dy_ref, hold):
    x = x_ref[...]
    centred = x - jnp.mean(x, axis=1, keepdims=True)
    inv_std = lax.rsqrt(jnp.mean(centred * centred, axis=1, keepdims=True) + LN_EPS)
    hold[...] = (centred * inv_std * gain_ref[...] + beta_ref[...]).astype(BF)
    wide = x.shape[1] // n_fsdp
    for p, k in enumerate(key_order(n_fsdp)):
        at = pl.multiple_of((f_ref[0] ^ k) * wide, wide)
        out_ref[:, p * wide : (p + 1) * wide] = hold[:, pl.ds(at, wide)]
    dy_ref[...] = g_ref[...].astype(BF)


def norm(x, g, gain, beta, f, n_fsdp):
    rows, cols = x.shape
    step = min(rows, 128)
    tile = pl.BlockSpec((step, cols), lambda i, f_ref: (i, 0))
    line = pl.BlockSpec((1, cols), lambda i, f_ref: (0, 0))
    own = jax.ShapeDtypeStruct((rows, cols), BF)
    return pl.pallas_call(
        functools.partial(norm_kernel, n_fsdp),
        grid_spec=pltpu.PrefetchScalarGridSpec(
            num_scalar_prefetch=1,
            grid=(rows // step,),
            in_specs=[tile, tile, line, line],
            out_specs=[tile, tile],
            scratch_shapes=[pltpu.VMEM((step, cols), BF)],
        ),
        out_shape=[own, own],
        **big("norm", 0, 12 * rows * cols),
    )(f[None], x, g, gain[None], beta[None])


def turn(u, c, s_up, s_down):
    half_rot = ROT_DIM // 2
    wide = u.shape[1]
    return (
        u * c
        + pltpu.roll(u, half_rot, 1) * s_up
        + pltpu.roll(u, wide - half_rot, 1) * s_down
    )


def dot(a, b, ca, cb):
    return lax.dot_general(a, b, (((ca,), (cb,)), ((), ())), preferred_element_type=F32)


def causal(s):
    keys, size = s.shape
    key_at = lax.broadcasted_iota(jnp.int32, (size, size), 0)
    query_at = lax.broadcasted_iota(jnp.int32, (size, size), 1)
    own = jnp.where(key_at <= query_at, s[keys - size :], NEG_BIG)
    return own if keys == size else jnp.concatenate([s[: keys - size], own], axis=0)


def att_kernel(q_ref, k_ref, v_ref, c_ref, u_ref, d_ref, qb_ref, kb_ref, vb_ref, att_ref, lse_ref):
    seq = q_ref.shape[0]
    size = math.gcd(seq, 256)
    c, su, sd = c_ref[...], u_ref[...], d_ref[...]
    qb_ref[...] = turn(q_ref[...], c, su, sd).astype(BF)
    kb_ref[...] = turn(k_ref[...], c, su, sd).astype(BF)
    vb_ref[...] = v_ref[...].astype(BF)
    scale = jnp.asarray(1.0 / math.sqrt(HEAD_DIM), BF)
    for i in range(seq // size):
        rows = slice(i * size, (i + 1) * size)
        keys = (i + 1) * size
        outs = []
        for h in range(2):
            lanes = slice(h * HEAD_DIM, (h + 1) * HEAD_DIM)
            s = causal(dot(kb_ref[:keys, lanes], qb_ref[rows, lanes] * scale, 1, 1))
            top = jnp.max(s, axis=0, keepdims=True)
            e = jnp.exp(s - top)
            total = jnp.sum(e, axis=0, keepdims=True)
            lse_ref[0, h : h + 1, rows] = top + jnp.log(total)
            p = (e * (1.0 / total)).astype(BF)
            outs.append(dot(p, vb_ref[:keys, lanes], 0, 0))
        att_ref[rows, :] = jnp.concatenate(outs, axis=1).astype(BF)


def attention(project, tables, n_heads, cat_width):
    seq = project.shape[0]
    pairs = n_heads // 2
    wide = 2 * HEAD_DIM

    def col(base):
        return pl.BlockSpec((seq, wide), lambda p: (0, base + p))

    table = pl.BlockSpec((seq, wide), lambda p: (0, 0))
    own = jax.ShapeDtypeStruct((seq, n_heads * HEAD_DIM), BF)
    return pl.pallas_call(
        att_kernel,
        grid=(pairs,),
        in_specs=[col(0), col(pairs), col(2 * pairs), table, table, table],
        out_specs=[col(0)] * 4 + [pl.BlockSpec((1, 2, seq), lambda p: (p, 0, 0))],
        out_shape=[own] * 3
        + [
            jax.ShapeDtypeStruct((seq, cat_width), BF),
            jax.ShapeDtypeStruct((pairs, 2, seq), F32),
        ],
        **big("attention", n_heads * seq * seq * 256, seq * n_heads * 64 * 20),
    )(project, project, project, *tables)


def back_kernel(
    pairs, q_ref, k_ref, v_ref, att_ref, datt_ref, lse_ref, c_ref, u_ref, d_ref, dproj_in,
    dproj_ref, sq_ref, sk_ref, sv_ref, aq, ak, av, hold, sems,
):
    del dproj_in
    seq = q_ref.shape[0]
    size = math.gcd(seq, 256)
    scale = jnp.asarray(1.0 / math.sqrt(HEAD_DIM), BF)
    ak[...] = jnp.zeros_like(ak)
    av[...] = jnp.zeros_like(av)
    for i in range(seq // size):
        rows = slice(i * size, (i + 1) * size)
        keys = (i + 1) * size
        dqs, dks, dvs = [], [], []
        prod = datt_ref[rows, :].astype(F32) * att_ref[rows, :].astype(F32)
        prod_t = prod.T
        for h in range(2):
            lanes = slice(h * HEAD_DIM, (h + 1) * HEAD_DIM)
            q, do = q_ref[rows, lanes], datt_ref[rows, lanes]
            k, v = k_ref[:keys, lanes], v_ref[:keys, lanes]
            delta = jnp.sum(prod_t[lanes, :], axis=0, keepdims=True)
            q = q * scale
            s = causal(dot(k, q, 1, 1))
            p = jnp.exp(s - lse_ref[0, h : h + 1, rows])
            dp = dot(v, do, 1, 1)
            ds = (p * (dp - delta)).astype(BF)
            dvs.append(dot(p.astype(BF), do, 1, 0))
            dks.append(dot(ds, q, 1, 0))
            dqs.append(dot(k, ds, 0, 0).T * scale.astype(F32))
        av[:keys, :] += jnp.concatenate(dvs, axis=1)
        ak[:keys, :] += jnp.concatenate(dks, axis=1)
        aq[rows, :] = jnp.concatenate(dqs, axis=1)
    wide = q_ref.shape[1]
    copies = []
    for i, (acc, total) in enumerate(((aq, sq_ref), (ak, sk_ref), (av, sv_ref))):
        g = acc[...]
        if i < 2:
            g = turn(g, c_ref[...], -u_ref[...], -d_ref[...])
        hold[i] = g.astype(BF)
        total[...] = jnp.sum(g, axis=0, keepdims=True)
        at = pl.multiple_of((i * pairs + pl.program_id(0)) * wide, wide)
        copies.append(
            pltpu.make_async_copy(hold.at[i], dproj_ref.at[:, pl.ds(at, wide)], sems.at[i])
        )
        copies[-1].start()
    for copy in copies:
        copy.wait()


def attention_back(q, k, v, cat, d_att, lse, tables, d_proj, n_heads):
    seq = q.shape[0]
    pairs = n_heads // 2
    wide = 2 * HEAD_DIM
    col = pl.BlockSpec((seq, wide), lambda p: (0, p))
    table = pl.BlockSpec((seq, wide), lambda p: (0, 0))
    line = pl.BlockSpec((1, wide), lambda p: (0, p))
    return pl.pallas_call(
        functools.partial(back_kernel, pairs),
        grid=(pairs,),
        in_specs=[col] * 5
        + [pl.BlockSpec((1, 2, seq), lambda p: (p, 0, 0))]
        + [table] * 3
        + [HBM_SPEC],
        out_specs=[HBM_SPEC] + [line] * 3,
        out_shape=[jax.ShapeDtypeStruct(d_proj.shape, BF)]
        + [jax.ShapeDtypeStruct((1, n_heads * HEAD_DIM), F32)] * 3,
        input_output_aliases={9: 0},
        scratch_shapes=[pltpu.VMEM((seq, wide), F32)] * 3
        + [pltpu.VMEM((3, seq, wide), BF), pltpu.SemaphoreType.DMA((3,))],
        **big("attention_back", n_heads * seq * seq * 640, seq * n_heads * 64 * 16),
    )(q, k, v, cat, d_att, lse, *tables, d_proj)


def grads_kernel(n_split, n_late, f_ref, left_ref, right_ref, *refs):
    outs = refs[n_late:]
    g = dot(left_ref[...], right_ref[...], 0, 0).astype(BF)
    if len(outs) == 1:
        outs[0][...] = g
        return
    rows = g.shape[0] // n_split
    for s in range(n_split):
        key = lax.bitwise_xor(f_ref[0], s)
        at = pl.ds(pl.multiple_of(lax.shift_right_logical(key, 1) * rows, 16), rows)
        for i, out in enumerate(outs):

            @pl.when(lax.bitwise_and(key, 1) == 1 - i)
            def _():
                out[at, :] = g[s * rows : (s + 1) * rows]


def grads(left, block, wide, right, first, width, f, n_split=None, late=()):
    rows = left.shape[0]
    tile = math.gcd(512, math.gcd(width, first) if first else width)
    n_out = 2 if n_split else 1
    return pl.pallas_call(
        functools.partial(grads_kernel, n_split, len(late)),
        grid_spec=pltpu.PrefetchScalarGridSpec(
            num_scalar_prefetch=1,
            grid=(width // tile,),
            in_specs=[
                pl.BlockSpec((rows, wide), lambda i, f_ref: (0, block)),
                pl.BlockSpec((rows, tile), lambda i, f_ref: (0, first // tile + i)),
            ]
            + [pl.BlockSpec(memory_space=pl.ANY)] * len(late),
            out_specs=[pl.BlockSpec((wide // n_out, tile), lambda i, f_ref: (0, i))] * n_out,
        ),
        out_shape=[jax.ShapeDtypeStruct((wide // n_out, width), BF)] * n_out,
        **big("grads", 2 * rows * wide * width, 2 * rows * (wide + width) + 2 * wide * width),
    )(f[None], left, right, *late)


def chunks(rows):
    step = math.gcd(rows, 256)
    return [slice(at, at + step) for at in range(0, rows, step)]


def gelu_parts(u):
    c = math.sqrt(2.0 / math.pi)
    square = u * u
    t = jnp.tanh(c * (u + 0.044715 * u * square))
    value = 0.5 * u * (1.0 + t)
    slope = 0.5 * (1.0 + t) + 0.5 * u * (1.0 - t * t) * (c * (1.0 + 3 * 0.044715 * square))
    return value, slope


def cost(flops, nbytes):
    return pl.CostEstimate(flops=flops, bytes_accessed=nbytes, transcendentals=0)


def big(name_of, flops, nbytes):
    return {
        "compiler_params": pltpu.CompilerParams(vmem_limit_bytes=VMEM_BYTES),
        "cost_estimate": cost(flops, nbytes),
        "name": name_of,
    }


def lay(parts, cuts, at_ref, base, dst):
    for c, (i, start, size) in enumerate(cuts):
        at = pl.multiple_of(at_ref[base + c], 16)
        dst[pl.ds(at, size), :] = parts[i][start : start + size, :]


def qkv_kernel(x_cuts, n_x, w_cuts, n_w, at_ref, *refs):
    xs, ws, b_ref = refs[:n_x], refs[n_x : n_x + n_w], refs[n_x + n_w]
    out_ref, x_ref, w_ref = refs[n_x + n_w + 1 :]

    @pl.when(pl.program_id(0) == 0)
    def _():
        lay(xs, x_cuts, at_ref, 0, x_ref)

    lay(ws, w_cuts, at_ref, len(x_cuts), w_ref)
    out_ref[...] = dot(x_ref[...], w_ref[...], 1, 0) + b_ref[...]


def qkv_project(xs, x_cuts, ws, w_cuts, places, b, rows, width, tile):
    deep, full = xs[0].shape[1], ws[0].shape[1]
    return pl.pallas_call(
        functools.partial(qkv_kernel, x_cuts, len(xs), w_cuts, len(ws)),
        grid_spec=pltpu.PrefetchScalarGridSpec(
            num_scalar_prefetch=1,
            grid=(width // tile,),
            in_specs=[pl.BlockSpec(x.shape, lambda i, at: (0, 0)) for x in xs]
            + [pl.BlockSpec((w.shape[0], tile), lambda i, at: (0, i)) for w in ws]
            + [pl.BlockSpec((1, tile), lambda i, at: (0, i))],
            out_specs=[
                pl.BlockSpec((rows, tile), lambda i, at: (0, i)),
                pl.BlockSpec((rows, deep), lambda i, at: (0, 0)),
                pl.BlockSpec((deep, tile), lambda i, at: (0, i)),
            ],
        ),
        out_shape=[
            jax.ShapeDtypeStruct((rows, width), F32),
            jax.ShapeDtypeStruct((rows, deep), BF),
            jax.ShapeDtypeStruct((deep, full), BF),
        ],
        **big("qkv_project", 2 * rows * deep * width, 2 * deep * (rows + width) + 4 * rows * width),
    )(places, *xs, *ws, b)


def pre_kernel(w_cuts, n_w, at_ref, x_ref, *refs):
    ws, b_ref = refs[:n_w], refs[n_w]
    pre_ref, cat_ref, w_ref = refs[-3:]
    lay(ws, w_cuts, at_ref, 0, w_ref)
    for rows in chunks(x_ref.shape[0]):
        pre = dot(x_ref[rows, :], w_ref[...], 1, 0) + b_ref[...]
        pre_ref[rows, :] = pre
        cat_ref[rows, :] = gelu_parts(pre)[0].astype(BF)


def pre_project(x, ws, w_cuts, places, b, cat, w_all, skip, tile):
    rows, deep = x.shape
    width = w_all.shape[1] - skip
    first, cat_first = skip // tile, (cat.shape[1] - width) // tile
    n_w = len(ws)
    return pl.pallas_call(
        functools.partial(pre_kernel, w_cuts, n_w),
        grid_spec=pltpu.PrefetchScalarGridSpec(
            num_scalar_prefetch=1,
            grid=(width // tile,),
            in_specs=[pl.BlockSpec((rows, deep), lambda i, at: (0, 0))]
            + [pl.BlockSpec((w.shape[0], tile), lambda i, at: (0, first + i)) for w in ws]
            + [pl.BlockSpec((1, tile), lambda i, at: (0, first + i))]
            + [pl.BlockSpec(memory_space=pl.ANY)] * 2,
            out_specs=[
                pl.BlockSpec((rows, tile), lambda i, at: (0, i)),
                pl.BlockSpec((rows, tile), lambda i, at: (0, cat_first + i)),
                pl.BlockSpec((deep, tile), lambda i, at: (0, first + i)),
            ],
        ),
        out_shape=[
            jax.ShapeDtypeStruct((rows, width), F32),
            jax.ShapeDtypeStruct(cat.shape, BF),
            jax.ShapeDtypeStruct(w_all.shape, BF),
        ],
        input_output_aliases={3 + n_w: 1, 4 + n_w: 2},
        **big("pre_project", 2 * rows * deep * width, 2 * deep * (rows + width) + 6 * rows * width),
    )(places, x, *ws, b, cat, w_all)


def by_rank(at_ref, x_ref, w, side, out, blk_size):
    for rows in chunks(x_ref.shape[0]):
        part = dot(x_ref[rows, :], w[...], 1, side).astype(out.dtype)
        for at in range(0, part.shape[0], blk_size):
            to = pl.multiple_of(at_ref[(rows.start + at) // blk_size], blk_size)
            out[pl.ds(to, blk_size), :] = part[at : at + blk_size]


def out_kernel(w_cuts, n_w, n_blk, blk_size, at_ref, x_ref, *refs):
    ws, out_ref, w_ref = refs[:n_w], refs[-2], refs[-1]
    lay(ws, w_cuts, at_ref, n_blk, w_ref)
    by_rank(at_ref, x_ref, w_ref, 0, out_ref, blk_size)


def out_project(x, ws, w_cuts, places, n_blk, blk_size):
    rows, deep = x.shape
    width = ws[0].shape[1]
    tile = min(512, width)
    return pl.pallas_call(
        functools.partial(out_kernel, w_cuts, len(ws), n_blk, blk_size),
        grid_spec=pltpu.PrefetchScalarGridSpec(
            num_scalar_prefetch=1,
            grid=(width // tile,),
            in_specs=[pl.BlockSpec((rows, deep), lambda i, at: (0, 0))]
            + [pl.BlockSpec((w.shape[0], tile), lambda i, at: (0, i)) for w in ws],
            out_specs=[
                pl.BlockSpec((rows, tile), lambda i, at: (0, i)),
                pl.BlockSpec((deep, tile), lambda i, at: (0, i)),
            ],
        ),
        out_shape=[
            jax.ShapeDtypeStruct((rows, width), BF),
            jax.ShapeDtypeStruct((deep, width), BF),
        ],
        **big("out_project", 2 * rows * deep * width, 2 * deep * (rows + width) + 3 * rows * width),
    )(places, x, *ws)


def norm_kernel_back(blk_size, at_ref, x_ref, w_ref, out_ref):
    by_rank(at_ref, x_ref, w_ref, 1, out_ref, blk_size)


def norm_back(x, w, places, blk_size):
    rows, deep = x.shape
    width = w.shape[0]
    tile = min(256, width)
    return pl.pallas_call(
        functools.partial(norm_kernel_back, blk_size),
        grid_spec=pltpu.PrefetchScalarGridSpec(
            num_scalar_prefetch=1,
            grid=(width // tile,),
            in_specs=[
                pl.BlockSpec((rows, deep), lambda i, at: (0, 0)),
                pl.BlockSpec((tile, deep), lambda i, at: (i, 0)),
            ],
            out_specs=pl.BlockSpec((rows, tile), lambda i, at: (0, i)),
        ),
        out_shape=jax.ShapeDtypeStruct((rows, width), BF),
        **big("norm_back", 2 * rows * deep * width, 2 * deep * (rows + width) + 3 * rows * width),
    )(places, x, w)


def d_cat_kernel(cuts, at_ref, g_ref, w_ref, pre_ref, datt_ref, dproj_ref, sum_ref, x_ref):
    @pl.when(pl.program_id(0) == 0)
    def _():
        lay([g_ref], cuts, at_ref, 0, x_ref)
        datt_ref[...] = dot(x_ref[...], w_ref[...], 1, 1).astype(BF)

    @pl.when(pl.program_id(0) > 0)
    def _():
        total = 0.0
        for rows in chunks(x_ref.shape[0]):
            d_pre = gelu_parts(pre_ref[rows, :])[1] * dot(x_ref[rows, :], w_ref[...], 1, 1)
            dproj_ref[rows, :] = d_pre.astype(BF)
            total = total + jnp.sum(d_pre, axis=0, keepdims=True)
        sum_ref[...] = total


def d_cat_parts(g, places, w, pre_act, wide_a):
    rows, deep = g.shape
    width = pre_act.shape[1]
    tile = wide_a
    total = 3 * wide_a + width
    blk = rows // places.shape[0]
    cuts = tuple((0, i * blk, blk) for i in range(places.shape[0]))

    def col(i):
        return jnp.maximum(i - 1, 0)

    return pl.pallas_call(
        functools.partial(d_cat_kernel, cuts),
        grid_spec=pltpu.PrefetchScalarGridSpec(
            num_scalar_prefetch=1,
            grid=(1 + width // tile,),
            in_specs=[
                pl.BlockSpec((rows, deep), lambda i, at: (0, 0)),
                pl.BlockSpec((tile, deep), lambda i, at: (i, 0)),
                pl.BlockSpec((rows, tile), lambda i, at: (0, col(i))),
            ],
            out_specs=[
                pl.BlockSpec((rows, tile), lambda i, at: (0, 0)),
                pl.BlockSpec((rows, tile), lambda i, at: (0, 3 + col(i))),
                pl.BlockSpec((1, tile), lambda i, at: (0, col(i))),
                pl.BlockSpec((rows, deep), lambda i, at: (0, 0)),
            ],
        ),
        out_shape=[
            jax.ShapeDtypeStruct((rows, tile), BF),
            jax.ShapeDtypeStruct((rows, total), BF),
            jax.ShapeDtypeStruct((1, width), F32),
            jax.ShapeDtypeStruct((rows, deep), BF),
        ],
        **big("d_cat_parts", 2 * rows * deep * (width + tile), 2 * deep * rows + (2 * deep + 6 * rows) * width),
    )(places, g, w, pre_act)


def join_kernel(n_parts, sizes, at_ref, *refs):
    dst = refs[-1]
    for j in range(n_parts):
        first = 0
        for i, size in enumerate(sizes):
            at = pl.multiple_of(at_ref[j * len(sizes) + i], 16)
            dst[pl.ds(at, size), :] = refs[j][first : first + size, :].astype(F32)
            first += size


def join_rows(parts, places, sizes):
    rows, width = parts[0].shape
    tile = min(512, width)
    return pl.pallas_call(
        functools.partial(join_kernel, len(parts), sizes),
        grid_spec=pltpu.PrefetchScalarGridSpec(
            num_scalar_prefetch=1,
            grid=(width // tile,),
            in_specs=[pl.BlockSpec((rows, tile), lambda i, at: (0, i))] * len(parts),
            out_specs=pl.BlockSpec((rows * len(parts), tile), lambda i, at: (0, i)),
        ),
        out_shape=jax.ShapeDtypeStruct((rows * len(parts), width), F32),
        **big("join_rows", 0, 6 * rows * len(parts) * width),
    )(places, *parts)


def after(x, *others):
    return lax.optimization_barrier((x, *others))[0]


def pass_on(x, hops):
    n = lax.axis_size("ctx")
    return lax.ppermute(x, "ctx", [(i, (i + hops) % n) for i in range(n)])


def reach(n):
    return n // 2, n - 1 - n // 2


def swap(x, axis, bit):
    n = lax.axis_size(axis)
    return lax.ppermute(x, axis, [(i, i ^ bit) for i in range(n)])


def near(x, bit):
    return swap(x, "fsdp", bit)


def far_keys(n):
    return sorted((k for k in range(2, n, 2)), key=lambda k: (k.bit_count(), k))


def top_bit(k):
    return 1 << (k.bit_length() - 1)


def low_bit(k):
    return k & -k


def halves(x):
    rows = x.shape[0] // 2
    return [x[:rows], x[rows:]]


class Line:
    def __init__(self):
        self.due = []

    def wait(self, *arrays):
        self.due += list(arrays)

    def tied(self, *xs):
        got = list(lax.optimization_barrier((*xs, *self.due)))[: len(xs)]
        self.due = got[:1]
        return got[0] if len(xs) == 1 else got


def ring_job(part, found):
    n = lax.axis_size("ctx")
    ups, downs = reach(n)
    found[0] = up = down = part
    for hop in range(1, ups + 1):
        if hop <= downs:
            up, down = yield [pass_on(up, 1), pass_on(down, -1)]
            found[n - hop] = down
        else:
            (up,) = yield [pass_on(up, 1)]
        found[hop] = up


def total_job(x, found):
    for axis in ("fsdp", "ctx"):
        bit = 1
        while bit < lax.axis_size(axis):
            (got,) = yield [swap(x, axis, bit)]
            x = x + got
            bit *= 2
    found.append(x)


def gather_job(shard, found):
    n = lax.axis_size("fsdp")
    have = {}
    keys = far_keys(n)
    fresh = [(0, None, shard)]
    found.extend(fresh)
    level = 0
    while True:
        level += 1
        send = []
        for k in keys:
            if k.bit_count() != level:
                continue
            if level == 1:
                send.append((k, None, near(shard, k)))
            else:
                for h, bit in ((0, top_bit(k)), (1, low_bit(k))):
                    send.append((k, h, near(have[k ^ bit, h], bit)))
        send += [(k | 1, h, near(x, 1)) for k, h, x in fresh if not k & 1]
        if not send:
            return
        got = yield [x for _, _, x in send]
        fresh = [(k, h, x) for (k, h, _), x in zip(send, got)]
        found.extend(fresh)
        for k, h, x in fresh:
            if not k & 1:
                if h is None:
                    have[k, 0], have[k, 1] = halves(x)
                else:
                    have[k, h] = x


def gather_order(n):
    got = [(0, None)]
    fresh = list(got)
    level = 0
    while True:
        level += 1
        new = []
        for k in far_keys(n):
            if k.bit_count() == level:
                new += [(k, None)] if level == 1 else [(k, 0), (k, 1)]
        new += [(k | 1, h) for k, h in fresh if not k & 1]
        if not new:
            return got
        got += new
        fresh = new


def scatter_job(away, home, found):
    n = lax.axis_size("fsdp")
    (got,) = yield [near(away, 1)]
    home = home() if callable(home) else home
    rows = home.shape[0] // (n // 2)
    hold = {}
    for i, k in enumerate(range(0, n, 2)):
        for h in range(2):
            at = i * rows + h * (rows // 2)
            cut = slice(at, at + rows // 2)
            hold[k, h] = home[cut].astype(F32) + got[cut].astype(F32)
    for level in range(n.bit_length() - 2, 0, -1):
        moves = []
        for k in far_keys(n):
            if k.bit_count() != level:
                continue
            if level > 1:
                for h, bit in ((0, top_bit(k)), (1, low_bit(k))):
                    moves.append((k ^ bit, h, near(hold[k, h].astype(BF), bit)))
            else:
                whole = jnp.concatenate([hold[k, 0], hold[k, 1]], axis=0).astype(BF)
                moves.append((0, None, near(whole, k)))
        got = yield [x for _, _, x in moves]
        for (k, h, _), x in zip(moves, got):
            if h is None:
                for i, part in enumerate(halves(x)):
                    hold[k, i] = hold[k, i] + part.astype(F32)
            else:
                hold[k, h] = hold[k, h] + x.astype(F32)
    found.append(jnp.concatenate([hold[0, 0], hold[0, 1]], axis=0).astype(BF))


class Move:
    def __init__(self, line, job):
        self.line, self.job, self.flight = line, job, next(job)

    def step(self, *more):
        moves = [m for m in (self, *more) if m.flight is not None]
        flights = [x for m in moves for x in m.flight]
        if not moves:
            return
        got = list(lax.optimization_barrier((*flights, *self.line.due)))[: len(flights)]
        self.line.due = list(got)
        for m in moves:
            own, got = got[: len(m.flight)], got[len(m.flight) :]
            try:
                m.flight = m.job.send(own)
            except StopIteration:
                m.flight = None

    def end(self, *more):
        while self.flight is not None:
            self.step(*more)


def gelu_tanh(values):
    return jax.nn.gelu(values, approximate=True)


def rotary_tables(positions):
    seq = positions.shape[0]
    half_rot = ROT_DIM // 2
    expon = jnp.arange(half_rot, dtype=F32) * (2.0 / ROT_DIM)
    freqs = ROPE_BASE ** (-expon)
    angles = positions.astype(F32)[:, None] * freqs[None, :]
    cosine, sine = jnp.cos(angles), jnp.sin(angles)
    zero = jnp.zeros_like(sine)
    rest = jnp.zeros((seq, HEAD_DIM - ROT_DIM), F32)
    c = jnp.concatenate([cosine, cosine, rest + 1.0], axis=1)
    up = jnp.concatenate([zero, sine, rest], axis=1)
    down = jnp.concatenate([-sine, zero, rest], axis=1)
    return tuple(jnp.concatenate([t, t], axis=1) for t in (c, up, down))


def shards(inputs, out_grad, block_order, ln_gain, ln_beta, w_in, b_in, w_out, b_out):
    n_ctx, n_fsdp = lax.axis_size("ctx"), lax.axis_size("fsdp")
    z, f = lax.axis_index("ctx"), lax.axis_index("fsdp")
    seq_in, seq_grad, blk_order = inputs[0], out_grad[0], block_order[0]
    tok_rows = seq_in.shape[0]
    seq_len = tok_rows * n_ctx
    n_blk = blk_order.shape[0]
    blk_size = seq_len // n_blk
    per = n_blk // n_ctx
    wide_d = D // n_fsdp
    shard = w_out.shape[0]
    cat_rows = shard * n_fsdp
    in_cols = w_in.shape[1]
    n_heads = HEADS // n_ctx
    wide_a, wide_m = D // n_ctx, (cat_rows - D) // n_ctx
    even, att_runs, act_runs = plan(n_fsdp, n_ctx, cat_rows)
    z_runs = [in_runs(att_runs[i], act_runs[i]) for i in range(n_ctx)]

    def position_of(k):
        return lax.shift_right_logical(k, 1) + lax.bitwise_and(k, 1) * (n_fsdp // 2)

    rank_places = blk_order * blk_size
    blocks_at = jnp.arange(n_blk, dtype=jnp.int32)
    slots = jnp.sum(
        (blk_order[None, :] == blocks_at[:, None]).astype(jnp.int32) * blocks_at[None, :],
        axis=1, dtype=jnp.int32,
    ) * blk_size
    ranks = lax.rem(z - jnp.arange(n_ctx, dtype=jnp.int32) + n_ctx, n_ctx)
    picks = (ranks[:, None] == jnp.arange(n_ctx, dtype=jnp.int32)[None, :]).astype(jnp.int32)
    row_places = jnp.sum(
        picks[:, :, None] * rank_places.reshape(1, n_ctx, per), axis=1, dtype=jnp.int32
    ).reshape(-1)

    line = Line()
    keys_at = {k: p for p, k in enumerate(key_order(n_fsdp))}
    share = shard // n_ctx
    mixed_f = [i for i in range(n_fsdp) if 0 < D - shard * i < shard]
    cut = (D - shard * mixed_f[0]) // n_ctx if mixed_f else share
    cut_m = share - cut
    is_mixed = (f == mixed_f[0]) if mixed_f else False

    def own_rows(whole):
        first = lax.dynamic_slice_in_dim(whole, z * share, share, 0)
        if not cut_m:
            return first
        both = jnp.concatenate(
            [
                lax.dynamic_slice_in_dim(whole, z * cut, cut, 0),
                lax.dynamic_slice_in_dim(whole, cut * n_ctx + z * cut_m, cut_m, 0),
            ],
            axis=0,
        )
        return jnp.where(is_mixed, both, first)

    def cuts_of(found):
        return [x for _, _, x in found], tuple((i, 0, x.shape[0]) for i, (_, _, x) in enumerate(found))

    order = gather_order(n_fsdp)
    w_at = jnp.asarray(
        [keys_at[k] * wide_d + (h or 0) * (wide_d // 2) for k, h in order], jnp.int32
    )
    o_keys = jnp.asarray([k for k, _ in order], jnp.int32)
    o_at = lax.bitwise_xor(f, o_keys) * share + jnp.asarray(
        [(h or 0) * (share // 2) for _, h in order], jnp.int32
    )
    qkv_at = jnp.concatenate([row_places, w_at])
    o_at = jnp.concatenate([slots, o_at if even else jnp.zeros((1,), jnp.int32)])

    normed_parts, w_in_parts, w_out_parts = {}, [], []
    normed_own, dy_own = norm(seq_in, seq_grad, ln_gain, ln_beta, f, n_fsdp)
    normed_ring = Move(line, ring_job(normed_own, normed_parts))
    line.wait(normed_own)
    w_in_own = pick_columns(line.tied(w_in), z, z_runs)
    w_in_move = Move(line, gather_job(w_in_own, w_in_parts))
    line.wait(w_in_own)
    tables = rotary_tables(line.tied(jnp.arange(seq_len, dtype=jnp.int32)))
    line.wait(*tables)
    b_in_z = jnp.stack([jnp.concatenate([b_in[s : s + n] for s, n in runs]) for runs in z_runs])[z]
    b_in_z = b_in_z[None]
    w_out_own = own_rows(line.tied(w_out)) if even else w_out
    line.wait(w_out_own, b_in_z, qkv_at, o_at, w_at, rank_places, slots)

    normed_ring.step()
    w_in_move.step()
    while normed_ring.flight is not None:
        normed_ring.step(w_in_move)
    dy_all = lax.all_gather(after(dy_own, *line.due), "ctx", axis=0, tiled=True)
    w_in_move.end()
    if even:
        w_out_move = Move(line, gather_job(line.tied(w_out_own), w_out_parts))

    wide_q = 3 * wide_a
    x_cuts = [(j, i * blk_size, blk_size) for j in range(n_ctx) for i in range(per)]
    w_arrays, w_cuts = cuts_of(w_in_parts)
    xs = [normed_parts[j] for j in range(n_ctx)]
    qkv, normed, w_in_all = qkv_project(
        [line.tied(xs[0])] + xs[1:], tuple(x_cuts), w_arrays, w_cuts, qkv_at,
        b_in_z, seq_len, wide_q, wide_a,
    )
    line.wait(qkv)
    q_b, k_b, v_b, cat_b, lse = attention(line.tied(qkv), tables, n_heads, cat_rows // n_ctx)
    line.wait(cat_b)
    if even:
        w_out_move.step()
    pre_act, cat_b, w_in_all = pre_project(
        line.tied(normed), w_arrays, w_cuts, w_at, b_in_z, cat_b, w_in_all, wide_q, wide_a
    )
    line.wait(cat_b)
    if even:
        w_out_move.end()
        o_arrays, o_cuts = cuts_of(w_out_parts)
    else:
        w_all = lax.all_gather(w_out, "fsdp", axis=0, tiled=True)
        w_all = jnp.concatenate(
            [
                lax.dynamic_slice_in_dim(w_all, z * wide_a, wide_a, 0),
                lax.dynamic_slice_in_dim(w_all, D + z * wide_m, wide_m, 0),
            ],
            axis=0,
        )
        o_arrays, o_cuts = [w_all], ((0, 0, cat_rows // n_ctx),)
    out_part, w_out_z = out_project(line.tied(cat_b), o_arrays, o_cuts, o_at, n_blk, blk_size)
    line.wait(out_part)

    def ctx_sum(x):
        return lax.psum_scatter(x, "ctx", scatter_dimension=0, tiled=True)

    out_sum = ctx_sum(out_part)

    line.wait(dy_all)
    d_att, d_proj, sum_pre, dy = d_cat_parts(
        line.tied(dy_all), rank_places, w_out_z, pre_act, wide_a
    )
    line.wait(d_att)
    d_proj, *sum_qkv = attention_back(
        q_b, k_b, v_b, cat_b, line.tied(d_att), lse, tables, d_proj, n_heads
    )
    line.wait(d_proj)
    norm_part = norm_back(line.tied(d_proj), w_in_all, slots, blk_size)
    line.wait(norm_part)
    norm_sum = ctx_sum(norm_part)

    half = D // 2
    out_own, pre_own, qkv_own = [], [], []
    out_parts, pre_parts, qkv_parts = {}, {}, {}
    away, home = grads(line.tied(cat_b), 0, cat_rows // n_ctx, dy, 0, D, f, n_fsdp)
    line.wait(away)
    out_scatter = Move(line, scatter_job(line.tied(away), home, out_own)) if even else None
    (pre_away,) = grads(line.tied(normed), 1, half, d_proj, wide_q, wide_m, f)
    line.wait(pre_away)
    if even:
        out_scatter.step()
    (pre_home,) = grads(line.tied(normed), 0, half, d_proj, wide_q, wide_m, f, late=(out_sum,))
    line.wait(pre_home)
    (qkv_away,) = grads(line.tied(normed), 1, half, d_proj, 0, wide_q, f)
    line.wait(qkv_away)
    if even:
        out_scatter.step()
    pre_scatter = Move(line, scatter_job(line.tied(pre_away), pre_home, pre_own))
    (qkv_home,) = grads(line.tied(normed), 0, half, d_proj, 0, wide_q, f)
    line.wait(qkv_home)
    if even:
        out_scatter.end()
        out_ring = Move(line, ring_job(line.tied(out_own[0]), out_parts))
    pre_scatter.step()
    qkv_scatter = Move(line, scatter_job(line.tied(qkv_away), qkv_home, qkv_own))
    pre_scatter.step()

    norm_sum = line.tied(norm_sum)

    seq_in_t = line.tied(seq_in)
    centred = seq_in_t - jnp.mean(seq_in_t, axis=1, keepdims=True)
    inv_std = lax.rsqrt(jnp.mean(centred * centred, axis=1, keepdims=True) + LN_EPS)
    x_hat = centred * inv_std
    d_norm = jnp.concatenate(
        [
            lax.dynamic_slice_in_dim(norm_sum.astype(F32), position_of(f ^ i) * wide_d, wide_d, 1)
            for i in range(n_fsdp)
        ],
        axis=1,
    )
    small = jnp.stack(
        [jnp.sum(seq_grad, axis=0), jnp.sum(d_norm * x_hat, axis=0), jnp.sum(d_norm, axis=0)]
    )
    gain_grad = d_norm * ln_gain
    d_input = seq_grad + inv_std * (
        gain_grad
        - jnp.mean(gain_grad, axis=1, keepdims=True)
        - x_hat * jnp.mean(gain_grad * x_hat, axis=1, keepdims=True)
    )
    out_y = seq_in + out_sum.astype(F32) + b_out

    g_b_in_z = jnp.concatenate([x[0] for x in (*sum_qkv, sum_pre)])
    masked = jnp.where(
        jnp.arange(n_ctx)[:, None] == z, g_b_in_z[None, :], jnp.zeros((), F32)
    )
    runs = sorted((s, n, i, at) for i in range(n_ctx) for s, n, at in run_offsets(z_runs[i]))
    vector = jnp.concatenate([small.reshape(-1)] + [masked[i, at : at + n] for _, n, i, at in runs])
    line.wait(d_input)

    pre_runs = [[(s - 3 * D, n) for s, n in runs if s >= 3 * D] for runs in z_runs]
    qkv_runs = [[(s, n) for s, n in runs if s < 3 * D] for runs in z_runs]
    if even:
        out_ring.step(pre_scatter, qkv_scatter)
    else:
        pre_scatter.step(qkv_scatter)
    pre_scatter.end()
    pre_ring = Move(line, ring_job(line.tied(pre_own[0]), pre_parts))
    vectors = []
    if even:
        out_ring.end(qkv_scatter)
    vector_move = Move(line, total_job(line.tied(vector), vectors))
    if even:
        at = []
        for j in range(n_ctx):
            rank = lax.rem(z - j + n_ctx, n_ctx)
            at.append(jnp.where(is_mixed, rank * cut, rank * share))
            if cut_m:
                at.append(jnp.where(is_mixed, cut * n_ctx + rank * cut_m, rank * share + cut))
        g_w_out = join_rows(
            [line.tied(out_parts[0])] + [out_parts[j] for j in range(1, n_ctx)],
            jnp.stack(at).astype(jnp.int32),
            (cut, cut_m) if cut_m else (cut,),
        )
        line.wait(g_w_out)
    else:
        blocks = jnp.concatenate([home, away], axis=0).reshape(n_fsdp, -1, D)
        g_out = jnp.concatenate(
            [lax.dynamic_index_in_dim(blocks, position_of(f ^ i), 0, False) for i in range(n_fsdp)]
        )
        spread = jnp.zeros((cat_rows, D), BF)
        spread = lax.dynamic_update_slice_in_dim(spread, g_out[:wide_a], z * wide_a, 0)
        spread = lax.dynamic_update_slice_in_dim(spread, g_out[wide_a:], D + z * wide_m, 0)
        g_w_out = lax.psum_scatter(spread.astype(F32), "fsdp", scatter_dimension=0, tiled=True)
        g_w_out = lax.psum(g_w_out, "ctx")
    pre_ring.step(qkv_scatter, vector_move)
    qkv_scatter.end()
    qkv_ring = Move(line, ring_job(line.tied(qkv_own[0]), qkv_parts))
    pre_ring.end(vector_move)
    vector_move.step()
    in_turn = range(n_ctx)
    g_w_in = spread_columns(
        None,
        [line.tied(pre_parts[0])] + [pre_parts[j] for j in in_turn[1:]],
        z, pre_runs, in_cols, 3 * D, in_cols - 3 * D,
    )
    line.wait(g_w_in)
    qkv_ring.step(vector_move)
    qkv_ring.end(vector_move)
    vector_move.end()
    g_w_in = spread_columns(
        g_w_in, [qkv_parts[j] for j in in_turn], z, qkv_runs, in_cols, 0, 3 * D
    )
    vector = vectors[0]
    small = vector[: 3 * D].reshape(3, D)
    g_b_in = vector[3 * D :]

    def own_part(vector):
        length_part = vector.shape[0] // n_fsdp
        return lax.dynamic_slice_in_dim(vector, f * length_part, length_part, 0)

    return (
        out_y[None],
        d_input[None],
        g_w_in,
        own_part(g_b_in),
        g_w_out,
        own_part(small[0]),
        own_part(small[1]),
        own_part(small[2]),
    )


def run_offsets(runs):
    at, found = 0, []
    for start, size in runs:
        found.append((start, size, at))
        at += size
    return found


def solution(mesh):
    placed = (
        P("fsdp", "ctx", None),
        P("fsdp", "ctx", None),
        P("fsdp", None),
        P(),
        P(),
        P("fsdp", None),
        P(),
        P("fsdp", None),
        P(),
    )
    return jax.shard_map(
        shards,
        mesh=mesh,
        in_specs=placed,
        out_specs=(
            P("fsdp", "ctx", None),
            P("fsdp", "ctx", None),
            P("fsdp", None),
            P("fsdp"),
            P("fsdp", None),
            P("fsdp"),
            P("fsdp"),
            P("fsdp"),
        ),
        check_vma=False,
    )
```

```python
import functools
import math

import jax
import jax.numpy as jnp
from jax import lax
from jax.experimental import pallas as pl
from jax.experimental.pallas import tpu as pltpu
from jax.sharding import PartitionSpec as P

D = 2048
HEADS = 32
HEAD_DIM = 64
ROT_DIM = 32

LN_EPS = 1e-05
NEG_BIG = -1e30
ROPE_BASE = 10000.0
BF = jnp.bfloat16
F32 = jnp.float32
VMEM_BYTES = 56 * 1024 * 1024
HBM_SPEC = pl.BlockSpec(memory_space=pltpu.HBM)


def plan(n_fsdp, n_ctx, cat_rows):
    shard = cat_rows // n_fsdp
    even = True
    att, act = [[] for _ in range(n_ctx)], [[] for _ in range(n_ctx)]
    for f in range(n_fsdp):
        a = min(max(D - shard * f, 0), shard)
        m = shard - a
        if a % (n_ctx * HEAD_DIM) or m % (n_ctx * 16):
            even = False
        for z in range(n_ctx):
            if a:
                att[z].append((shard * f + z * (a // n_ctx), a // n_ctx))
            if m:
                act[z].append((shard * f + a + z * (m // n_ctx), m // n_ctx))
    if not even:
        wide_a, wide_m = D // n_ctx, (cat_rows - D) // n_ctx
        att = [[(z * wide_a, wide_a)] for z in range(n_ctx)]
        act = [[(D + z * wide_m, wide_m)] for z in range(n_ctx)]
    return even, att, act


def in_runs(att, act):
    runs = [(part * D + s, n) for part in range(3) for s, n in att]
    return runs + [(2 * D + s, n) for s, n in act]


def key_order(n):
    return list(range(0, n, 2)) + list(range(1, n, 2))


def pick_kernel(all_runs, z_ref, src_ref, dst_ref):
    for z, runs in enumerate(all_runs):

        @pl.when(z_ref[0] == z)
        def _():
            at = 0
            for start, size in runs:
                dst_ref[:, at : at + size] = src_ref[:, start : start + size]
                at += size


def pick_columns(src, z, all_runs):
    rows, cols = src.shape
    width = sum(n for _, n in all_runs[0])
    step = min(rows, 128)
    return pl.pallas_call(
        functools.partial(pick_kernel, all_runs),
        grid_spec=pltpu.PrefetchScalarGridSpec(
            num_scalar_prefetch=1,
            grid=(rows // step,),
            in_specs=[pl.BlockSpec((step, cols), lambda i, z_ref: (i, 0))],
            out_specs=pl.BlockSpec((step, width), lambda i, z_ref: (i, 0)),
        ),
        out_shape=jax.ShapeDtypeStruct((rows, width), src.dtype),
        **big("pick_columns", 0, 2 * rows * (cols + width)),
    )(z[None], src)


def spread_kernel(all_runs, n_ctx, z_ref, *refs):
    srcs, dst_ref = refs[:n_ctx], refs[-1]
    for z in range(n_ctx):

        @pl.when(z_ref[0] == z)
        def _():
            for j, src_ref in enumerate(srcs):
                at = 0
                for start, size in all_runs[(z - j) % n_ctx]:
                    dst_ref[:, start : start + size] = src_ref[:, at : at + size].astype(F32)
                    at += size


def spread_columns(whole, parts, z, all_runs, cols, first, width_out):
    rows, width = parts[0].shape
    n_ctx = len(parts)
    step = min(rows, 128)
    fresh = whole is None
    return pl.pallas_call(
        functools.partial(spread_kernel, all_runs, n_ctx),
        grid_spec=pltpu.PrefetchScalarGridSpec(
            num_scalar_prefetch=1,
            grid=(rows // step,),
            in_specs=[pl.BlockSpec((step, width), lambda i, z_ref: (i, 0))] * n_ctx
            + [pl.BlockSpec(memory_space=pl.ANY)] * (not fresh),
            out_specs=pl.BlockSpec(
                (pl.Element(step), pl.Element(width_out)), lambda i, z_ref: (i * step, first)
            ),
        ),
        out_shape=jax.ShapeDtypeStruct((rows, cols), F32),
        input_output_aliases={} if fresh else {1 + n_ctx: 0},
        **big("spread_columns", 0, rows * width_out * 6),
    )(z[None], *parts, *([] if fresh else [whole]))


def norm_kernel(n_fsdp, f_ref, x_ref, g_ref, gain_ref, beta_ref, out_ref, dy_ref, hold):
    x = x_ref[...]
    centred = x - jnp.mean(x, axis=1, keepdims=True)
    inv_std = lax.rsqrt(jnp.mean(centred * centred, axis=1, keepdims=True) + LN_EPS)
    hold[...] = (centred * inv_std * gain_ref[...] + beta_ref[...]).astype(BF)
    wide = x.shape[1] // n_fsdp
    for p, k in enumerate(key_order(n_fsdp)):
        at = pl.multiple_of((f_ref[0] ^ k) * wide, wide)
        out_ref[:, p * wide : (p + 1) * wide] = hold[:, pl.ds(at, wide)]
    dy_ref[...] = g_ref[...].astype(BF)


def norm(x, g, gain, beta, f, n_fsdp):
    rows, cols = x.shape
    step = min(rows, 128)
    tile = pl.BlockSpec((step, cols), lambda i, f_ref: (i, 0))
    line = pl.BlockSpec((1, cols), lambda i, f_ref: (0, 0))
    own = jax.ShapeDtypeStruct((rows, cols), BF)
    return pl.pallas_call(
        functools.partial(norm_kernel, n_fsdp),
        grid_spec=pltpu.PrefetchScalarGridSpec(
            num_scalar_prefetch=1,
            grid=(rows // step,),
            in_specs=[tile, tile, line, line],
            out_specs=[tile, tile],
            scratch_shapes=[pltpu.VMEM((step, cols), BF)],
        ),
        out_shape=[own, own],
        **big("norm", 0, 12 * rows * cols),
    )(f[None], x, g, gain[None], beta[None])


def turn(u, c, s_up, s_down):
    half_rot = ROT_DIM // 2
    wide = u.shape[1]
    return (
        u * c
        + pltpu.roll(u, half_rot, 1) * s_up
        + pltpu.roll(u, wide - half_rot, 1) * s_down
    )


def dot(a, b, ca, cb):
    return lax.dot_general(a, b, (((ca,), (cb,)), ((), ())), preferred_element_type=F32)


def causal(s):
    keys, size = s.shape
    key_at = lax.broadcasted_iota(jnp.int32, (size, size), 0)
    query_at = lax.broadcasted_iota(jnp.int32, (size, size), 1)
    own = jnp.where(key_at <= query_at, s[keys - size :], NEG_BIG)
    return own if keys == size else jnp.concatenate([s[: keys - size], own], axis=0)


def att_kernel(q_ref, k_ref, v_ref, c_ref, u_ref, d_ref, qb_ref, kb_ref, vb_ref, att_ref, lse_ref):
    seq = q_ref.shape[0]
    size = math.gcd(seq, 256)
    c, su, sd = c_ref[...], u_ref[...], d_ref[...]
    qb_ref[...] = turn(q_ref[...], c, su, sd).astype(BF)
    kb_ref[...] = turn(k_ref[...], c, su, sd).astype(BF)
    vb_ref[...] = v_ref[...].astype(BF)
    scale = jnp.asarray(1.0 / math.sqrt(HEAD_DIM), BF)
    for i in range(seq // size):
        rows = slice(i * size, (i + 1) * size)
        keys = (i + 1) * size
        outs = []
        for h in range(2):
            lanes = slice(h * HEAD_DIM, (h + 1) * HEAD_DIM)
            s = causal(dot(kb_ref[:keys, lanes], qb_ref[rows, lanes] * scale, 1, 1))
            top = jnp.max(s, axis=0, keepdims=True)
            e = jnp.exp(s - top)
            total = jnp.sum(e, axis=0, keepdims=True)
            lse_ref[0, h : h + 1, rows] = top + jnp.log(total)
            p = (e * (1.0 / total)).astype(BF)
            outs.append(dot(p, vb_ref[:keys, lanes], 0, 0))
        att_ref[rows, :] = jnp.concatenate(outs, axis=1).astype(BF)


def attention(project, tables, n_heads, cat_width):
    seq = project.shape[0]
    pairs = n_heads // 2
    wide = 2 * HEAD_DIM

    def col(base):
        return pl.BlockSpec((seq, wide), lambda p: (0, base + p))

    table = pl.BlockSpec((seq, wide), lambda p: (0, 0))
    own = jax.ShapeDtypeStruct((seq, n_heads * HEAD_DIM), BF)
    return pl.pallas_call(
        att_kernel,
        grid=(pairs,),
        in_specs=[col(0), col(pairs), col(2 * pairs), table, table, table],
        out_specs=[col(0)] * 4 + [pl.BlockSpec((1, 2, seq), lambda p: (p, 0, 0))],
        out_shape=[own] * 3
        + [
            jax.ShapeDtypeStruct((seq, cat_width), BF),
            jax.ShapeDtypeStruct((pairs, 2, seq), F32),
        ],
        **big("attention", n_heads * seq * seq * 256, seq * n_heads * 64 * 20),
    )(project, project, project, *tables)


def back_kernel(
    pairs, q_ref, k_ref, v_ref, att_ref, datt_ref, lse_ref, c_ref, u_ref, d_ref, dproj_in,
    dproj_ref, sq_ref, sk_ref, sv_ref, aq, ak, av, hold, sems,
):
    del dproj_in
    seq = q_ref.shape[0]
    size = math.gcd(seq, 256)
    scale = jnp.asarray(1.0 / math.sqrt(HEAD_DIM), BF)
    ak[...] = jnp.zeros_like(ak)
    av[...] = jnp.zeros_like(av)
    for i in range(seq // size):
        rows = slice(i * size, (i + 1) * size)
        keys = (i + 1) * size
        dqs, dks, dvs = [], [], []
        prod = datt_ref[rows, :].astype(F32) * att_ref[rows, :].astype(F32)
        prod_t = prod.T
        for h in range(2):
            lanes = slice(h * HEAD_DIM, (h + 1) * HEAD_DIM)
            q, do = q_ref[rows, lanes], datt_ref[rows, lanes]
            k, v = k_ref[:keys, lanes], v_ref[:keys, lanes]
            delta = jnp.sum(prod_t[lanes, :], axis=0, keepdims=True)
            q = q * scale
            s = causal(dot(k, q, 1, 1))
            p = jnp.exp(s - lse_ref[0, h : h + 1, rows])
            dp = dot(v, do, 1, 1)
            ds = (p * (dp - delta)).astype(BF)
            dvs.append(dot(p.astype(BF), do, 1, 0))
            dks.append(dot(ds, q, 1, 0))
            dqs.append(dot(k, ds, 0, 0).T * scale.astype(F32))
        av[:keys, :] += jnp.concatenate(dvs, axis=1)
        ak[:keys, :] += jnp.concatenate(dks, axis=1)
        aq[rows, :] = jnp.concatenate(dqs, axis=1)
    wide = q_ref.shape[1]
    copies = []
    for i, (acc, total) in enumerate(((aq, sq_ref), (ak, sk_ref), (av, sv_ref))):
        g = acc[...]
        if i < 2:
            g = turn(g, c_ref[...], -u_ref[...], -d_ref[...])
        hold[i] = g.astype(BF)
        total[...] = jnp.sum(g, axis=0, keepdims=True)
        at = pl.multiple_of((i * pairs + pl.program_id(0)) * wide, wide)
        copies.append(
            pltpu.make_async_copy(hold.at[i], dproj_ref.at[:, pl.ds(at, wide)], sems.at[i])
        )
        copies[-1].start()
    for copy in copies:
        copy.wait()


def attention_back(q, k, v, cat, d_att, lse, tables, d_proj, n_heads):
    seq = q.shape[0]
    pairs = n_heads // 2
    wide = 2 * HEAD_DIM
    col = pl.BlockSpec((seq, wide), lambda p: (0, p))
    table = pl.BlockSpec((seq, wide), lambda p: (0, 0))
    line = pl.BlockSpec((1, wide), lambda p: (0, p))
    return pl.pallas_call(
        functools.partial(back_kernel, pairs),
        grid=(pairs,),
        in_specs=[col] * 5
        + [pl.BlockSpec((1, 2, seq), lambda p: (p, 0, 0))]
        + [table] * 3
        + [HBM_SPEC],
        out_specs=[HBM_SPEC] + [line] * 3,
        out_shape=[jax.ShapeDtypeStruct(d_proj.shape, BF)]
        + [jax.ShapeDtypeStruct((1, n_heads * HEAD_DIM), F32)] * 3,
        input_output_aliases={9: 0},
        scratch_shapes=[pltpu.VMEM((seq, wide), F32)] * 3
        + [pltpu.VMEM((3, seq, wide), BF), pltpu.SemaphoreType.DMA((3,))],
        **big("attention_back", n_heads * seq * seq * 640, seq * n_heads * 64 * 16),
    )(q, k, v, cat, d_att, lse, *tables, d_proj)


def grads_kernel(n_split, n_late, f_ref, left_ref, right_ref, *refs):
    outs = refs[n_late:]
    g = dot(left_ref[...], right_ref[...], 0, 0).astype(BF)
    if len(outs) == 1:
        outs[0][...] = g
        return
    rows = g.shape[0] // n_split
    for s in range(n_split):
        key = lax.bitwise_xor(f_ref[0], s)
        at = pl.ds(pl.multiple_of(lax.shift_right_logical(key, 1) * rows, 16), rows)
        for i, out in enumerate(outs):

            @pl.when(lax.bitwise_and(key, 1) == 1 - i)
            def _():
                out[at, :] = g[s * rows : (s + 1) * rows]


def grads(left, block, wide, right, first, width, f, n_split=None, late=()):
    rows = left.shape[0]
    tile = math.gcd(512, math.gcd(width, first) if first else width)
    n_out = 2 if n_split else 1
    return pl.pallas_call(
        functools.partial(grads_kernel, n_split, len(late)),
        grid_spec=pltpu.PrefetchScalarGridSpec(
            num_scalar_prefetch=1,
            grid=(width // tile,),
            in_specs=[
                pl.BlockSpec((rows, wide), lambda i, f_ref: (0, block)),
                pl.BlockSpec((rows, tile), lambda i, f_ref: (0, first // tile + i)),
            ]
            + [pl.BlockSpec(memory_space=pl.ANY)] * len(late),
            out_specs=[pl.BlockSpec((wide // n_out, tile), lambda i, f_ref: (0, i))] * n_out,
        ),
        out_shape=[jax.ShapeDtypeStruct((wide // n_out, width), BF)] * n_out,
        **big("grads", 2 * rows * wide * width, 2 * rows * (wide + width) + 2 * wide * width),
    )(f[None], left, right, *late)


def chunks(rows):
    step = math.gcd(rows, 256)
    return [slice(at, at + step) for at in range(0, rows, step)]


def gelu_parts(u):
    c = math.sqrt(2.0 / math.pi)
    square = u * u
    half = 0.5 * jnp.tanh(u * (c + (c * 0.044715) * square)) + 0.5
    value = u * half
    slope = half + half * (1.0 - half) * (u * (2.0 * c + (6.0 * c * 0.044715) * square))
    return value, slope


def cost(flops, nbytes):
    return pl.CostEstimate(flops=flops, bytes_accessed=nbytes, transcendentals=0)


def big(name_of, flops, nbytes):
    return {
        "compiler_params": pltpu.CompilerParams(vmem_limit_bytes=VMEM_BYTES),
        "cost_estimate": cost(flops, nbytes),
        "name": name_of,
    }


def lay(parts, cuts, at_ref, base, dst):
    for c, (i, start, size) in enumerate(cuts):
        at = pl.multiple_of(at_ref[base + c], 16)
        dst[pl.ds(at, size), :] = parts[i][start : start + size, :]


def qkv_kernel(x_cuts, n_x, w_cuts, n_w, at_ref, *refs):
    xs, ws, b_ref = refs[:n_x], refs[n_x : n_x + n_w], refs[n_x + n_w]
    out_ref, x_ref, w_ref = refs[n_x + n_w + 1 :]

    @pl.when(pl.program_id(0) == 0)
    def _():
        lay(xs, x_cuts, at_ref, 0, x_ref)

    lay(ws, w_cuts, at_ref, len(x_cuts), w_ref)
    out_ref[...] = dot(x_ref[...], w_ref[...], 1, 0) + b_ref[...]


def qkv_project(xs, x_cuts, ws, w_cuts, places, b, rows, width, tile):
    deep, full = xs[0].shape[1], ws[0].shape[1]
    return pl.pallas_call(
        functools.partial(qkv_kernel, x_cuts, len(xs), w_cuts, len(ws)),
        grid_spec=pltpu.PrefetchScalarGridSpec(
            num_scalar_prefetch=1,
            grid=(width // tile,),
            in_specs=[pl.BlockSpec(x.shape, lambda i, at: (0, 0)) for x in xs]
            + [pl.BlockSpec((w.shape[0], tile), lambda i, at: (0, i)) for w in ws]
            + [pl.BlockSpec((1, tile), lambda i, at: (0, i))],
            out_specs=[
                pl.BlockSpec((rows, tile), lambda i, at: (0, i)),
                pl.BlockSpec((rows, deep), lambda i, at: (0, 0)),
                pl.BlockSpec((deep, tile), lambda i, at: (0, i)),
            ],
        ),
        out_shape=[
            jax.ShapeDtypeStruct((rows, width), F32),
            jax.ShapeDtypeStruct((rows, deep), BF),
            jax.ShapeDtypeStruct((deep, full), BF),
        ],
        **big("qkv_project", 2 * rows * deep * width, 2 * deep * (rows + width) + 4 * rows * width),
    )(places, *xs, *ws, b)


def pre_kernel(w_cuts, n_w, at_ref, x_ref, *refs):
    ws, b_ref = refs[:n_w], refs[n_w]
    pre_ref, cat_ref, w_ref = refs[-3:]
    lay(ws, w_cuts, at_ref, 0, w_ref)
    for rows in chunks(x_ref.shape[0]):
        pre = dot(x_ref[rows, :], w_ref[...], 1, 0) + b_ref[...]
        pre_ref[rows, :] = pre
        cat_ref[rows, :] = gelu_parts(pre)[0].astype(BF)


def pre_project(x, ws, w_cuts, places, b, cat, w_all, skip, tile):
    rows, deep = x.shape
    width = w_all.shape[1] - skip
    first, cat_first = skip // tile, (cat.shape[1] - width) // tile
    n_w = len(ws)
    return pl.pallas_call(
        functools.partial(pre_kernel, w_cuts, n_w),
        grid_spec=pltpu.PrefetchScalarGridSpec(
            num_scalar_prefetch=1,
            grid=(width // tile,),
            in_specs=[pl.BlockSpec((rows, deep), lambda i, at: (0, 0))]
            + [pl.BlockSpec((w.shape[0], tile), lambda i, at: (0, first + i)) for w in ws]
            + [pl.BlockSpec((1, tile), lambda i, at: (0, first + i))]
            + [pl.BlockSpec(memory_space=pl.ANY)] * 2,
            out_specs=[
                pl.BlockSpec((rows, tile), lambda i, at: (0, i)),
                pl.BlockSpec((rows, tile), lambda i, at: (0, cat_first + i)),
                pl.BlockSpec((deep, tile), lambda i, at: (0, first + i)),
            ],
        ),
        out_shape=[
            jax.ShapeDtypeStruct((rows, width), F32),
            jax.ShapeDtypeStruct(cat.shape, BF),
            jax.ShapeDtypeStruct(w_all.shape, BF),
        ],
        input_output_aliases={3 + n_w: 1, 4 + n_w: 2},
        **big("pre_project", 2 * rows * deep * width, 2 * deep * (rows + width) + 6 * rows * width),
    )(places, x, *ws, b, cat, w_all)


def by_rank(at_ref, x_ref, w, side, out, blk_size):
    for rows in chunks(x_ref.shape[0]):
        part = dot(x_ref[rows, :], w[...], 1, side).astype(out.dtype)
        for at in range(0, part.shape[0], blk_size):
            to = pl.multiple_of(at_ref[(rows.start + at) // blk_size], blk_size)
            out[pl.ds(to, blk_size), :] = part[at : at + blk_size]


def out_kernel(w_cuts, n_w, n_blk, blk_size, at_ref, x_ref, *refs):
    ws, out_ref, w_ref = refs[:n_w], refs[-2], refs[-1]
    lay(ws, w_cuts, at_ref, n_blk, w_ref)
    by_rank(at_ref, x_ref, w_ref, 0, out_ref, blk_size)


def out_project(x, ws, w_cuts, places, n_blk, blk_size):
    rows, deep = x.shape
    width = ws[0].shape[1]
    tile = min(512, width)
    return pl.pallas_call(
        functools.partial(out_kernel, w_cuts, len(ws), n_blk, blk_size),
        grid_spec=pltpu.PrefetchScalarGridSpec(
            num_scalar_prefetch=1,
            grid=(width // tile,),
            in_specs=[pl.BlockSpec((rows, deep), lambda i, at: (0, 0))]
            + [pl.BlockSpec((w.shape[0], tile), lambda i, at: (0, i)) for w in ws],
            out_specs=[
                pl.BlockSpec((rows, tile), lambda i, at: (0, i)),
                pl.BlockSpec((deep, tile), lambda i, at: (0, i)),
            ],
        ),
        out_shape=[
            jax.ShapeDtypeStruct((rows, width), BF),
            jax.ShapeDtypeStruct((deep, width), BF),
        ],
        **big("out_project", 2 * rows * deep * width, 2 * deep * (rows + width) + 3 * rows * width),
    )(places, x, *ws)


def norm_kernel_back(blk_size, at_ref, x_ref, w_ref, out_ref):
    by_rank(at_ref, x_ref, w_ref, 1, out_ref, blk_size)


def norm_back(x, w, places, blk_size):
    rows, deep = x.shape
    width = w.shape[0]
    tile = min(256, width)
    return pl.pallas_call(
        functools.partial(norm_kernel_back, blk_size),
        grid_spec=pltpu.PrefetchScalarGridSpec(
            num_scalar_prefetch=1,
            grid=(width // tile,),
            in_specs=[
                pl.BlockSpec((rows, deep), lambda i, at: (0, 0)),
                pl.BlockSpec((tile, deep), lambda i, at: (i, 0)),
            ],
            out_specs=pl.BlockSpec((rows, tile), lambda i, at: (0, i)),
        ),
        out_shape=jax.ShapeDtypeStruct((rows, width), BF),
        **big("norm_back", 2 * rows * deep * width, 2 * deep * (rows + width) + 3 * rows * width),
    )(places, x, w)


def d_cat_kernel(cuts, at_ref, g_ref, w_ref, pre_ref, datt_ref, dproj_ref, sum_ref, x_ref):
    @pl.when(pl.program_id(0) == 0)
    def _():
        lay([g_ref], cuts, at_ref, 0, x_ref)
        datt_ref[...] = dot(x_ref[...], w_ref[...], 1, 1).astype(BF)

    @pl.when(pl.program_id(0) > 0)
    def _():
        total = 0.0
        for rows in chunks(x_ref.shape[0]):
            d_pre = gelu_parts(pre_ref[rows, :])[1] * dot(x_ref[rows, :], w_ref[...], 1, 1)
            dproj_ref[rows, :] = d_pre.astype(BF)
            total = total + jnp.sum(d_pre, axis=0, keepdims=True)
        sum_ref[...] = total


def d_cat_parts(g, places, w, pre_act, wide_a):
    rows, deep = g.shape
    width = pre_act.shape[1]
    tile = wide_a
    total = 3 * wide_a + width
    blk = rows // places.shape[0]
    cuts = tuple((0, i * blk, blk) for i in range(places.shape[0]))

    def col(i):
        return jnp.maximum(i - 1, 0)

    return pl.pallas_call(
        functools.partial(d_cat_kernel, cuts),
        grid_spec=pltpu.PrefetchScalarGridSpec(
            num_scalar_prefetch=1,
            grid=(1 + width // tile,),
            in_specs=[
                pl.BlockSpec((rows, deep), lambda i, at: (0, 0)),
                pl.BlockSpec((tile, deep), lambda i, at: (i, 0)),
                pl.BlockSpec((rows, tile), lambda i, at: (0, col(i))),
            ],
            out_specs=[
                pl.BlockSpec((rows, tile), lambda i, at: (0, 0)),
                pl.BlockSpec((rows, tile), lambda i, at: (0, 3 + col(i))),
                pl.BlockSpec((1, tile), lambda i, at: (0, col(i))),
                pl.BlockSpec((rows, deep), lambda i, at: (0, 0)),
            ],
        ),
        out_shape=[
            jax.ShapeDtypeStruct((rows, tile), BF),
            jax.ShapeDtypeStruct((rows, total), BF),
            jax.ShapeDtypeStruct((1, width), F32),
            jax.ShapeDtypeStruct((rows, deep), BF),
        ],
        **big("d_cat_parts", 2 * rows * deep * (width + tile), 2 * deep * rows + (2 * deep + 6 * rows) * width),
    )(places, g, w, pre_act)


def join_kernel(n_parts, sizes, at_ref, *refs):
    dst = refs[-1]
    for j in range(n_parts):
        first = 0
        for i, size in enumerate(sizes):
            at = pl.multiple_of(at_ref[j * len(sizes) + i], 16)
            dst[pl.ds(at, size), :] = refs[j][first : first + size, :].astype(F32)
            first += size


def join_rows(parts, places, sizes):
    rows, width = parts[0].shape
    tile = min(512, width)
    return pl.pallas_call(
        functools.partial(join_kernel, len(parts), sizes),
        grid_spec=pltpu.PrefetchScalarGridSpec(
            num_scalar_prefetch=1,
            grid=(width // tile,),
            in_specs=[pl.BlockSpec((rows, tile), lambda i, at: (0, i))] * len(parts),
            out_specs=pl.BlockSpec((rows * len(parts), tile), lambda i, at: (0, i)),
        ),
        out_shape=jax.ShapeDtypeStruct((rows * len(parts), width), F32),
        **big("join_rows", 0, 6 * rows * len(parts) * width),
    )(places, *parts)


def after(x, *others):
    return lax.optimization_barrier((x, *others))[0]


def pass_on(x, hops):
    n = lax.axis_size("ctx")
    return lax.ppermute(x, "ctx", [(i, (i + hops) % n) for i in range(n)])


def reach(n):
    return n // 2, n - 1 - n // 2


def swap(x, axis, bit):
    n = lax.axis_size(axis)
    return lax.ppermute(x, axis, [(i, i ^ bit) for i in range(n)])


def near(x, bit):
    return swap(x, "fsdp", bit)


def far_keys(n):
    return sorted((k for k in range(2, n, 2)), key=lambda k: (k.bit_count(), k))


def top_bit(k):
    return 1 << (k.bit_length() - 1)


def low_bit(k):
    return k & -k


def halves(x):
    rows = x.shape[0] // 2
    return [x[:rows], x[rows:]]


class Line:
    def __init__(self):
        self.due = []

    def wait(self, *arrays):
        self.due += list(arrays)

    def tied(self, *xs):
        got = list(lax.optimization_barrier((*xs, *self.due)))[: len(xs)]
        self.due = got[:1]
        return got[0] if len(xs) == 1 else got


def ring_job(part, found):
    n = lax.axis_size("ctx")
    ups, downs = reach(n)
    found[0] = up = down = part
    for hop in range(1, ups + 1):
        if hop <= downs:
            up, down = yield [pass_on(up, 1), pass_on(down, -1)]
            found[n - hop] = down
        else:
            (up,) = yield [pass_on(up, 1)]
        found[hop] = up


def total_job(x, found):
    for axis in ("fsdp", "ctx"):
        bit = 1
        while bit < lax.axis_size(axis):
            (got,) = yield [swap(x, axis, bit)]
            x = x + got
            bit *= 2
    found.append(x)


def gather_job(shard, found):
    n = lax.axis_size("fsdp")
    have = {}
    keys = far_keys(n)
    fresh = [(0, None, shard)]
    found.extend(fresh)
    level = 0
    while True:
        level += 1
        send = []
        for k in keys:
            if k.bit_count() != level:
                continue
            if level == 1:
                send.append((k, None, near(shard, k)))
            else:
                for h, bit in ((0, top_bit(k)), (1, low_bit(k))):
                    send.append((k, h, near(have[k ^ bit, h], bit)))
        send += [(k | 1, h, near(x, 1)) for k, h, x in fresh if not k & 1]
        if not send:
            return
        got = yield [x for _, _, x in send]
        fresh = [(k, h, x) for (k, h, _), x in zip(send, got)]
        found.extend(fresh)
        for k, h, x in fresh:
            if not k & 1:
                if h is None:
                    have[k, 0], have[k, 1] = halves(x)
                else:
                    have[k, h] = x


def gather_order(n):
    got = [(0, None)]
    fresh = list(got)
    level = 0
    while True:
        level += 1
        new = []
        for k in far_keys(n):
            if k.bit_count() == level:
                new += [(k, None)] if level == 1 else [(k, 0), (k, 1)]
        new += [(k | 1, h) for k, h in fresh if not k & 1]
        if not new:
            return got
        got += new
        fresh = new


def scatter_job(away, home, found):
    n = lax.axis_size("fsdp")
    (got,) = yield [near(away, 1)]
    home = home() if callable(home) else home
    rows = home.shape[0] // (n // 2)
    hold = {}
    for i, k in enumerate(range(0, n, 2)):
        for h in range(2):
            at = i * rows + h * (rows // 2)
            cut = slice(at, at + rows // 2)
            hold[k, h] = home[cut].astype(F32) + got[cut].astype(F32)
    for level in range(n.bit_length() - 2, 0, -1):
        moves = []
        for k in far_keys(n):
            if k.bit_count() != level:
                continue
            if level > 1:
                for h, bit in ((0, top_bit(k)), (1, low_bit(k))):
                    moves.append((k ^ bit, h, near(hold[k, h].astype(BF), bit)))
            else:
                whole = jnp.concatenate([hold[k, 0], hold[k, 1]], axis=0).astype(BF)
                moves.append((0, None, near(whole, k)))
        got = yield [x for _, _, x in moves]
        for (k, h, _), x in zip(moves, got):
            if h is None:
                for i, part in enumerate(halves(x)):
                    hold[k, i] = hold[k, i] + part.astype(F32)
            else:
                hold[k, h] = hold[k, h] + x.astype(F32)
    found.append(jnp.concatenate([hold[0, 0], hold[0, 1]], axis=0).astype(BF))


class Move:
    def __init__(self, line, job):
        self.line, self.job, self.flight = line, job, next(job)

    def step(self, *more):
        moves = [m for m in (self, *more) if m.flight is not None]
        flights = [x for m in moves for x in m.flight]
        if not moves:
            return
        got = list(lax.optimization_barrier((*flights, *self.line.due)))[: len(flights)]
        self.line.due = list(got)
        for m in moves:
            own, got = got[: len(m.flight)], got[len(m.flight) :]
            try:
                m.flight = m.job.send(own)
            except StopIteration:
                m.flight = None

    def end(self, *more):
        while self.flight is not None:
            self.step(*more)


def gelu_tanh(values):
    return jax.nn.gelu(values, approximate=True)


def rotary_tables(positions):
    seq = positions.shape[0]
    half_rot = ROT_DIM // 2
    expon = jnp.arange(half_rot, dtype=F32) * (2.0 / ROT_DIM)
    freqs = ROPE_BASE ** (-expon)
    angles = positions.astype(F32)[:, None] * freqs[None, :]
    cosine, sine = jnp.cos(angles), jnp.sin(angles)
    zero = jnp.zeros_like(sine)
    rest = jnp.zeros((seq, HEAD_DIM - ROT_DIM), F32)
    c = jnp.concatenate([cosine, cosine, rest + 1.0], axis=1)
    up = jnp.concatenate([zero, sine, rest], axis=1)
    down = jnp.concatenate([-sine, zero, rest], axis=1)
    return tuple(jnp.concatenate([t, t], axis=1) for t in (c, up, down))


def shards(inputs, out_grad, block_order, ln_gain, ln_beta, w_in, b_in, w_out, b_out):
    n_ctx, n_fsdp = lax.axis_size("ctx"), lax.axis_size("fsdp")
    z, f = lax.axis_index("ctx"), lax.axis_index("fsdp")
    seq_in, seq_grad, blk_order = inputs[0], out_grad[0], block_order[0]
    tok_rows = seq_in.shape[0]
    seq_len = tok_rows * n_ctx
    n_blk = blk_order.shape[0]
    blk_size = seq_len // n_blk
    per = n_blk // n_ctx
    wide_d = D // n_fsdp
    shard = w_out.shape[0]
    cat_rows = shard * n_fsdp
    in_cols = w_in.shape[1]
    n_heads = HEADS // n_ctx
    wide_a, wide_m = D // n_ctx, (cat_rows - D) // n_ctx
    even, att_runs, act_runs = plan(n_fsdp, n_ctx, cat_rows)
    z_runs = [in_runs(att_runs[i], act_runs[i]) for i in range(n_ctx)]

    def position_of(k):
        return lax.shift_right_logical(k, 1) + lax.bitwise_and(k, 1) * (n_fsdp // 2)

    rank_places = blk_order * blk_size
    blocks_at = jnp.arange(n_blk, dtype=jnp.int32)
    slots = jnp.sum(
        (blk_order[None, :] == blocks_at[:, None]).astype(jnp.int32) * blocks_at[None, :],
        axis=1, dtype=jnp.int32,
    ) * blk_size
    ranks = lax.rem(z - jnp.arange(n_ctx, dtype=jnp.int32) + n_ctx, n_ctx)
    picks = (ranks[:, None] == jnp.arange(n_ctx, dtype=jnp.int32)[None, :]).astype(jnp.int32)
    row_places = jnp.sum(
        picks[:, :, None] * rank_places.reshape(1, n_ctx, per), axis=1, dtype=jnp.int32
    ).reshape(-1)

    line = Line()
    keys_at = {k: p for p, k in enumerate(key_order(n_fsdp))}
    share = shard // n_ctx
    mixed_f = [i for i in range(n_fsdp) if 0 < D - shard * i < shard]
    cut = (D - shard * mixed_f[0]) // n_ctx if mixed_f else share
    cut_m = share - cut
    is_mixed = (f == mixed_f[0]) if mixed_f else False

    def own_rows(whole):
        first = lax.dynamic_slice_in_dim(whole, z * share, share, 0)
        if not cut_m:
            return first
        both = jnp.concatenate(
            [
                lax.dynamic_slice_in_dim(whole, z * cut, cut, 0),
                lax.dynamic_slice_in_dim(whole, cut * n_ctx + z * cut_m, cut_m, 0),
            ],
            axis=0,
        )
        return jnp.where(is_mixed, both, first)

    def cuts_of(found):
        return [x for _, _, x in found], tuple((i, 0, x.shape[0]) for i, (_, _, x) in enumerate(found))

    order = gather_order(n_fsdp)
    w_at = jnp.asarray(
        [keys_at[k] * wide_d + (h or 0) * (wide_d // 2) for k, h in order], jnp.int32
    )
    o_keys = jnp.asarray([k for k, _ in order], jnp.int32)
    o_at = lax.bitwise_xor(f, o_keys) * share + jnp.asarray(
        [(h or 0) * (share // 2) for _, h in order], jnp.int32
    )
    qkv_at = jnp.concatenate([row_places, w_at])
    o_at = jnp.concatenate([slots, o_at if even else jnp.zeros((1,), jnp.int32)])

    normed_parts, w_in_parts, w_out_parts = {}, [], []
    normed_own, dy_own = norm(seq_in, seq_grad, ln_gain, ln_beta, f, n_fsdp)
    normed_ring = Move(line, ring_job(normed_own, normed_parts))
    line.wait(normed_own)
    w_in_own = pick_columns(line.tied(w_in), z, z_runs)
    w_in_move = Move(line, gather_job(w_in_own, w_in_parts))
    line.wait(w_in_own)
    tables = rotary_tables(line.tied(jnp.arange(seq_len, dtype=jnp.int32)))
    line.wait(*tables)
    b_in_z = jnp.stack([jnp.concatenate([b_in[s : s + n] for s, n in runs]) for runs in z_runs])[z]
    b_in_z = b_in_z[None]
    w_out_own = own_rows(line.tied(w_out)) if even else w_out
    line.wait(w_out_own, b_in_z, qkv_at, o_at, w_at, rank_places, slots)

    normed_ring.step()
    w_in_move.step()
    while normed_ring.flight is not None:
        normed_ring.step(w_in_move)
    dy_all = lax.all_gather(after(dy_own, *line.due), "ctx", axis=0, tiled=True)
    w_in_move.end()
    if even:
        w_out_move = Move(line, gather_job(line.tied(w_out_own), w_out_parts))

    wide_q = 3 * wide_a
    x_cuts = [(j, i * blk_size, blk_size) for j in range(n_ctx) for i in range(per)]
    w_arrays, w_cuts = cuts_of(w_in_parts)
    xs = [normed_parts[j] for j in range(n_ctx)]
    qkv, normed, w_in_all = qkv_project(
        [line.tied(xs[0])] + xs[1:], tuple(x_cuts), w_arrays, w_cuts, qkv_at,
        b_in_z, seq_len, wide_q, wide_a,
    )
    line.wait(qkv)
    q_b, k_b, v_b, cat_b, lse = attention(line.tied(qkv), tables, n_heads, cat_rows // n_ctx)
    line.wait(cat_b)
    if even:
        w_out_move.step()
    pre_act, cat_b, w_in_all = pre_project(
        line.tied(normed), w_arrays, w_cuts, w_at, b_in_z, cat_b, w_in_all, wide_q, wide_a
    )
    line.wait(cat_b)
    if even:
        w_out_move.end()
        o_arrays, o_cuts = cuts_of(w_out_parts)
    else:
        w_all = lax.all_gather(w_out, "fsdp", axis=0, tiled=True)
        w_all = jnp.concatenate(
            [
                lax.dynamic_slice_in_dim(w_all, z * wide_a, wide_a, 0),
                lax.dynamic_slice_in_dim(w_all, D + z * wide_m, wide_m, 0),
            ],
            axis=0,
        )
        o_arrays, o_cuts = [w_all], ((0, 0, cat_rows // n_ctx),)
    out_part, w_out_z = out_project(line.tied(cat_b), o_arrays, o_cuts, o_at, n_blk, blk_size)
    line.wait(out_part)

    def ctx_sum(x):
        return lax.psum_scatter(x, "ctx", scatter_dimension=0, tiled=True)

    out_sum = ctx_sum(out_part)

    line.wait(dy_all)
    d_att, d_proj, sum_pre, dy = d_cat_parts(
        line.tied(dy_all), rank_places, w_out_z, pre_act, wide_a
    )
    line.wait(d_att)
    d_proj, *sum_qkv = attention_back(
        q_b, k_b, v_b, cat_b, line.tied(d_att), lse, tables, d_proj, n_heads
    )
    line.wait(d_proj)
    norm_part = norm_back(line.tied(d_proj), w_in_all, slots, blk_size)
    line.wait(norm_part)
    norm_sum = ctx_sum(norm_part)

    half = D // 2
    out_own, pre_own, qkv_own = [], [], []
    out_parts, pre_parts, qkv_parts = {}, {}, {}
    away, home = grads(line.tied(cat_b), 0, cat_rows // n_ctx, dy, 0, D, f, n_fsdp)
    line.wait(away)
    out_scatter = Move(line, scatter_job(line.tied(away), home, out_own)) if even else None
    (pre_away,) = grads(line.tied(normed), 1, half, d_proj, wide_q, wide_m, f)
    line.wait(pre_away)
    if even:
        out_scatter.step()
    (pre_home,) = grads(line.tied(normed), 0, half, d_proj, wide_q, wide_m, f, late=(out_sum,))
    line.wait(pre_home)
    (qkv_away,) = grads(line.tied(normed), 1, half, d_proj, 0, wide_q, f)
    line.wait(qkv_away)
    if even:
        out_scatter.step()
    pre_scatter = Move(line, scatter_job(line.tied(pre_away), pre_home, pre_own))
    (qkv_home,) = grads(line.tied(normed), 0, half, d_proj, 0, wide_q, f)
    line.wait(qkv_home)
    if even:
        out_scatter.end()
        out_ring = Move(line, ring_job(line.tied(out_own[0]), out_parts))
    pre_scatter.step()
    qkv_scatter = Move(line, scatter_job(line.tied(qkv_away), qkv_home, qkv_own))
    pre_scatter.step()

    norm_sum = line.tied(norm_sum)

    seq_in_t = line.tied(seq_in)
    centred = seq_in_t - jnp.mean(seq_in_t, axis=1, keepdims=True)
    inv_std = lax.rsqrt(jnp.mean(centred * centred, axis=1, keepdims=True) + LN_EPS)
    x_hat = centred * inv_std
    d_norm = jnp.concatenate(
        [
            lax.dynamic_slice_in_dim(norm_sum.astype(F32), position_of(f ^ i) * wide_d, wide_d, 1)
            for i in range(n_fsdp)
        ],
        axis=1,
    )
    small = jnp.stack(
        [jnp.sum(seq_grad, axis=0), jnp.sum(d_norm * x_hat, axis=0), jnp.sum(d_norm, axis=0)]
    )
    gain_grad = d_norm * ln_gain
    d_input = seq_grad + inv_std * (
        gain_grad
        - jnp.mean(gain_grad, axis=1, keepdims=True)
        - x_hat * jnp.mean(gain_grad * x_hat, axis=1, keepdims=True)
    )
    out_y = seq_in + out_sum.astype(F32) + b_out

    g_b_in_z = jnp.concatenate([x[0] for x in (*sum_qkv, sum_pre)])
    masked = jnp.where(
        jnp.arange(n_ctx)[:, None] == z, g_b_in_z[None, :], jnp.zeros((), F32)
    )
    runs = sorted((s, n, i, at) for i in range(n_ctx) for s, n, at in run_offsets(z_runs[i]))
    vector = jnp.concatenate([small.reshape(-1)] + [masked[i, at : at + n] for _, n, i, at in runs])
    line.wait(d_input)

    pre_runs = [[(s - 3 * D, n) for s, n in runs if s >= 3 * D] for runs in z_runs]
    qkv_runs = [[(s, n) for s, n in runs if s < 3 * D] for runs in z_runs]
    if even:
        out_ring.step(pre_scatter, qkv_scatter)
    else:
        pre_scatter.step(qkv_scatter)
    pre_scatter.end()
    pre_ring = Move(line, ring_job(line.tied(pre_own[0]), pre_parts))
    vectors = []
    if even:
        out_ring.end(qkv_scatter)
    vector_move = Move(line, total_job(line.tied(vector), vectors))
    if even:
        at = []
        for j in range(n_ctx):
            rank = lax.rem(z - j + n_ctx, n_ctx)
            at.append(jnp.where(is_mixed, rank * cut, rank * share))
            if cut_m:
                at.append(jnp.where(is_mixed, cut * n_ctx + rank * cut_m, rank * share + cut))
        g_w_out = join_rows(
            [line.tied(out_parts[0])] + [out_parts[j] for j in range(1, n_ctx)],
            jnp.stack(at).astype(jnp.int32),
            (cut, cut_m) if cut_m else (cut,),
        )
        line.wait(g_w_out)
    else:
        blocks = jnp.concatenate([home, away], axis=0).reshape(n_fsdp, -1, D)
        g_out = jnp.concatenate(
            [lax.dynamic_index_in_dim(blocks, position_of(f ^ i), 0, False) for i in range(n_fsdp)]
        )
        spread = jnp.zeros((cat_rows, D), BF)
        spread = lax.dynamic_update_slice_in_dim(spread, g_out[:wide_a], z * wide_a, 0)
        spread = lax.dynamic_update_slice_in_dim(spread, g_out[wide_a:], D + z * wide_m, 0)
        g_w_out = lax.psum_scatter(spread.astype(F32), "fsdp", scatter_dimension=0, tiled=True)
        g_w_out = lax.psum(g_w_out, "ctx")
    pre_ring.step(qkv_scatter, vector_move)
    qkv_scatter.end()
    qkv_ring = Move(line, ring_job(line.tied(qkv_own[0]), qkv_parts))
    pre_ring.end(vector_move)
    vector_move.step()
    in_turn = range(n_ctx)
    g_w_in = spread_columns(
        None,
        [line.tied(pre_parts[0])] + [pre_parts[j] for j in in_turn[1:]],
        z, pre_runs, in_cols, 3 * D, in_cols - 3 * D,
    )
    line.wait(g_w_in)
    qkv_ring.step(vector_move)
    qkv_ring.end(vector_move)
    vector_move.end()
    g_w_in = spread_columns(
        g_w_in, [qkv_parts[j] for j in in_turn], z, qkv_runs, in_cols, 0, 3 * D
    )
    vector = vectors[0]
    small = vector[: 3 * D].reshape(3, D)
    g_b_in = vector[3 * D :]

    def own_part(vector):
        length_part = vector.shape[0] // n_fsdp
        return lax.dynamic_slice_in_dim(vector, f * length_part, length_part, 0)

    return (
        out_y[None],
        d_input[None],
        g_w_in,
        own_part(g_b_in),
        g_w_out,
        own_part(small[0]),
        own_part(small[1]),
        own_part(small[2]),
    )


def run_offsets(runs):
    at, found = 0, []
    for start, size in runs:
        found.append((start, size, at))
        at += size
    return found


def solution(mesh):
    placed = (
        P("fsdp", "ctx", None),
        P("fsdp", "ctx", None),
        P("fsdp", None),
        P(),
        P(),
        P("fsdp", None),
        P(),
        P("fsdp", None),
        P(),
    )
    return jax.shard_map(
        shards,
        mesh=mesh,
        in_specs=placed,
        out_specs=(
            P("fsdp", "ctx", None),
            P("fsdp", "ctx", None),
            P("fsdp", None),
            P("fsdp"),
            P("fsdp", None),
            P("fsdp"),
            P("fsdp"),
            P("fsdp"),
        ),
        check_vma=False,
    )
```

```python
import functools
import math

import jax
import jax.numpy as jnp
from jax import lax
from jax.experimental import pallas as pl
from jax.experimental.pallas import tpu as pltpu
from jax.sharding import PartitionSpec as P

D = 2048
HEADS = 32
HEAD_DIM = 64
ROT_DIM = 32

LN_EPS = 1e-05
NEG_BIG = -1e30
ROPE_BASE = 10000.0
BF = jnp.bfloat16
F32 = jnp.float32
VMEM_BYTES = 56 * 1024 * 1024
HBM_SPEC = pl.BlockSpec(memory_space=pltpu.HBM)


def plan(n_fsdp, n_ctx, cat_rows):
    shard = cat_rows // n_fsdp
    even = True
    att, act = [[] for _ in range(n_ctx)], [[] for _ in range(n_ctx)]
    for f in range(n_fsdp):
        a = min(max(D - shard * f, 0), shard)
        m = shard - a
        if a % (n_ctx * HEAD_DIM) or m % (n_ctx * 16):
            even = False
        for z in range(n_ctx):
            if a:
                att[z].append((shard * f + z * (a // n_ctx), a // n_ctx))
            if m:
                act[z].append((shard * f + a + z * (m // n_ctx), m // n_ctx))
    if not even:
        wide_a, wide_m = D // n_ctx, (cat_rows - D) // n_ctx
        att = [[(z * wide_a, wide_a)] for z in range(n_ctx)]
        act = [[(D + z * wide_m, wide_m)] for z in range(n_ctx)]
    return even, att, act


def in_runs(att, act):
    runs = [(part * D + s, n) for part in range(3) for s, n in att]
    return runs + [(2 * D + s, n) for s, n in act]


def key_order(n):
    return list(range(0, n, 2)) + list(range(1, n, 2))


def pick_kernel(all_runs, z_ref, src_ref, dst_ref):
    for z, runs in enumerate(all_runs):

        @pl.when(z_ref[0] == z)
        def _():
            at = 0
            for start, size in runs:
                dst_ref[:, at : at + size] = src_ref[:, start : start + size]
                at += size


def pick_columns(src, z, all_runs):
    rows, cols = src.shape
    width = sum(n for _, n in all_runs[0])
    step = min(rows, 128)
    return pl.pallas_call(
        functools.partial(pick_kernel, all_runs),
        grid_spec=pltpu.PrefetchScalarGridSpec(
            num_scalar_prefetch=1,
            grid=(rows // step,),
            in_specs=[pl.BlockSpec((step, cols), lambda i, z_ref: (i, 0))],
            out_specs=pl.BlockSpec((step, width), lambda i, z_ref: (i, 0)),
        ),
        out_shape=jax.ShapeDtypeStruct((rows, width), src.dtype),
        **big("pick_columns", 0, 2 * rows * (cols + width)),
    )(z[None], src)


def spread_kernel(all_runs, n_ctx, z_ref, *refs):
    srcs, dst_ref = refs[:n_ctx], refs[-1]
    for z in range(n_ctx):

        @pl.when(z_ref[0] == z)
        def _():
            for j, src_ref in enumerate(srcs):
                at = 0
                for start, size in all_runs[(z - j) % n_ctx]:
                    dst_ref[:, start : start + size] = src_ref[:, at : at + size].astype(F32)
                    at += size


def spread_columns(whole, parts, z, all_runs, cols, first, width_out):
    rows, width = parts[0].shape
    n_ctx = len(parts)
    step = min(rows, 128)
    fresh = whole is None
    return pl.pallas_call(
        functools.partial(spread_kernel, all_runs, n_ctx),
        grid_spec=pltpu.PrefetchScalarGridSpec(
            num_scalar_prefetch=1,
            grid=(rows // step,),
            in_specs=[pl.BlockSpec((step, width), lambda i, z_ref: (i, 0))] * n_ctx
            + [pl.BlockSpec(memory_space=pl.ANY)] * (not fresh),
            out_specs=pl.BlockSpec(
                (pl.Element(step), pl.Element(width_out)), lambda i, z_ref: (i * step, first)
            ),
        ),
        out_shape=jax.ShapeDtypeStruct((rows, cols), F32),
        input_output_aliases={} if fresh else {1 + n_ctx: 0},
        **big("spread_columns", 0, rows * width_out * 6),
    )(z[None], *parts, *([] if fresh else [whole]))


def norm_kernel(n_fsdp, f_ref, x_ref, g_ref, gain_ref, beta_ref, out_ref, dy_ref, hold):
    x = x_ref[...]
    centred = x - jnp.mean(x, axis=1, keepdims=True)
    inv_std = lax.rsqrt(jnp.mean(centred * centred, axis=1, keepdims=True) + LN_EPS)
    hold[...] = (centred * inv_std * gain_ref[...] + beta_ref[...]).astype(BF)
    wide = x.shape[1] // n_fsdp
    for p, k in enumerate(key_order(n_fsdp)):
        at = pl.multiple_of((f_ref[0] ^ k) * wide, wide)
        out_ref[:, p * wide : (p + 1) * wide] = hold[:, pl.ds(at, wide)]
    dy_ref[...] = g_ref[...].astype(BF)


def norm(x, g, gain, beta, f, n_fsdp):
    rows, cols = x.shape
    step = min(rows, 128)
    tile = pl.BlockSpec((step, cols), lambda i, f_ref: (i, 0))
    line = pl.BlockSpec((1, cols), lambda i, f_ref: (0, 0))
    own = jax.ShapeDtypeStruct((rows, cols), BF)
    return pl.pallas_call(
        functools.partial(norm_kernel, n_fsdp),
        grid_spec=pltpu.PrefetchScalarGridSpec(
            num_scalar_prefetch=1,
            grid=(rows // step,),
            in_specs=[tile, tile, line, line],
            out_specs=[tile, tile],
            scratch_shapes=[pltpu.VMEM((step, cols), BF)],
        ),
        out_shape=[own, own],
        **big("norm", 0, 12 * rows * cols),
    )(f[None], x, g, gain[None], beta[None])


def turn(u, c, s_up, s_down):
    half_rot = ROT_DIM // 2
    wide = u.shape[1]
    return (
        u * c
        + pltpu.roll(u, half_rot, 1) * s_up
        + pltpu.roll(u, wide - half_rot, 1) * s_down
    )


def dot(a, b, ca, cb):
    return lax.dot_general(a, b, (((ca,), (cb,)), ((), ())), preferred_element_type=F32)


def causal(s):
    keys, size = s.shape
    key_at = lax.broadcasted_iota(jnp.int32, (size, size), 0)
    query_at = lax.broadcasted_iota(jnp.int32, (size, size), 1)
    own = jnp.where(key_at <= query_at, s[keys - size :], NEG_BIG)
    return own if keys == size else jnp.concatenate([s[: keys - size], own], axis=0)


def att_kernel(q_ref, k_ref, v_ref, c_ref, u_ref, d_ref, qb_ref, kb_ref, vb_ref, att_ref, lse_ref):
    seq = q_ref.shape[0]
    size = math.gcd(seq, 256)
    c, su, sd = c_ref[...], u_ref[...], d_ref[...]
    qb_ref[...] = turn(q_ref[...], c, su, sd).astype(BF)
    kb_ref[...] = turn(k_ref[...], c, su, sd).astype(BF)
    vb_ref[...] = v_ref[...].astype(BF)
    scale = jnp.asarray(1.0 / math.sqrt(HEAD_DIM), BF)
    for i in range(seq // size):
        rows = slice(i * size, (i + 1) * size)
        keys = (i + 1) * size
        outs = []
        for h in range(2):
            lanes = slice(h * HEAD_DIM, (h + 1) * HEAD_DIM)
            s = causal(dot(kb_ref[:keys, lanes], qb_ref[rows, lanes] * scale, 1, 1))
            top = jnp.max(s, axis=0, keepdims=True)
            e = jnp.exp(s - top)
            total = jnp.sum(e, axis=0, keepdims=True)
            lse_ref[0, h : h + 1, rows] = top + jnp.log(total)
            p = (e * (1.0 / total)).astype(BF)
            outs.append(dot(p, vb_ref[:keys, lanes], 0, 0))
        att_ref[rows, :] = jnp.concatenate(outs, axis=1).astype(BF)


def attention(project, tables, n_heads, cat_width):
    seq = project.shape[0]
    pairs = n_heads // 2
    wide = 2 * HEAD_DIM

    def col(base):
        return pl.BlockSpec((seq, wide), lambda p: (0, base + p))

    table = pl.BlockSpec((seq, wide), lambda p: (0, 0))
    own = jax.ShapeDtypeStruct((seq, n_heads * HEAD_DIM), BF)
    return pl.pallas_call(
        att_kernel,
        grid=(pairs,),
        in_specs=[col(0), col(pairs), col(2 * pairs), table, table, table],
        out_specs=[col(0)] * 4 + [pl.BlockSpec((1, 2, seq), lambda p: (p, 0, 0))],
        out_shape=[own] * 3
        + [
            jax.ShapeDtypeStruct((seq, cat_width), BF),
            jax.ShapeDtypeStruct((pairs, 2, seq), F32),
        ],
        **big("attention", n_heads * seq * seq * 256, seq * n_heads * 64 * 20),
    )(project, project, project, *tables)


def back_kernel(
    pairs, q_ref, k_ref, v_ref, att_ref, datt_ref, lse_ref, c_ref, u_ref, d_ref, dproj_in,
    dproj_ref, sq_ref, sk_ref, sv_ref, aq, ak, av, hold, sems,
):
    del dproj_in
    seq = q_ref.shape[0]
    size = math.gcd(seq, 256)
    scale = jnp.asarray(1.0 / math.sqrt(HEAD_DIM), BF)
    ak[...] = jnp.zeros_like(ak)
    av[...] = jnp.zeros_like(av)
    for i in range(seq // size):
        rows = slice(i * size, (i + 1) * size)
        keys = (i + 1) * size
        dqs, dks, dvs = [], [], []
        prod = datt_ref[rows, :].astype(F32) * att_ref[rows, :].astype(F32)
        prod_t = prod.T
        for h in range(2):
            lanes = slice(h * HEAD_DIM, (h + 1) * HEAD_DIM)
            q, do = q_ref[rows, lanes], datt_ref[rows, lanes]
            k, v = k_ref[:keys, lanes], v_ref[:keys, lanes]
            delta = jnp.sum(prod_t[lanes, :], axis=0, keepdims=True)
            q = q * scale
            s = causal(dot(k, q, 1, 1))
            p = jnp.exp(s - lse_ref[0, h : h + 1, rows])
            dp = dot(v, do, 1, 1)
            ds = (p * (dp - delta)).astype(BF)
            dvs.append(dot(p.astype(BF), do, 1, 0))
            dks.append(dot(ds, q, 1, 0))
            dqs.append(dot(k, ds, 0, 0).T * scale.astype(F32))
        av[:keys, :] += jnp.concatenate(dvs, axis=1)
        ak[:keys, :] += jnp.concatenate(dks, axis=1)
        aq[rows, :] = jnp.concatenate(dqs, axis=1)
    wide = q_ref.shape[1]
    copies = []
    for i, (acc, total) in enumerate(((aq, sq_ref), (ak, sk_ref), (av, sv_ref))):
        g = acc[...]
        if i < 2:
            g = turn(g, c_ref[...], -u_ref[...], -d_ref[...])
        hold[i] = g.astype(BF)
        total[...] = jnp.sum(g, axis=0, keepdims=True)
        at = pl.multiple_of((i * pairs + pl.program_id(0)) * wide, wide)
        copies.append(
            pltpu.make_async_copy(hold.at[i], dproj_ref.at[:, pl.ds(at, wide)], sems.at[i])
        )
        copies[-1].start()
    for copy in copies:
        copy.wait()


def attention_back(q, k, v, cat, d_att, lse, tables, d_proj, n_heads):
    seq = q.shape[0]
    pairs = n_heads // 2
    wide = 2 * HEAD_DIM
    col = pl.BlockSpec((seq, wide), lambda p: (0, p))
    table = pl.BlockSpec((seq, wide), lambda p: (0, 0))
    line = pl.BlockSpec((1, wide), lambda p: (0, p))
    return pl.pallas_call(
        functools.partial(back_kernel, pairs),
        grid=(pairs,),
        in_specs=[col] * 5
        + [pl.BlockSpec((1, 2, seq), lambda p: (p, 0, 0))]
        + [table] * 3
        + [HBM_SPEC],
        out_specs=[HBM_SPEC] + [line] * 3,
        out_shape=[jax.ShapeDtypeStruct(d_proj.shape, BF)]
        + [jax.ShapeDtypeStruct((1, n_heads * HEAD_DIM), F32)] * 3,
        input_output_aliases={9: 0},
        scratch_shapes=[pltpu.VMEM((seq, wide), F32)] * 3
        + [pltpu.VMEM((3, seq, wide), BF), pltpu.SemaphoreType.DMA((3,))],
        **big("attention_back", n_heads * seq * seq * 640, seq * n_heads * 64 * 16),
    )(q, k, v, cat, d_att, lse, *tables, d_proj)


def grads_kernel(n_split, n_late, f_ref, left_ref, right_ref, *refs):
    outs = refs[n_late:]
    g = dot(left_ref[...], right_ref[...], 0, 0).astype(BF)
    if len(outs) == 1:
        outs[0][...] = g
        return
    rows = g.shape[0] // n_split
    for s in range(n_split):
        key = lax.bitwise_xor(f_ref[0], s)
        at = pl.ds(pl.multiple_of(lax.shift_right_logical(key, 1) * rows, 16), rows)
        for i, out in enumerate(outs):

            @pl.when(lax.bitwise_and(key, 1) == 1 - i)
            def _():
                out[at, :] = g[s * rows : (s + 1) * rows]


def grads(left, block, wide, right, first, width, f, n_split=None, late=()):
    rows = left.shape[0]
    tile = math.gcd(512, math.gcd(width, first) if first else width)
    n_out = 2 if n_split else 1
    return pl.pallas_call(
        functools.partial(grads_kernel, n_split, len(late)),
        grid_spec=pltpu.PrefetchScalarGridSpec(
            num_scalar_prefetch=1,
            grid=(width // tile,),
            in_specs=[
                pl.BlockSpec((rows, wide), lambda i, f_ref: (0, block)),
                pl.BlockSpec((rows, tile), lambda i, f_ref: (0, first // tile + i)),
            ]
            + [pl.BlockSpec(memory_space=pl.ANY)] * len(late),
            out_specs=[pl.BlockSpec((wide // n_out, tile), lambda i, f_ref: (0, i))] * n_out,
        ),
        out_shape=[jax.ShapeDtypeStruct((wide // n_out, width), BF)] * n_out,
        **big("grads", 2 * rows * wide * width, 2 * rows * (wide + width) + 2 * wide * width),
    )(f[None], left, right, *late)


def chunks(rows):
    step = math.gcd(rows, 256)
    return [slice(at, at + step) for at in range(0, rows, step)]


def gelu_parts(u):
    c = math.sqrt(2.0 / math.pi)
    square = u * u
    half = 0.5 * jnp.tanh(u * (c + (c * 0.044715) * square)) + 0.5
    value = u * half
    slope = half + half * (1.0 - half) * (u * (2.0 * c + (6.0 * c * 0.044715) * square))
    return value, slope


def cost(flops, nbytes):
    return pl.CostEstimate(flops=flops, bytes_accessed=nbytes, transcendentals=0)


def big(name_of, flops, nbytes):
    return {
        "compiler_params": pltpu.CompilerParams(vmem_limit_bytes=VMEM_BYTES),
        "cost_estimate": cost(flops, nbytes),
        "name": name_of,
    }


def lay(parts, cuts, at_ref, base, dst):
    for c, (i, start, size) in enumerate(cuts):
        at = pl.multiple_of(at_ref[base + c], 16)
        dst[pl.ds(at, size), :] = parts[i][start : start + size, :]


def qkv_kernel(x_cuts, n_x, w_cuts, n_w, at_ref, *refs):
    xs, ws, b_ref = refs[:n_x], refs[n_x : n_x + n_w], refs[n_x + n_w]
    out_ref, x_ref, w_ref = refs[n_x + n_w + 1 :]

    @pl.when(pl.program_id(0) == 0)
    def _():
        lay(xs, x_cuts, at_ref, 0, x_ref)

    lay(ws, w_cuts, at_ref, len(x_cuts), w_ref)
    out_ref[...] = dot(x_ref[...], w_ref[...], 1, 0) + b_ref[...]


def qkv_project(xs, x_cuts, ws, w_cuts, places, b, rows, width, tile):
    deep, full = xs[0].shape[1], ws[0].shape[1]
    return pl.pallas_call(
        functools.partial(qkv_kernel, x_cuts, len(xs), w_cuts, len(ws)),
        grid_spec=pltpu.PrefetchScalarGridSpec(
            num_scalar_prefetch=1,
            grid=(width // tile,),
            in_specs=[pl.BlockSpec(x.shape, lambda i, at: (0, 0)) for x in xs]
            + [pl.BlockSpec((w.shape[0], tile), lambda i, at: (0, i)) for w in ws]
            + [pl.BlockSpec((1, tile), lambda i, at: (0, i))],
            out_specs=[
                pl.BlockSpec((rows, tile), lambda i, at: (0, i)),
                pl.BlockSpec((rows, deep), lambda i, at: (0, 0)),
                pl.BlockSpec((deep, tile), lambda i, at: (0, i)),
            ],
        ),
        out_shape=[
            jax.ShapeDtypeStruct((rows, width), F32),
            jax.ShapeDtypeStruct((rows, deep), BF),
            jax.ShapeDtypeStruct((deep, full), BF),
        ],
        **big("qkv_project", 2 * rows * deep * width, 2 * deep * (rows + width) + 4 * rows * width),
    )(places, *xs, *ws, b)


def pre_kernel(w_cuts, n_w, at_ref, x_ref, *refs):
    ws, b_ref = refs[:n_w], refs[n_w]
    pre_ref, cat_ref, w_ref = refs[-3:]
    lay(ws, w_cuts, at_ref, 0, w_ref)
    for rows in chunks(x_ref.shape[0]):
        pre = dot(x_ref[rows, :], w_ref[...], 1, 0) + b_ref[...]
        pre_ref[rows, :] = pre
        cat_ref[rows, :] = gelu_parts(pre)[0].astype(BF)


def pre_project(x, ws, w_cuts, places, b, cat, w_all, skip, tile):
    rows, deep = x.shape
    width = w_all.shape[1] - skip
    first, cat_first = skip // tile, (cat.shape[1] - width) // tile
    n_w = len(ws)
    return pl.pallas_call(
        functools.partial(pre_kernel, w_cuts, n_w),
        grid_spec=pltpu.PrefetchScalarGridSpec(
            num_scalar_prefetch=1,
            grid=(width // tile,),
            in_specs=[pl.BlockSpec((rows, deep), lambda i, at: (0, 0))]
            + [pl.BlockSpec((w.shape[0], tile), lambda i, at: (0, first + i)) for w in ws]
            + [pl.BlockSpec((1, tile), lambda i, at: (0, first + i))]
            + [pl.BlockSpec(memory_space=pl.ANY)] * 2,
            out_specs=[
                pl.BlockSpec((rows, tile), lambda i, at: (0, i)),
                pl.BlockSpec((rows, tile), lambda i, at: (0, cat_first + i)),
                pl.BlockSpec((deep, tile), lambda i, at: (0, first + i)),
            ],
        ),
        out_shape=[
            jax.ShapeDtypeStruct((rows, width), F32),
            jax.ShapeDtypeStruct(cat.shape, BF),
            jax.ShapeDtypeStruct(w_all.shape, BF),
        ],
        input_output_aliases={3 + n_w: 1, 4 + n_w: 2},
        **big("pre_project", 2 * rows * deep * width, 2 * deep * (rows + width) + 6 * rows * width),
    )(places, x, *ws, b, cat, w_all)


def by_rank(at_ref, x_ref, w, side, out, blk_size):
    for rows in chunks(x_ref.shape[0]):
        part = dot(x_ref[rows, :], w[...], 1, side).astype(out.dtype)
        for at in range(0, part.shape[0], blk_size):
            to = pl.multiple_of(at_ref[(rows.start + at) // blk_size], blk_size)
            out[pl.ds(to, blk_size), :] = part[at : at + blk_size]


def out_kernel(w_cuts, n_w, n_blk, blk_size, at_ref, x_ref, *refs):
    ws, out_ref, w_ref = refs[:n_w], refs[-2], refs[-1]
    lay(ws, w_cuts, at_ref, n_blk, w_ref)
    by_rank(at_ref, x_ref, w_ref, 0, out_ref, blk_size)


def out_project(x, ws, w_cuts, places, n_blk, blk_size):
    rows, deep = x.shape
    width = ws[0].shape[1]
    tile = min(512, width)
    return pl.pallas_call(
        functools.partial(out_kernel, w_cuts, len(ws), n_blk, blk_size),
        grid_spec=pltpu.PrefetchScalarGridSpec(
            num_scalar_prefetch=1,
            grid=(width // tile,),
            in_specs=[pl.BlockSpec((rows, deep), lambda i, at: (0, 0))]
            + [pl.BlockSpec((w.shape[0], tile), lambda i, at: (0, i)) for w in ws],
            out_specs=[
                pl.BlockSpec((rows, tile), lambda i, at: (0, i)),
                pl.BlockSpec((deep, tile), lambda i, at: (0, i)),
            ],
        ),
        out_shape=[
            jax.ShapeDtypeStruct((rows, width), BF),
            jax.ShapeDtypeStruct((deep, width), BF),
        ],
        **big("out_project", 2 * rows * deep * width, 2 * deep * (rows + width) + 3 * rows * width),
    )(places, x, *ws)


def norm_kernel_back(blk_size, at_ref, x_ref, w_ref, out_ref):
    by_rank(at_ref, x_ref, w_ref, 1, out_ref, blk_size)


def norm_back(x, w, places, blk_size):
    rows, deep = x.shape
    width = w.shape[0]
    tile = min(256, width)
    return pl.pallas_call(
        functools.partial(norm_kernel_back, blk_size),
        grid_spec=pltpu.PrefetchScalarGridSpec(
            num_scalar_prefetch=1,
            grid=(width // tile,),
            in_specs=[
                pl.BlockSpec((rows, deep), lambda i, at: (0, 0)),
                pl.BlockSpec((tile, deep), lambda i, at: (i, 0)),
            ],
            out_specs=pl.BlockSpec((rows, tile), lambda i, at: (0, i)),
        ),
        out_shape=jax.ShapeDtypeStruct((rows, width), BF),
        **big("norm_back", 2 * rows * deep * width, 2 * deep * (rows + width) + 3 * rows * width),
    )(places, x, w)


def d_cat_kernel(cuts, at_ref, g_ref, w_ref, pre_ref, datt_ref, dproj_ref, sum_ref, x_ref):
    @pl.when(pl.program_id(0) == 0)
    def _():
        lay([g_ref], cuts, at_ref, 0, x_ref)
        datt_ref[...] = dot(x_ref[...], w_ref[...], 1, 1).astype(BF)

    @pl.when(pl.program_id(0) > 0)
    def _():
        total = 0.0
        for rows in chunks(x_ref.shape[0]):
            d_pre = gelu_parts(pre_ref[rows, :])[1] * dot(x_ref[rows, :], w_ref[...], 1, 1)
            dproj_ref[rows, :] = d_pre.astype(BF)
            total = total + jnp.sum(d_pre, axis=0, keepdims=True)
        sum_ref[...] = total


def d_cat_parts(g, places, w, pre_act, wide_a):
    rows, deep = g.shape
    width = pre_act.shape[1]
    tile = wide_a
    total = 3 * wide_a + width
    blk = rows // places.shape[0]
    cuts = tuple((0, i * blk, blk) for i in range(places.shape[0]))

    def col(i):
        return jnp.maximum(i - 1, 0)

    return pl.pallas_call(
        functools.partial(d_cat_kernel, cuts),
        grid_spec=pltpu.PrefetchScalarGridSpec(
            num_scalar_prefetch=1,
            grid=(1 + width // tile,),
            in_specs=[
                pl.BlockSpec((rows, deep), lambda i, at: (0, 0)),
                pl.BlockSpec((tile, deep), lambda i, at: (i, 0)),
                pl.BlockSpec((rows, tile), lambda i, at: (0, col(i))),
            ],
            out_specs=[
                pl.BlockSpec((rows, tile), lambda i, at: (0, 0)),
                pl.BlockSpec((rows, tile), lambda i, at: (0, 3 + col(i))),
                pl.BlockSpec((1, tile), lambda i, at: (0, col(i))),
                pl.BlockSpec((rows, deep), lambda i, at: (0, 0)),
            ],
        ),
        out_shape=[
            jax.ShapeDtypeStruct((rows, tile), BF),
            jax.ShapeDtypeStruct((rows, total), BF),
            jax.ShapeDtypeStruct((1, width), F32),
            jax.ShapeDtypeStruct((rows, deep), BF),
        ],
        **big("d_cat_parts", 2 * rows * deep * (width + tile), 2 * deep * rows + (2 * deep + 6 * rows) * width),
    )(places, g, w, pre_act)


def join_kernel(n_parts, sizes, at_ref, *refs):
    dst = refs[-1]
    for j in range(n_parts):
        first = 0
        for i, size in enumerate(sizes):
            at = pl.multiple_of(at_ref[j * len(sizes) + i], 16)
            dst[pl.ds(at, size), :] = refs[j][first : first + size, :].astype(F32)
            first += size


def join_rows(parts, places, sizes):
    rows, width = parts[0].shape
    tile = min(512, width)
    return pl.pallas_call(
        functools.partial(join_kernel, len(parts), sizes),
        grid_spec=pltpu.PrefetchScalarGridSpec(
            num_scalar_prefetch=1,
            grid=(width // tile,),
            in_specs=[pl.BlockSpec((rows, tile), lambda i, at: (0, i))] * len(parts),
            out_specs=pl.BlockSpec((rows * len(parts), tile), lambda i, at: (0, i)),
        ),
        out_shape=jax.ShapeDtypeStruct((rows * len(parts), width), F32),
        **big("join_rows", 0, 6 * rows * len(parts) * width),
    )(places, *parts)


def after(x, *others):
    return lax.optimization_barrier((x, *others))[0]


def pass_on(x, hops):
    n = lax.axis_size("ctx")
    return lax.ppermute(x, "ctx", [(i, (i + hops) % n) for i in range(n)])


def reach(n):
    return n // 2, n - 1 - n // 2


def swap(x, axis, bit):
    n = lax.axis_size(axis)
    return lax.ppermute(x, axis, [(i, i ^ bit) for i in range(n)])


def near(x, bit):
    return swap(x, "fsdp", bit)


def far_keys(n):
    return sorted((k for k in range(2, n, 2)), key=lambda k: (k.bit_count(), k))


def top_bit(k):
    return 1 << (k.bit_length() - 1)


def low_bit(k):
    return k & -k


def halves(x):
    rows = x.shape[0] // 2
    return [x[:rows], x[rows:]]


class Line:
    def __init__(self):
        self.due = []

    def wait(self, *arrays):
        self.due += list(arrays)

    def tied(self, *xs):
        got = list(lax.optimization_barrier((*xs, *self.due)))[: len(xs)]
        self.due = got[:1]
        return got[0] if len(xs) == 1 else got


def ring_job(part, found):
    n = lax.axis_size("ctx")
    ups, downs = reach(n)
    found[0] = up = down = part
    for hop in range(1, ups + 1):
        if hop <= downs:
            up, down = yield [pass_on(up, 1), pass_on(down, -1)]
            found[n - hop] = down
        else:
            (up,) = yield [pass_on(up, 1)]
        found[hop] = up


def total_job(x, found):
    for axis in ("fsdp", "ctx"):
        bit = 1
        while bit < lax.axis_size(axis):
            (got,) = yield [swap(x, axis, bit)]
            x = x + got
            bit *= 2
    found.append(x)


def gather_job(shard, found):
    n = lax.axis_size("fsdp")
    have = {}
    keys = far_keys(n)
    fresh = [(0, None, shard)]
    found.extend(fresh)
    level = 0
    while True:
        level += 1
        send = []
        for k in keys:
            if k.bit_count() != level:
                continue
            if level == 1:
                send.append((k, None, near(shard, k)))
            else:
                for h, bit in ((0, top_bit(k)), (1, low_bit(k))):
                    send.append((k, h, near(have[k ^ bit, h], bit)))
        send += [(k | 1, h, near(x, 1)) for k, h, x in fresh if not k & 1]
        if not send:
            return
        got = yield [x for _, _, x in send]
        fresh = [(k, h, x) for (k, h, _), x in zip(send, got)]
        found.extend(fresh)
        for k, h, x in fresh:
            if not k & 1:
                if h is None:
                    have[k, 0], have[k, 1] = halves(x)
                else:
                    have[k, h] = x


def gather_order(n):
    got = [(0, None)]
    fresh = list(got)
    level = 0
    while True:
        level += 1
        new = []
        for k in far_keys(n):
            if k.bit_count() == level:
                new += [(k, None)] if level == 1 else [(k, 0), (k, 1)]
        new += [(k | 1, h) for k, h in fresh if not k & 1]
        if not new:
            return got
        got += new
        fresh = new


def scatter_job(away, home, found):
    n = lax.axis_size("fsdp")
    (got,) = yield [near(away, 1)]
    home = home() if callable(home) else home
    rows = home.shape[0] // (n // 2)
    hold = {}
    for i, k in enumerate(range(0, n, 2)):
        for h in range(2):
            at = i * rows + h * (rows // 2)
            cut = slice(at, at + rows // 2)
            hold[k, h] = home[cut].astype(F32) + got[cut].astype(F32)
    for level in range(n.bit_length() - 2, 0, -1):
        moves = []
        for k in far_keys(n):
            if k.bit_count() != level:
                continue
            if level > 1:
                for h, bit in ((0, top_bit(k)), (1, low_bit(k))):
                    moves.append((k ^ bit, h, near(hold[k, h].astype(BF), bit)))
            else:
                whole = jnp.concatenate([hold[k, 0], hold[k, 1]], axis=0).astype(BF)
                moves.append((0, None, near(whole, k)))
        got = yield [x for _, _, x in moves]
        for (k, h, _), x in zip(moves, got):
            if h is None:
                for i, part in enumerate(halves(x)):
                    hold[k, i] = hold[k, i] + part.astype(F32)
            else:
                hold[k, h] = hold[k, h] + x.astype(F32)
    found.append(jnp.concatenate([hold[0, 0], hold[0, 1]], axis=0).astype(BF))


class Move:
    def __init__(self, line, job):
        self.line, self.job, self.flight = line, job, next(job)

    def step(self, *more):
        moves = [m for m in (self, *more) if m.flight is not None]
        flights = [x for m in moves for x in m.flight]
        if not moves:
            return
        got = list(lax.optimization_barrier((*flights, *self.line.due)))[: len(flights)]
        self.line.due = list(got)
        for m in moves:
            own, got = got[: len(m.flight)], got[len(m.flight) :]
            try:
                m.flight = m.job.send(own)
            except StopIteration:
                m.flight = None

    def end(self, *more):
        while self.flight is not None:
            self.step(*more)


def gelu_tanh(values):
    return jax.nn.gelu(values, approximate=True)


def rotary_tables(positions):
    seq = positions.shape[0]
    half_rot = ROT_DIM // 2
    expon = jnp.arange(half_rot, dtype=F32) * (2.0 / ROT_DIM)
    freqs = ROPE_BASE ** (-expon)
    angles = positions.astype(F32)[:, None] * freqs[None, :]
    cosine, sine = jnp.cos(angles), jnp.sin(angles)
    zero = jnp.zeros_like(sine)
    rest = jnp.zeros((seq, HEAD_DIM - ROT_DIM), F32)
    c = jnp.concatenate([cosine, cosine, rest + 1.0], axis=1)
    up = jnp.concatenate([zero, sine, rest], axis=1)
    down = jnp.concatenate([-sine, zero, rest], axis=1)
    return tuple(jnp.concatenate([t, t], axis=1) for t in (c, up, down))


def shards(inputs, out_grad, block_order, ln_gain, ln_beta, w_in, b_in, w_out, b_out):
    n_ctx, n_fsdp = lax.axis_size("ctx"), lax.axis_size("fsdp")
    z, f = lax.axis_index("ctx"), lax.axis_index("fsdp")
    seq_in, seq_grad, blk_order = inputs[0], out_grad[0], block_order[0]
    tok_rows = seq_in.shape[0]
    seq_len = tok_rows * n_ctx
    n_blk = blk_order.shape[0]
    blk_size = seq_len // n_blk
    per = n_blk // n_ctx
    wide_d = D // n_fsdp
    shard = w_out.shape[0]
    cat_rows = shard * n_fsdp
    in_cols = w_in.shape[1]
    n_heads = HEADS // n_ctx
    wide_a, wide_m = D // n_ctx, (cat_rows - D) // n_ctx
    even, att_runs, act_runs = plan(n_fsdp, n_ctx, cat_rows)
    z_runs = [in_runs(att_runs[i], act_runs[i]) for i in range(n_ctx)]

    def position_of(k):
        return lax.shift_right_logical(k, 1) + lax.bitwise_and(k, 1) * (n_fsdp // 2)

    rank_places = blk_order * blk_size
    blocks_at = jnp.arange(n_blk, dtype=jnp.int32)
    slots = jnp.sum(
        (blk_order[None, :] == blocks_at[:, None]).astype(jnp.int32) * blocks_at[None, :],
        axis=1, dtype=jnp.int32,
    ) * blk_size
    ranks = lax.rem(z - jnp.arange(n_ctx, dtype=jnp.int32) + n_ctx, n_ctx)
    picks = (ranks[:, None] == jnp.arange(n_ctx, dtype=jnp.int32)[None, :]).astype(jnp.int32)
    row_places = jnp.sum(
        picks[:, :, None] * rank_places.reshape(1, n_ctx, per), axis=1, dtype=jnp.int32
    ).reshape(-1)

    line = Line()
    keys_at = {k: p for p, k in enumerate(key_order(n_fsdp))}
    share = shard // n_ctx
    mixed_f = [i for i in range(n_fsdp) if 0 < D - shard * i < shard]
    cut = (D - shard * mixed_f[0]) // n_ctx if mixed_f else share
    cut_m = share - cut
    is_mixed = (f == mixed_f[0]) if mixed_f else False

    def own_rows(whole):
        first = lax.dynamic_slice_in_dim(whole, z * share, share, 0)
        if not cut_m:
            return first
        both = jnp.concatenate(
            [
                lax.dynamic_slice_in_dim(whole, z * cut, cut, 0),
                lax.dynamic_slice_in_dim(whole, cut * n_ctx + z * cut_m, cut_m, 0),
            ],
            axis=0,
        )
        return jnp.where(is_mixed, both, first)

    def cuts_of(found):
        return [x for _, _, x in found], tuple((i, 0, x.shape[0]) for i, (_, _, x) in enumerate(found))

    order = gather_order(n_fsdp)
    w_at = jnp.asarray(
        [keys_at[k] * wide_d + (h or 0) * (wide_d // 2) for k, h in order], jnp.int32
    )
    o_keys = jnp.asarray([k for k, _ in order], jnp.int32)
    o_at = lax.bitwise_xor(f, o_keys) * share + jnp.asarray(
        [(h or 0) * (share // 2) for _, h in order], jnp.int32
    )
    qkv_at = jnp.concatenate([row_places, w_at])
    o_at = jnp.concatenate([slots, o_at if even else jnp.zeros((1,), jnp.int32)])

    normed_parts, w_in_parts, w_out_parts = {}, [], []
    normed_own, dy_own = norm(seq_in, seq_grad, ln_gain, ln_beta, f, n_fsdp)
    normed_ring = Move(line, ring_job(normed_own, normed_parts))
    line.wait(normed_own)
    w_in_own = pick_columns(line.tied(w_in), z, z_runs)
    w_in_move = Move(line, gather_job(w_in_own, w_in_parts))
    line.wait(w_in_own)
    tables = rotary_tables(line.tied(jnp.arange(seq_len, dtype=jnp.int32)))
    line.wait(*tables)
    b_in_z = jnp.stack([jnp.concatenate([b_in[s : s + n] for s, n in runs]) for runs in z_runs])[z]
    b_in_z = b_in_z[None]
    w_out_own = own_rows(line.tied(w_out)) if even else w_out
    line.wait(w_out_own, b_in_z, qkv_at, o_at, w_at, rank_places, slots)

    normed_ring.step()
    w_in_move.step()
    while normed_ring.flight is not None:
        normed_ring.step(w_in_move)
    dy_all = lax.all_gather(after(dy_own, *line.due), "ctx", axis=0, tiled=True)
    w_in_move.end()
    if even:
        w_out_move = Move(line, gather_job(line.tied(w_out_own), w_out_parts))

    wide_q = 3 * wide_a
    x_cuts = [(j, i * blk_size, blk_size) for j in range(n_ctx) for i in range(per)]
    w_arrays, w_cuts = cuts_of(w_in_parts)
    xs = [normed_parts[j] for j in range(n_ctx)]
    qkv, normed, w_in_all = qkv_project(
        [line.tied(xs[0])] + xs[1:], tuple(x_cuts), w_arrays, w_cuts, qkv_at,
        b_in_z, seq_len, wide_q, wide_a,
    )
    line.wait(qkv)
    q_b, k_b, v_b, cat_b, lse = attention(line.tied(qkv), tables, n_heads, cat_rows // n_ctx)
    line.wait(cat_b)
    if even:
        w_out_move.step()
    pre_act, cat_b, w_in_all = pre_project(
        line.tied(normed), w_arrays, w_cuts, w_at, b_in_z, cat_b, w_in_all, wide_q, wide_a
    )
    line.wait(cat_b)
    if even:
        w_out_move.end()
        o_arrays, o_cuts = cuts_of(w_out_parts)
    else:
        w_all = lax.all_gather(w_out, "fsdp", axis=0, tiled=True)
        w_all = jnp.concatenate(
            [
                lax.dynamic_slice_in_dim(w_all, z * wide_a, wide_a, 0),
                lax.dynamic_slice_in_dim(w_all, D + z * wide_m, wide_m, 0),
            ],
            axis=0,
        )
        o_arrays, o_cuts = [w_all], ((0, 0, cat_rows // n_ctx),)
    out_part, w_out_z = out_project(line.tied(cat_b), o_arrays, o_cuts, o_at, n_blk, blk_size)
    line.wait(out_part)

    def ctx_sum(x):
        return lax.psum_scatter(x, "ctx", scatter_dimension=0, tiled=True)

    out_sum = ctx_sum(out_part)

    line.wait(dy_all)
    d_att, d_proj, sum_pre, dy = d_cat_parts(
        line.tied(dy_all), rank_places, w_out_z, pre_act, wide_a
    )
    line.wait(d_att)
    d_proj, *sum_qkv = attention_back(
        q_b, k_b, v_b, cat_b, line.tied(d_att), lse, tables, d_proj, n_heads
    )
    line.wait(d_proj)
    half = D // 2
    out_own, pre_own, qkv_own = [], [], []
    out_parts, pre_parts, qkv_parts = {}, {}, {}
    away, home = grads(line.tied(cat_b), 0, cat_rows // n_ctx, dy, 0, D, f, n_fsdp)
    line.wait(away)
    out_scatter = Move(line, scatter_job(line.tied(away), home, out_own)) if even else None
    norm_part = norm_back(line.tied(d_proj), w_in_all, slots, blk_size)
    line.wait(norm_part)
    norm_sum = ctx_sum(norm_part)
    if even:
        out_scatter.step()
    (pre_away,) = grads(line.tied(normed), 1, half, d_proj, wide_q, wide_m, f)
    line.wait(pre_away)
    (pre_home,) = grads(line.tied(normed), 0, half, d_proj, wide_q, wide_m, f, late=(out_sum,))
    line.wait(pre_home)
    (qkv_away,) = grads(line.tied(normed), 1, half, d_proj, 0, wide_q, f)
    line.wait(qkv_away)
    if even:
        out_scatter.step()
    pre_scatter = Move(line, scatter_job(line.tied(pre_away), pre_home, pre_own))
    (qkv_home,) = grads(line.tied(normed), 0, half, d_proj, 0, wide_q, f)
    line.wait(qkv_home)
    if even:
        out_scatter.end()
        out_ring = Move(line, ring_job(line.tied(out_own[0]), out_parts))
    pre_scatter.step()
    qkv_scatter = Move(line, scatter_job(line.tied(qkv_away), qkv_home, qkv_own))
    pre_scatter.step()

    norm_sum = line.tied(norm_sum)

    seq_in_t = line.tied(seq_in)
    centred = seq_in_t - jnp.mean(seq_in_t, axis=1, keepdims=True)
    inv_std = lax.rsqrt(jnp.mean(centred * centred, axis=1, keepdims=True) + LN_EPS)
    x_hat = centred * inv_std
    d_norm = jnp.concatenate(
        [
            lax.dynamic_slice_in_dim(norm_sum.astype(F32), position_of(f ^ i) * wide_d, wide_d, 1)
            for i in range(n_fsdp)
        ],
        axis=1,
    )
    small = jnp.stack(
        [jnp.sum(seq_grad, axis=0), jnp.sum(d_norm * x_hat, axis=0), jnp.sum(d_norm, axis=0)]
    )
    gain_grad = d_norm * ln_gain
    d_input = seq_grad + inv_std * (
        gain_grad
        - jnp.mean(gain_grad, axis=1, keepdims=True)
        - x_hat * jnp.mean(gain_grad * x_hat, axis=1, keepdims=True)
    )
    out_y = seq_in + out_sum.astype(F32) + b_out

    g_b_in_z = jnp.concatenate([x[0] for x in (*sum_qkv, sum_pre)])
    masked = jnp.where(
        jnp.arange(n_ctx)[:, None] == z, g_b_in_z[None, :], jnp.zeros((), F32)
    )
    runs = sorted((s, n, i, at) for i in range(n_ctx) for s, n, at in run_offsets(z_runs[i]))
    vector = jnp.concatenate([small.reshape(-1)] + [masked[i, at : at + n] for _, n, i, at in runs])
    line.wait(d_input)

    pre_runs = [[(s - 3 * D, n) for s, n in runs if s >= 3 * D] for runs in z_runs]
    qkv_runs = [[(s, n) for s, n in runs if s < 3 * D] for runs in z_runs]
    if even:
        out_ring.step(pre_scatter, qkv_scatter)
    else:
        pre_scatter.step(qkv_scatter)
    pre_scatter.end()
    pre_ring = Move(line, ring_job(line.tied(pre_own[0]), pre_parts))
    vectors = []
    if even:
        out_ring.end(qkv_scatter)
    vector_move = Move(line, total_job(line.tied(vector), vectors))
    if even:
        at = []
        for j in range(n_ctx):
            rank = lax.rem(z - j + n_ctx, n_ctx)
            at.append(jnp.where(is_mixed, rank * cut, rank * share))
            if cut_m:
                at.append(jnp.where(is_mixed, cut * n_ctx + rank * cut_m, rank * share + cut))
        g_w_out = join_rows(
            [line.tied(out_parts[0])] + [out_parts[j] for j in range(1, n_ctx)],
            jnp.stack(at).astype(jnp.int32),
            (cut, cut_m) if cut_m else (cut,),
        )
        line.wait(g_w_out)
    else:
        blocks = jnp.concatenate([home, away], axis=0).reshape(n_fsdp, -1, D)
        g_out = jnp.concatenate(
            [lax.dynamic_index_in_dim(blocks, position_of(f ^ i), 0, False) for i in range(n_fsdp)]
        )
        spread = jnp.zeros((cat_rows, D), BF)
        spread = lax.dynamic_update_slice_in_dim(spread, g_out[:wide_a], z * wide_a, 0)
        spread = lax.dynamic_update_slice_in_dim(spread, g_out[wide_a:], D + z * wide_m, 0)
        g_w_out = lax.psum_scatter(spread.astype(F32), "fsdp", scatter_dimension=0, tiled=True)
        g_w_out = lax.psum(g_w_out, "ctx")
    pre_ring.step(qkv_scatter, vector_move)
    qkv_scatter.end()
    qkv_ring = Move(line, ring_job(line.tied(qkv_own[0]), qkv_parts))
    pre_ring.end(vector_move)
    vector_move.step()
    in_turn = range(n_ctx)
    g_w_in = spread_columns(
        None,
        [line.tied(pre_parts[0])] + [pre_parts[j] for j in in_turn[1:]],
        z, pre_runs, in_cols, 3 * D, in_cols - 3 * D,
    )
    line.wait(g_w_in)
    qkv_ring.step(vector_move)
    qkv_ring.end(vector_move)
    vector_move.end()
    g_w_in = spread_columns(
        g_w_in, [qkv_parts[j] for j in in_turn], z, qkv_runs, in_cols, 0, 3 * D
    )
    vector = vectors[0]
    small = vector[: 3 * D].reshape(3, D)
    g_b_in = vector[3 * D :]

    def own_part(vector):
        length_part = vector.shape[0] // n_fsdp
        return lax.dynamic_slice_in_dim(vector, f * length_part, length_part, 0)

    return (
        out_y[None],
        d_input[None],
        g_w_in,
        own_part(g_b_in),
        g_w_out,
        own_part(small[0]),
        own_part(small[1]),
        own_part(small[2]),
    )


def run_offsets(runs):
    at, found = 0, []
    for start, size in runs:
        found.append((start, size, at))
        at += size
    return found


def solution(mesh):
    placed = (
        P("fsdp", "ctx", None),
        P("fsdp", "ctx", None),
        P("fsdp", None),
        P(),
        P(),
        P("fsdp", None),
        P(),
        P("fsdp", None),
        P(),
    )
    return jax.shard_map(
        shards,
        mesh=mesh,
        in_specs=placed,
        out_specs=(
            P("fsdp", "ctx", None),
            P("fsdp", "ctx", None),
            P("fsdp", None),
            P("fsdp"),
            P("fsdp", None),
            P("fsdp"),
            P("fsdp"),
            P("fsdp"),
        ),
        check_vma=False,
    )
```
